32 devices in a mesh: dp: 8 (over y, x, core), fsdp: 4 (over z).
Axes of the slice: x: 2, y: 2, z: 4, core: 2. Of those that a mesh axis runs over, the one named last changes fastest.
Arguments:
- tokens: bfloat16 [128, 197, 768], P(('dp', 'fsdp')), may hold values from -6 to 6
- first_gain: bfloat16 [768], P('fsdp'), may hold values from 0.5 to 1.5
- first_shift: bfloat16 [768], P('fsdp'), may hold values from -1.796875 to 1.796875
- qkv_weight: bfloat16 [768, 2304], P('fsdp'), may hold values from -0.21875 to 0.21875
- query_bias: bfloat16 [768], P('fsdp'), may hold values from -4 to 4
- value_bias: bfloat16 [768], P('fsdp'), may hold values from -0.75 to 0.75
- bias_table: bfloat16 [732, 12], P('fsdp'), may hold values from -4 to 4
- bias_index: int32 [197, 197], replicated, may hold values from 0 to 731
- out_weight: bfloat16 [768, 768], P('fsdp'), may hold values from -1.5 to 1.5
- out_bias: bfloat16 [768], P('fsdp'), may hold values from -3 to 3
- first_scale: bfloat16 [768], P('fsdp'), may hold values from 0.5 to 2
- second_gain: bfloat16 [768], P('fsdp'), may hold values from 0.5 to 1.5
- second_shift: bfloat16 [768], P('fsdp'), may hold values from -1.796875 to 1.796875
- up_weight: bfloat16 [768, 3072], P('fsdp'), may hold values from -0.21875 to 0.21875
- up_bias: bfloat16 [3072], P('fsdp'), may hold values from -3 to 3
- down_weight: bfloat16 [3072, 768], P('fsdp'), may hold values from -0.109375 to 0.109375
- down_bias: bfloat16 [768], P('fsdp'), may hold values from -3 to 3
- second_scale: bfloat16 [768], P('fsdp'), may hold values from 0.5 to 2
- patch_mask: int32 [128, 197], P(('dp', 'fsdp')), may hold values 0 or 1
- upstream: bfloat16 [128, 197, 768], P(('dp', 'fsdp')), may hold values from -6 to 6
Outputs:
- layer_out: bfloat16 [128, 197, 768], P(('dp', 'fsdp'))
- tokens_grad: float32 [128, 197, 768], P(('dp', 'fsdp'))
- grad_first_gain: float32 [768], P('fsdp')
- grad_first_shift: float32 [768], P('fsdp')
- grad_qkv_weight: float32 [768, 2304], P('fsdp')
- grad_query_bias: float32 [768], P('fsdp')
- grad_value_bias: float32 [768], P('fsdp')
- grad_bias_table: float32 [732, 12], P('fsdp')
- grad_out_weight: float32 [768, 768], P('fsdp')
- grad_out_bias: float32 [768], P('fsdp')
- grad_first_scale: float32 [768], P('fsdp')
- grad_second_gain: float32 [768], P('fsdp')
- grad_second_shift: float32 [768], P('fsdp')
- grad_up_weight: float32 [768, 3072], P('fsdp')
- grad_up_bias: float32 [3072], P('fsdp')
- grad_down_weight: float32 [3072, 768], P('fsdp')
- grad_down_bias: float32 [768], P('fsdp')
- grad_second_scale: float32 [768], P('fsdp')
The draws below stay inside these ranges and needn't reach their ends.
All inputs are finite; a program needn't handle non-finite values. No bound on the sum of `patch_mask` on one device may be relied on, other than what follows from the above.
Results may differ from the reference program's by a relative error of at most 0.015.
Values may be sent and summed in bfloat16 or wider, within the bound.
A program may use at most 192 MiB of HBM per device.

```python
import math
import jax
import jax.numpy as jnp
from jax import lax

D = 768
HEADS = 12
HEAD_DIM = 64
FF = 3072
SEQ = 197
RELS = 732
IMG_DEV = 4
IMAGES = 128
N_FSDP = 4


def plant(result, stream_key, low, largest):
    index_at = [jax.random.randint(jax.random.fold_in(stream_key, axis), (), 0, length) for axis, length in enumerate(result.shape)]
    widest = result.shape.index(max(result.shape))
    beside = index_at[:widest] + [(index_at[widest] + 1) % result.shape[widest]] + index_at[widest + 1:]
    return result.at[tuple(index_at)].set(low).at[tuple(beside)].set(largest)


def shard_levels(stream_key, extent, cuts, least, largest):
    gain, own = 1.0, jax.random.fold_in(stream_key, 6)
    for dim, shards_of in cuts:
        draws = jnp.exp(jax.random.uniform(jax.random.fold_in(own, dim), (shards_of,), jnp.float32, least / len(cuts), largest / len(cuts)))
        gain = gain * jnp.repeat(draws, extent[dim] // shards_of).reshape([-1 if axis == dim else 1 for axis in range(len(extent))])
    return gain


def normal_values(stream_key, shape, deviation, limit, split=(), dtype=jnp.bfloat16):
    drawn = jax.random.normal(stream_key, shape, jnp.float32) * deviation
    if len(split) > 0:
        drawn = shard_levels(stream_key, shape, split, -0.22, 0.18) * drawn
    return jnp.clip(drawn, min=-limit, max=limit).astype(dtype)


def setup_inputs(seed: int = 0) -> dict:
    streams_of = jax.random.split(jax.random.key(seed), 21)
    tokens = normal_values(streams_of[0], (IMAGES, SEQ, D), 1.0, 6.0, ((0, 32),))
    first_gain = jnp.clip(1.0 + 0.1 * jax.random.normal(streams_of[1], (D,), jnp.float32), 0.5, 1.5).astype(jnp.bfloat16)
    first_shift = normal_values(streams_of[2], (D,), 0.3, 1.796875, ((0, 4),))
    qkv_weight = normal_values(streams_of[3], (D, 3 * D), D ** -0.5, 0.21875, ((0, 4),))
    query_bias = normal_values(streams_of[4], (D,), 1.0, 4.0, ((0, 4),))
    value_bias = normal_values(streams_of[5], (D,), 0.125, 0.75, ((0, 4),))
    bias_table = normal_values(streams_of[6], (RELS, HEADS), 1.0, 4.0, ((0, 4),))
    bias_index = plant(jax.random.randint(streams_of[7], (SEQ, SEQ), 0, RELS), jax.random.fold_in(streams_of[7], 1), 0, RELS - 1).astype(jnp.int32)
    out_weight = normal_values(streams_of[8], (D, D), (D * 4 // SEQ) ** -0.5, 1.5, ((0, 4),))
    out_bias = normal_values(streams_of[9], (D,), 0.5, 3.0, ((0, 4),))
    first_scale = jnp.clip(jnp.exp(math.log(2.0) - 1.3862944 * jax.random.uniform(streams_of[10], (D,), jnp.float32) ** shard_levels(streams_of[10], (D,), ((0, 4),), -0.2, 0.2)), 0.5, 2.0).astype(jnp.bfloat16)
    second_gain = jnp.clip(1.0 + 0.1 * jax.random.normal(streams_of[11], (D,), jnp.float32), 0.5, 1.5).astype(jnp.bfloat16)
    second_shift = normal_values(streams_of[12], (D,), 0.3, 1.796875, ((0, 4),))
    up_weight = normal_values(streams_of[13], (D, FF), D ** -0.5, 0.21875, ((0, 4),))
    up_bias = normal_values(streams_of[14], (FF,), 0.5, 3.0, ((0, 4),))
    down_weight = normal_values(streams_of[15], (FF, D), FF ** -0.5, 0.109375, ((0, 4),))
    down_bias = normal_values(streams_of[16], (D,), 0.5, 3.0, ((0, 4),))
    second_scale = jnp.clip(jnp.exp(math.log(2.0) - 1.3862944 * jax.random.uniform(streams_of[17], (D,), jnp.float32) ** shard_levels(streams_of[17], (D,), ((0, 4),), -0.2, 0.2)), 0.5, 2.0).astype(jnp.bfloat16)
    patch_mask = plant((jax.random.randint(streams_of[18], (IMAGES, SEQ), 0, 5) < 2).astype(jnp.int32), jax.random.fold_in(streams_of[18], 1), 0, 1)
    upstream = normal_values(streams_of[19], (IMAGES, SEQ, D), 1.0, 6.0, ((0, 32),))
    return dict(tokens=tokens, first_gain=first_gain, first_shift=first_shift, qkv_weight=qkv_weight, query_bias=query_bias, value_bias=value_bias, bias_table=bias_table, bias_index=bias_index, out_weight=out_weight, out_bias=out_bias, first_scale=first_scale, second_gain=second_gain, second_shift=second_shift, up_weight=up_weight, up_bias=up_bias, down_weight=down_weight, down_bias=down_bias, second_scale=second_scale, patch_mask=patch_mask, upstream=upstream)


@jax.custom_vjp
def low(v):
    return lax.optimization_barrier(v.astype(jnp.bfloat16)).astype(jnp.float32)

@jax.custom_vjp
def low_back(v):
    return v

def low_keep(v):
    return (low(v), None)

def low_pass(kept, grad):
    return (grad,)

def back_keep(v):
    return (v, None)

def back_low(kept, grad):
    return (low(grad),)
low.defvjp(low_keep, low_pass)
low_back.defvjp(back_keep, back_low)
highest = lax.Precision.HIGHEST

def matmul(left, right):
    return jnp.dot(left, right, precision=highest, preferred_element_type=jnp.float32)

def layer_norm(values, scaling, offset):
    middle = lax.optimization_barrier(jnp.mean(values, axis=-1, keepdims=True))
    centred = values - middle
    spread = lax.optimization_barrier(jnp.mean(centred * centred, axis=-1, keepdims=True))
    return centred * lax.rsqrt(spread + 1e-06) * scaling + offset

def layer_block(images, parameters, bias_index):
    first_gain, first_shift, qkv_weight, query_bias, value_bias, bias_table, out_weight, out_bias, first_scale, second_gain, second_shift, up_weight, up_bias, down_weight, down_bias, second_scale = parameters
    number = images.shape[0]
    inputs = images.reshape(number * SEQ, D)
    factor = HEAD_DIM ** (-0.5)
    norm_one = low(layer_norm(inputs, first_gain, first_shift))
    projected = low_back(matmul(norm_one, qkv_weight))
    query = low((projected[:, :D] + query_bias) * factor).reshape(number, SEQ, HEADS, HEAD_DIM)
    key_heads = low(projected[:, D:2 * D]).reshape(number, SEQ, HEADS, HEAD_DIM)
    value_heads = low(projected[:, 2 * D:] + value_bias).reshape(number, SEQ, HEADS, HEAD_DIM)
    relative = jnp.transpose(bias_table[bias_index], (2, 0, 1))
    products = low_back(jnp.einsum('bqhd,bkhd->bhqk', query, key_heads, precision=highest))
    attend = low(jax.nn.softmax(products + relative[None], axis=-1))
    context = jnp.einsum('bhqk,bkhd->bqhd', attend, value_heads, precision=highest).reshape(number * SEQ, D)
    context = low(low_back(context))
    attn_out = low_back(matmul(context, out_weight)) + out_bias
    hidden = inputs + first_scale * attn_out
    norm_two = low(layer_norm(hidden, second_gain, second_shift))
    up_act = low_back(matmul(norm_two, up_weight)) + up_bias
    gelu_act = low(jax.nn.gelu(up_act, approximate=False))
    down_out = low_back(matmul(gelu_act, down_weight)) + down_bias
    return (hidden + second_scale * down_out).reshape(number, SEQ, D)

def reference(tokens, first_gain, first_shift, qkv_weight, query_bias, value_bias, bias_table, bias_index, out_weight, out_bias, first_scale, second_gain, second_shift, up_weight, up_bias, down_weight, down_bias, second_scale, patch_mask, upstream):
    parameters = tuple((weight.astype(jnp.float32) for weight in (first_gain, first_shift, qkv_weight, query_bias, value_bias, bias_table, out_weight, out_bias, first_scale, second_gain, second_shift, up_weight, up_bias, down_weight, down_bias, second_scale)))
    group = IMG_DEV * N_FSDP
    blocks = IMAGES // group
    inputs = tokens.astype(jnp.float32).reshape(blocks, group, SEQ, D)

    def forward(stacked, weights):

        def one_block(images):
            return layer_block(images, weights, bias_index)
        return lax.map(jax.checkpoint(one_block), stacked)
    outputs, pullback = jax.vjp(forward, inputs, parameters)
    cotangent = upstream.astype(jnp.float32) * patch_mask.astype(jnp.float32)[:, :, None]
    grad_inputs, gradients = pullback(cotangent.reshape(blocks, group, SEQ, D))
    grad_first_gain, grad_first_shift, grad_qkv_weight, grad_query_bias, grad_value_bias, grad_bias_table, grad_out_weight, grad_out_bias, grad_first_scale, grad_second_gain, grad_second_shift, grad_up_weight, grad_up_bias, grad_down_weight, grad_down_bias, grad_second_scale = gradients
    return (outputs.reshape(IMAGES, SEQ, D).astype(jnp.bfloat16), grad_inputs.reshape(IMAGES, SEQ, D), grad_first_gain, grad_first_shift, grad_qkv_weight, grad_query_bias, grad_value_bias, grad_bias_table, grad_out_weight, grad_out_bias, grad_first_scale, grad_second_gain, grad_second_shift, grad_up_weight, grad_up_bias, grad_down_weight, grad_down_bias, grad_second_scale)
```

```python
import functools
import jax
import jax.numpy as jnp
from jax import lax
from jax.experimental import pallas as pl
from jax.experimental.pallas import tpu as pltpu
from jax.sharding import PartitionSpec as P

D = 768
HEADS = 12
HEAD_DIM = 64
FF = 3072
SEQ = 197
RELS = 732
SP = 208
KP = 256
HALF = SP * KP
EPS = 1e-06
BF = jnp.bfloat16
F32 = jnp.float32
VMEM = pl.BlockSpec(memory_space=pltpu.VMEM)
ANY = pl.BlockSpec(memory_space=pl.ANY)
LIMIT = 62 * 2**20


def dot(a, b):
    return lax.dot_general(a, b, (((1,), (0,)), ((), ())), preferred_element_type=F32)


def dot_nt(a, b):
    return lax.dot_general(a, b, (((1,), (1,)), ((), ())), preferred_element_type=F32)


def dot_tn(a, b):
    return lax.dot_general(a, b, (((0,), (0,)), ((), ())), preferred_element_type=F32)


def rowmean(v):
    return jnp.sum(v, axis=-1, keepdims=True) * (1.0 / D)


def colsum(v):
    return jnp.sum(v, axis=0, keepdims=True)


def xhat_of(v):
    centred = v - rowmean(v)
    rstd = lax.rsqrt(rowmean(centred * centred) + EPS)
    return centred * rstd, rstd


def pad_rows(v):
    return jnp.concatenate([v, jnp.zeros((SP - SEQ, v.shape[1]), v.dtype)], axis=0)


GAIN1, SHIFT1, QBIAS, VBIAS, OBIAS, SCALE1, GAIN2, SHIFT2, DBIAS, SCALE2 = range(10)


def front_kernel(tok, vec, table, index, norm_one, relative):
    images = tok.shape[0]
    gain, shift = vec[GAIN1 : GAIN1 + 1, :], vec[SHIFT1 : SHIFT1 + 1, :]
    for b in range(images):
        xhat, _ = xhat_of(pad_rows(tok[b].astype(F32)))
        norm_one[b] = (xhat * gain + shift).astype(BF)
    lookup(table, index, relative)


def lookup(table, index, relative):
    lanes = lax.broadcasted_iota(jnp.int32, (16, 128), 1)

    def rows(r, carry):
        at = pl.ds(pl.multiple_of(r * 16, 16), 16)
        for half in range(2):
            idx = index[at, half * 128 : half * 128 + 128]
            low = idx & 127
            high = idx >> 7
            for h in range(HEADS):
                out = jnp.zeros((16, 128), F32)
                for c in range(6):
                    part = jnp.broadcast_to(table[h : h + 1, c * 128 : c * 128 + 128], (16, 128))
                    got = jnp.take_along_axis(part, low, axis=1, mode="promise_in_bounds")
                    out = jnp.where(high == c, got, out)
                if half == 1:
                    out = jnp.where(lanes < SEQ - 128, out, -1e30)
                relative[h, at, half * 128 : half * 128 + 128] = out.astype(BF)
        return carry

    lax.fori_loop(0, SP // 16, rows, 0)


def lane_masks(rows):
    lane = lax.broadcasted_iota(jnp.int32, (rows, 128), 1)
    return lane < HEAD_DIM


def split_heads(v, first):
    zero = jnp.zeros_like(v)
    return jnp.where(first, v, zero), jnp.where(first, zero, v)


def project(norm_one, qkv, vec, q, k, v):
    images = norm_one.shape[0]
    k[:, SP:, :] = jnp.zeros((images, KP - SP, D), BF)
    v[:, SP:, :] = jnp.zeros((images, KP - SP, D), BF)

    def chunk(i, carry):
        at = pl.ds(pl.multiple_of(i * 256, 256), 256)
        rows = norm_one[...].reshape(images * SP, D)
        pq = dot(rows, qkv[:, at])
        q[:, :, at] = ((pq + vec[QBIAS : QBIAS + 1, at]) * 0.125).astype(BF).reshape(images, SP, 256)
        pk = dot(rows, qkv[:, pl.ds(pl.multiple_of(D + i * 256, 256), 256)])
        k[:, :SP, at] = pk.astype(BF).reshape(images, SP, 256)
        pv = dot(rows, qkv[:, pl.ds(pl.multiple_of(2 * D + i * 256, 256), 256)])
        v[:, :SP, at] = (pv + vec[VBIAS : VBIAS + 1, at]).astype(BF).reshape(images, SP, 256)
        return carry

    lax.fori_loop(0, D // 256, chunk, 0)


def attend_pair(b, hp, at, q, k, v, relative, attend, context):
    first = lane_masks(KP)
    q2 = q[b, :, at]
    ks = split_heads(k[b, :, at], first)
    vs = split_heads(v[b, :, at], first)
    probs = []
    for e in range(2):
        h = 2 * hp + e
        s = dot_nt(q2, ks[e]) + relative[h].astype(F32)
        s = jnp.exp(s - jnp.max(s, axis=-1, keepdims=True))
        p = (s * (1.0 / jnp.sum(s, axis=-1, keepdims=True))).astype(BF)
        attend[b, h] = p
        probs.append(p)
    context[b, :, at] = (dot(probs[0], vs[0]) + dot(probs[1], vs[1])).astype(BF)


def attention_kernel(norm_one, qkv, vec, relative, q, k, v, attend, context):
    images = norm_one.shape[0]
    project(norm_one, qkv, vec, q, k, v)

    def image(b, carry):
        for hp in range(HEADS // 2):
            attend_pair(b, hp, slice(hp * 128, hp * 128 + 128), q, k, v, relative, attend, context)
        return carry

    lax.fori_loop(0, images, image, 0)


def gelu_both(v):
    cdf = 0.5 * (1.0 + lax.erf(v * 0.7071067811865476))
    pdf = jnp.exp(v * v * -0.5) * 0.3989422804014327
    return v * cdf, cdf + v * pdf


def mlp_kernel(tok, ctx, out_hbm, up_hbm, down_hbm, vec, upb, mask, ups,
               layer_out, dout, dup, ddown, gctx, gres, small, small_up,
               outw, upw, downw, hid, att, n2, act, slope, acc, gd, gy_s, sems):
    images = tok.shape[0]
    R = images * SP
    loads = [pltpu.make_async_copy(s, d, sems.at[i]) for i, (s, d) in enumerate(
        ((out_hbm, outw), (up_hbm, upw), (down_hbm, downw)))]
    for l in loads:
        l.start()
    obias, scale1 = vec[OBIAS : OBIAS + 1, :], vec[SCALE1 : SCALE1 + 1, :]
    gain2, shift2 = vec[GAIN2 : GAIN2 + 1, :], vec[SHIFT2 : SHIFT2 + 1, :]
    dbias, scale2 = vec[DBIAS : DBIAS + 1, :], vec[SCALE2 : SCALE2 + 1, :]
    maskt = jnp.transpose(mask[...], (1, 0))
    loads[0].wait()
    for b in range(images):
        attn = dot(ctx[b], outw[...]) + obias
        att[b] = attn
        h = pad_rows(tok[b].astype(F32)) + scale1 * attn
        hid[b] = h
        xhat, _ = xhat_of(h)
        n2[b] = (xhat * gain2 + shift2).astype(BF)
    loads[1].wait()
    loads[2].wait()
    acc[...] = jnp.zeros_like(acc)
    W = 256

    def forward(f, carry):
        at = pl.ds(pl.multiple_of(f * W, W), W)
        for b in range(images):
            u = dot(n2[b], upw[:, at]) + upb[:, at]
            g, s = gelu_both(u)
            g = g.astype(BF)
            act[b, :, at] = g
            slope[b, :, at] = s.astype(BF)
            acc[b] += dot(g, downw[at, :])
        return carry

    lax.fori_loop(0, FF // W, forward, 0)
    sums = [jnp.zeros((1, D), F32) for _ in range(6)]
    for b in range(images):
        down = acc[b] + dbias
        layer_out[b] = (hid[b] + scale2 * down).astype(BF)[:SEQ]
        gy = pad_rows(ups[b].astype(F32)) * maskt[:SP, b : b + 1]
        gy_s[b] = gy.astype(BF)
        sums[0] += colsum(gy * down)
        full = gy * scale2
        sums[1] += colsum(full)
        gd[b] = full.astype(BF)
    acc[...] = jnp.zeros_like(acc)

    def backward(f, carry):
        at = pl.ds(pl.multiple_of(f * W, W), W)
        total = jnp.zeros((1, W), F32)
        lows = []
        for b in range(images):
            gg = dot_nt(gd[b], downw[at, :]) * slope[b, :, at].astype(F32)
            total += colsum(gg)
            low = gg.astype(BF)
            lows.append(low)
            acc[b] += dot_nt(low, upw[:, at])
        small_up[:, at] = total
        low = jnp.concatenate(lows, axis=0)
        dup[:, at] = dot_tn(n2[...].reshape(R, D), low).astype(BF)
        ddown[at, :] = dot_tn(act[:, :, at].reshape(R, W), gd[...].reshape(R, D)).astype(BF)
        return carry

    lax.fori_loop(0, FF // W, backward, 0)
    for b in range(images):
        xhat, rstd = xhat_of(hid[b])
        g = acc[b]
        sums[2] += colsum(g * xhat)
        sums[3] += colsum(g)
        gg = g * gain2
        gh = (gg - rowmean(gg) - xhat * rowmean(gg * xhat)) * rstd
        res = gy_s[b].astype(F32) + gh
        gres[b] = res
        sums[4] += colsum(res * att[b])
        full = res * scale1
        sums[5] += colsum(full)
        n2[b] = full.astype(BF)
    dout[...] = dot_tn(ctx[...].reshape(R, D), n2[...].reshape(R, D)).astype(BF)
    for b in range(images):
        gctx[b] = dot_nt(n2[b], outw[...]).astype(BF)
    small[...] = jnp.concatenate(sums + [jnp.zeros((2, D), F32)], axis=0)


def attend_back(b, hp, at, q, k, v, attend, gctx, gtab, gq, gk, gv, qsum, vsum):
    first = lane_masks(KP)
    firsts = first[:SP]
    v2 = split_heads(v[b, :, at], first)
    k2 = split_heads(k[b, :, at], first)
    q2 = split_heads(q[b, :, at], firsts)
    g2 = gctx[b, :, at]
    gs2 = split_heads(g2, firsts)
    dq = jnp.zeros((SP, 128), F32)
    dk = jnp.zeros((KP, 128), F32)
    dv = jnp.zeros((KP, 128), F32)
    for e in range(2):
        h = 2 * hp + e
        a = attend[b, h]
        af = a.astype(F32)
        ga = dot_nt(g2, v2[e])
        w = af * ga
        inner = jnp.sum(w, axis=-1, keepdims=True)
        gs = w - af * inner
        gtab[h] += gs
        low = gs.astype(BF)
        dq += dot(low, k2[e])
        dk += dot_tn(low, q2[e])
        dv += dot_tn(a, gs2[e])
    dq = dq * 0.125
    qsum[:, at] += colsum(dq)
    vsum[:, at] += colsum(dv)
    gq[b, :, at] = dq.astype(BF)
    gk[b, :, at] = dk[:SP].astype(BF)
    gv[b, :, at] = dv[:SP].astype(BF)


def table_back(gtab, index, out):
    ids = lax.broadcasted_iota(jnp.int32, (128, KP), 0)

    def row(i, acc):
        idx = index[pl.ds(i, 1), :]
        low, high = idx & 127, idx >> 7
        hot = jnp.where(ids == low, 1.0, 0.0).astype(BF)
        g = gtab[:, pl.ds(i, 1), :].reshape(16, KP)
        g1 = g.astype(BF).astype(F32)
        g2 = g - g1
        parts = []
        for src in (g1, g2):
            for c in range(6):
                parts.append(jnp.where(high == c, src, 0.0).astype(BF))
        return acc + dot_nt(jnp.concatenate(parts, axis=0), hot)

    acc = lax.fori_loop(0, SEQ, row, jnp.zeros((192, 128), F32))
    out[...] = acc[:96] + acc[96:]


def back_kernel(tok, norm_one, qkv_hbm, vec, index, q, k, v, attend, gctx, gres,
                tgrad, dqkv, small, tab, gtab, gqkv, qkv, sem):
    images = tok.shape[0]
    R = images * SP
    load = pltpu.make_async_copy(qkv_hbm, qkv, sem)
    load.start()
    gtab[...] = jnp.zeros_like(gtab)
    small[...] = jnp.zeros_like(small)
    gq, gk, gv = (gqkv.at[:, :, i * D : (i + 1) * D] for i in range(3))
    qsum, vsum = small.at[0:1, :], small.at[1:2, :]

    def pair(hp, carry):
        at = pl.ds(pl.multiple_of(hp * 128, 128), 128)
        for b in range(images):
            attend_back(b, hp, at, q, k, v, attend, gctx, gtab, gq, gk, gv, qsum, vsum)
        return carry

    lax.fori_loop(0, HEADS // 2, pair, 0)
    table_back(gtab, index, tab)

    def chunk(i, carry):
        at = pl.ds(pl.multiple_of(i * 256, 256), 256)
        dqkv[:, at] = dot_tn(norm_one[...].reshape(R, D), gqkv[:, :, at].reshape(R, 256)).astype(BF)
        return carry

    lax.fori_loop(0, 3 * D // 256, chunk, 0)
    load.wait()
    gain = vec[GAIN1 : GAIN1 + 1, :]
    for b in range(images):
        xhat, rstd = xhat_of(pad_rows(tok[b].astype(F32)))
        g = dot_nt(gqkv[b], qkv[...])
        small[2:3, :] += colsum(g * xhat)
        small[3:4, :] += colsum(g)
        gg = g * gain
        gi = (gg - rowmean(gg) - xhat * rowmean(gg * xhat)) * rstd
        tgrad[b] = (gres[b] + gi)[:SEQ]


def params(**kw):
    return pltpu.CompilerParams(vmem_limit_bytes=LIMIT, **kw)


def S(shape, dtype):
    return jax.ShapeDtypeStruct(shape, dtype)


def front(tok, vec, table, index):
    n = tok.shape[0]
    return pl.pallas_call(front_kernel, out_shape=(S((n, SP, D), BF), S((HEADS, SP, KP), BF)),
                          in_specs=[VMEM] * 4, out_specs=(VMEM, VMEM), compiler_params=params(), name="front")(tok, vec, table, index)


def attention(norm_one, qkv, vec, relative):
    n = norm_one.shape[0]
    return pl.pallas_call(attention_kernel,
                          out_shape=(S((n, SP, D), BF), S((n, KP, D), BF), S((n, KP, D), BF), S((n, HEADS, SP, KP), BF), S((n, SP, D), BF)),
                          in_specs=[VMEM] * 4, out_specs=(VMEM,) * 5, compiler_params=params(), name="attention")(norm_one, qkv, vec, relative)


def mlp(tok, ctx, outw, upw, downw, vec, upb, mask, ups):
    n = tok.shape[0]
    return pl.pallas_call(
        mlp_kernel,
        out_shape=(S((n, SEQ, D), BF), S((D, D), BF), S((D, FF), BF), S((FF, D), BF), S((n, SP, D), BF), S((n, SP, D), F32), S((8, D), F32), S((1, FF), F32)),
        in_specs=[VMEM, VMEM, ANY, ANY, ANY, VMEM, VMEM, VMEM, VMEM], out_specs=(VMEM,) * 8,
        scratch_shapes=[pltpu.VMEM((D, D), BF), pltpu.VMEM((D, FF), BF), pltpu.VMEM((FF, D), BF),
                        pltpu.VMEM((n, SP, D), F32), pltpu.VMEM((n, SP, D), F32), pltpu.VMEM((n, SP, D), BF),
                        pltpu.VMEM((n, SP, FF), BF), pltpu.VMEM((n, SP, FF), BF), pltpu.VMEM((n, SP, D), F32),
                        pltpu.VMEM((n, SP, D), BF), pltpu.VMEM((n, SP, D), BF), pltpu.SemaphoreType.DMA((3,))],
        compiler_params=params(), name="mlp")(tok, ctx, outw, upw, downw, vec, upb, mask, ups)


def back(tok, norm_one, qkv, vec, index, q, k, v, attend, gctx, gres):
    n = tok.shape[0]
    return pl.pallas_call(
        back_kernel,
        out_shape=(S((n, SEQ, D), F32), S((D, 3 * D), BF), S((8, D), F32), S((96, 128), F32)),
        in_specs=[VMEM, VMEM, ANY] + [VMEM] * 8, out_specs=(VMEM,) * 4,
        scratch_shapes=[pltpu.VMEM((16, SP, KP), F32), pltpu.VMEM((n, SP, 3 * D), BF), pltpu.VMEM((D, 3 * D), BF), pltpu.SemaphoreType.DMA(())],
        compiler_params=params(), name="back")(tok, norm_one, qkv, vec, index, q, k, v, attend, gctx, gres)


def pad_index(bias_index):
    return jnp.pad(bias_index, ((0, SP - SEQ), (0, KP - SEQ)))
MESH = pl.DeviceIdType.MESH


class Place:
    def __init__(self):
        dp, z = lax.axis_index("dp"), lax.axis_index("fsdp")
        y, x, c = dp // 4, (dp // 2) % 2, dp % 2
        xn, yn = dp + 2 - 4 * x, dp + 4 - 8 * y
        q = dp // 2
        qx, qy = q + 1 - 2 * x, q + 2 - 4 * y
        self.dp, self.z, self.c, self.q = dp, z, c, q
        self.near = (xn * (1 - c) + yn * c, z)
        self.far = (yn * (1 - c) + xn * c, z)
        self.x, self.y = (xn, z), (yn, z)
        self.twin = (dp + 1 - 2 * c, z)
        self.q_near = qx * (1 - c) + qy * c
        self.q_far = qy * (1 - c) + qx * c
        self.q_both = 3 - q

    def up(self, d):
        return (self.dp, (self.z + d) % 4)

    def barrier(self):
        sem = pltpu.get_barrier_semaphore()
        peers = [self.near, self.far, self.twin] + [self.up(d) for d in (1, 2, 3)]
        for peer in peers:
            pl.semaphore_signal(sem, inc=1, device_id=peer, device_id_type=MESH)
        pl.semaphore_wait(sem, len(peers))


def aligned(i, size):
    return pl.ds(pl.multiple_of(i * size, size), size)


class Gather:
    def __init__(self, place, shard, full, send, recv, local):
        self.p, self.shard, self.full, self.send, self.recv, self.local = place, shard, full, send, recv, local
        self.rows, self.cols = shard.shape[0] // 4, shard.shape[1] // 2

    def region(self, zb, q, c):
        return self.full.at[zb, aligned(q, self.rows), aligned(c, self.cols)]

    def copy(self, d, slot, src, dst, peer):
        return pltpu.make_async_remote_copy(src_ref=src, dst_ref=dst, send_sem=self.send.at[d - 1, slot], recv_sem=self.recv.at[d - 1, slot],
                                            device_id=peer, device_id_type=MESH)

    def over_z(self, d):
        p = self.p
        src = self.shard.at[aligned(p.q, self.rows), aligned(p.c, self.cols)]
        return self.copy(d, 0, src, self.region(p.z, p.q, p.c), p.up(d))

    def passed(self, d, slot, q, peer):
        p = self.p
        r = self.region((p.z + 4 - d) % 4, q, p.c)
        return self.copy(d, slot, r, r, peer)

    def own(self):
        return pltpu.make_async_copy(self.shard, self.full.at[self.p.z], self.local)

    def begin(self):
        for d in (1, 2, 3):
            self.over_z(d).start()
        self.own().start()

    def part(self, d, i):
        p = self.p
        slot, q, peer = ((1, p.q, p.near), (2, p.q, p.far), (4, p.q, p.twin), (3, p.q_near, p.far), (5, p.q_near, p.twin),
                         (6, p.q_far, p.twin), (7, p.q_both, p.twin))[i]
        return self.passed(d, slot, q, peer)

    def spread(self, d):
        self.over_z(d).wait_recv()
        for i in (0, 1, 2):
            self.part(d, i).start()

    def relay(self, d):
        self.part(d, 0).wait_recv()
        for i in (3, 4):
            self.part(d, i).start()

    def close(self, d):
        self.part(d, 1).wait_recv()
        self.part(d, 5).start()
        self.part(d, 3).wait_recv()
        self.part(d, 6).start()

    def finish(self):
        self.own().wait()
        for d in (1, 2, 3):
            for i in (2, 4, 5, 6):
                self.part(d, i).wait_recv()

    def drain(self):
        for d in (1, 2, 3):
            self.over_z(d).wait_send()
            for i in range(7):
                self.part(d, i).wait_send()

    def steps(self):
        return [lambda d=d: self.spread(d) for d in (1, 2, 3)] + [lambda d=d: self.relay(d) for d in (1, 2, 3)] + [
            lambda d=d: self.close(d) for d in (1, 2, 3)] + [self.finish]


class Reduce:
    def __init__(self, place, grad, got, mine, half, quarter, pieces, out, send, recv, local):
        self.p, self.grad, self.got, self.mine, self.half, self.quarter, self.pieces, self.out = place, grad, got, mine, half, quarter, pieces, out
        self.send, self.recv, self.local = send, recv, local
        self.rows, self.cols = grad.shape[1] // 4, grad.shape[2] // 2

    def copy(self, slot, src, dst, peer):
        return pltpu.make_async_remote_copy(src_ref=src, dst_ref=dst, send_sem=self.send.at[slot], recv_sem=self.recv.at[slot], device_id=peer, device_id_type=MESH)

    def twin(self):
        other = self.grad.at[:, :, aligned(1 - self.p.c, self.cols)]
        return self.copy(0, other, self.got, self.p.twin)

    def keep(self):
        return pltpu.make_async_copy(self.grad.at[:, :, aligned(self.p.c, self.cols)], self.mine, self.local)

    def near(self, i):
        q = (self.p.q_near, self.p.q_both)[i]
        return self.copy(1 + i, self.mine.at[:, aligned(q, self.rows), :], self.half.at[i], self.p.near)

    def far(self):
        return self.copy(3, self.half.at[1], self.quarter, self.p.far)

    def over_z(self, d):
        return self.copy(3 + d, self.quarter.at[(self.p.z + d) % 4], self.pieces.at[d - 1], self.p.up(d))

    def region(self, q):
        return self.out.at[aligned(q, self.rows), aligned(self.p.c, self.cols)]

    def passed(self, i):
        p = self.p
        q, peer = ((p.q, p.near), (p.q, p.far), (p.q, p.twin), (p.q_near, p.far), (p.q_near, p.twin), (p.q_far, p.twin), (p.q_both, p.twin))[i]
        return self.copy(7 + i, self.region(q), self.region(q), peer)

    def begin(self):
        self.twin().start()
        self.keep().start()

    def add(self, dst, src):
        def one(i, carry):
            dst[i] = (dst[i].astype(F32) + src[i].astype(F32)).astype(BF)
            return carry

        lax.fori_loop(0, 4, one, 0)

    def fold(self, q):
        self.add(self.mine.at[:, aligned(q, self.rows), :], self.got.at[:, aligned(q, self.rows), :])

    def first(self):
        self.keep().wait()
        self.twin().wait_recv()
        self.fold(self.p.q_near)
        self.near(0).start()
        self.fold(self.p.q_both)
        self.near(1).start()
        self.fold(self.p.q)
        self.fold(self.p.q_far)

    def second(self):
        self.near(1).wait_recv()
        self.add(self.half.at[1], self.mine.at[:, aligned(self.p.q_far, self.rows), :])
        self.far().start()
        self.near(0).wait_recv()
        self.add(self.half.at[0], self.mine.at[:, aligned(self.p.q, self.rows), :])

    def third(self):
        self.far().wait_recv()
        self.add(self.quarter, self.half.at[0])
        for d in (1, 2, 3):
            self.over_z(d).start()

    def fourth(self):
        for d in (1, 2, 3):
            self.over_z(d).wait_recv()
        total = self.quarter[self.p.z].astype(F32)
        for d in (1, 2, 3):
            total += self.pieces[d - 1].astype(F32)
        self.out[aligned(self.p.q, self.rows), aligned(self.p.c, self.cols)] = total.astype(BF)
        for i in (0, 1, 2):
            self.passed(i).start()

    def fifth(self):
        self.passed(0).wait_recv()
        self.passed(3).start()
        self.passed(4).start()

    def sixth(self):
        self.passed(1).wait_recv()
        self.passed(5).start()
        self.passed(3).wait_recv()
        self.passed(6).start()

    def finish(self):
        for i in (2, 4, 5, 6):
            self.passed(i).wait_recv()

    def drain(self):
        self.twin().wait_send()
        self.near(0).wait_send()
        self.near(1).wait_send()
        self.far().wait_send()
        for d in (1, 2, 3):
            self.over_z(d).wait_send()
        for i in range(7):
            self.passed(i).wait_send()

    def steps(self):
        return [self.first, self.second, self.third, self.fourth, self.fifth, self.sixth, self.finish]
def stack_small(vectors, up_bias, table):
    k = vectors[0].shape[0]
    rows = jnp.concatenate([jnp.stack(vectors), up_bias.reshape(-1, k), jnp.zeros((2, k), BF)], axis=0)
    rows = jnp.pad(rows, ((0, 0), (0, 256 - k)))
    table = jnp.pad(table.T, ((0, 4), (0, 256 - table.shape[0])))
    return jnp.concatenate([rows, table], axis=0)


def unstack_small(block, vec, upb, table):
    vec[...] = jnp.zeros_like(vec)
    table[...] = jnp.zeros_like(table)
    for z in range(4):
        part = block[z].astype(F32)
        vec[:, z * 192 : z * 192 + 192] = part[:16, :192]
        for k in range(4):
            upb[:, z * 768 + k * 192 : z * 768 + k * 192 + 192] = part[10 + k : 11 + k, :192]
        table[:, z * 183 : z * 183 + 183] = part[16:32, :183]


def forward_kernel(tok, small_in, index, qkv_s, out_s, up_s, down_s,
                   norm_one, q, k, v, attend, context, vec, upb, qkv_hbm, out_f, up_f, down_f,
                   qkv, block, table, relative, send, recv, local, ssend, srecv):
    p = Place()
    p.barrier()
    images = tok.shape[0]
    gathers = [Gather(p, s, f, send.at[i], recv.at[i], local.at[i]) for i, (s, f) in enumerate(((qkv_s, qkv), (out_s, out_f), (up_s, up_f), (down_s, down_f)))]
    block[p.z] = small_in[...]
    smalls = [pltpu.make_async_remote_copy(src_ref=small_in, dst_ref=block.at[p.z], send_sem=ssend.at[d - 1], recv_sem=srecv.at[d - 1], device_id=p.up(d), device_id_type=MESH) for d in (1, 2, 3)]
    for s in smalls:
        s.start()
    gathers[0].begin()
    gathers[1].begin()
    for s in smalls:
        s.wait_recv()
    unstack_small(block, vec, upb, table)
    gain, shift = vec[GAIN1 : GAIN1 + 1, :], vec[SHIFT1 : SHIFT1 + 1, :]
    first = gathers[0].steps()
    for b in range(images):
        xhat, _ = xhat_of(pad_rows(tok[b].astype(F32)))
        norm_one[b] = (xhat * gain + shift).astype(BF)
        if b < 3:
            first[b]()
    for s in first[3:6]:
        s()
    gathers[2].begin()
    lookup(table, index, relative)
    for s in first[6:]:
        s()
    back_copy = pltpu.make_async_copy(qkv, qkv_hbm, local.at[4])
    back_copy.start()
    todo = list(gathers[1].steps()) + [gathers[3].begin] + list(gathers[2].steps()) + list(gathers[3].steps())

    def advance(n):
        for _ in range(min(n, len(todo))):
            todo.pop(0)()

    k[:, SP:, :] = jnp.zeros((images, KP - SP, D), BF)
    v[:, SP:, :] = jnp.zeros((images, KP - SP, D), BF)
    rows = norm_one[...].reshape(images * SP, D)
    for i in range(D // 256):
        at = slice(i * 256, i * 256 + 256)

        def weight(j):
            return qkv[:, :, j * D + i * 256 : j * D + i * 256 + 256].reshape(D, 256)

        q[:, :, at] = ((dot(rows, weight(0)) + vec[QBIAS : QBIAS + 1, at]) * 0.125).astype(BF).reshape(images, SP, 256)
        k[:, :SP, at] = dot(rows, weight(1)).astype(BF).reshape(images, SP, 256)
        v[:, :SP, at] = (dot(rows, weight(2)) + vec[VBIAS : VBIAS + 1, at]).astype(BF).reshape(images, SP, 256)
        advance(4)
    for b in range(images):
        for part in range(2):

            def pair(i, carry, b=b, part=part):
                hp = part * 3 + i
                attend_pair(b, hp, aligned(hp, 128), q, k, v, relative, attend, context)
                return carry

            lax.fori_loop(0, 3, pair, 0)
            advance(3)
    advance(len(todo))
    back_copy.wait()
    for s in smalls:
        s.wait_send()
    for g in gathers:
        g.drain()


def forward(tok, small, index, qkv_s, out_s, up_s, down_s):
    n = tok.shape[0]
    shards = (qkv_s, out_s, up_s, down_s)
    fulls = tuple(S((4,) + s.shape, BF) for s in shards)
    return pl.pallas_call(
        forward_kernel,
        out_shape=(S((n, SP, D), BF), S((n, SP, D), BF), S((n, KP, D), BF), S((n, KP, D), BF), S((n, HEADS, SP, KP), BF), S((n, SP, D), BF),
                   S((16, D), F32), S((1, FF), F32)) + fulls,
        in_specs=[VMEM] * 3 + [ANY] * 4, out_specs=(VMEM,) * 8 + (ANY,) * 4,
        scratch_shapes=[pltpu.VMEM(fulls[0].shape, BF), pltpu.VMEM((4, 32, 256), BF), pltpu.VMEM((16, D), F32), pltpu.VMEM((HEADS, SP, KP), BF),
                        pltpu.SemaphoreType.DMA((4, 3, 8)), pltpu.SemaphoreType.DMA((4, 3, 8)), pltpu.SemaphoreType.DMA((5,)),
                        pltpu.SemaphoreType.DMA((3,)), pltpu.SemaphoreType.DMA((3,))],
        compiler_params=params(collective_id=0, has_side_effects=True), name="forward")(tok, small, index, *shards)


def backward_kernel(tok, norm_one, qkv_hbm, vec, index, q, k, v, attend, gctx, gres, small_mlp, small_up, dout, dup, ddown,
                    tgrad, sm_out, rqkv, rout, rup, rdown,
                    gtab, gqkv, qkv, dqkv, small, tab, sm, sm_got, sm_piece,
                    got0, mine0, half0, quart0, piece0, got1, mine1, half1, quart1, piece1,
                    got2, mine2, half2, quart2, piece2, got3, mine3, half3, quart3, piece3, load_sem, send, recv, local, ssend, srecv):
    p = Place()
    p.barrier()
    images = tok.shape[0]
    R = images * SP
    load = pltpu.make_async_copy(qkv_hbm, qkv, load_sem)
    load.start()
    bufs = ((got0, mine0, half0, quart0, piece0), (got1, mine1, half1, quart1, piece1), (got2, mine2, half2, quart2, piece2), (got3, mine3, half3, quart3, piece3))
    red = [Reduce(p, g, *bufs[i], o, send.at[i], recv.at[i], local.at[i]) for i, (g, o) in enumerate(((ddown, rdown), (dup, rup), (dout, rout), (dqkv, rqkv)))]
    red[0].begin()
    red[1].begin()
    red[2].begin()
    steps = [r.steps() for r in red]
    todo = [steps[0][0], steps[1][0], steps[0][1], steps[2][0], steps[1][1], steps[0][2], steps[2][1], steps[1][2], steps[0][3], steps[2][2], steps[1][3], steps[0][4],
            steps[2][3], steps[1][4], steps[0][5], steps[2][4], steps[1][5], steps[2][5]]

    def advance(n):
        for _ in range(min(n, len(todo))):
            todo.pop(0)()

    gtab[...] = jnp.zeros_like(gtab)
    small[...] = jnp.zeros_like(small)
    gq, gk, gv = (gqkv.at[:, :, i * D : (i + 1) * D] for i in range(3))
    qsum, vsum = small.at[0:1, :], small.at[1:2, :]
    for hp in range(HEADS // 2):
        for part in range(2):

            def one(i, carry, hp=hp, part=part):
                attend_back(part * (images // 2) + i, hp, slice(hp * 128, hp * 128 + 128), q, k, v, attend, gctx, gtab, gq, gk, gv, qsum, vsum)
                return carry

            lax.fori_loop(0, images // 2, one, 0)
            advance(1)
    for i in range(3 * D // 256):
        at = slice(i * 256, i * 256 + 256)
        dqkv[:, :, at] = dot_tn(norm_one[...].reshape(R, D), gqkv[:, :, at].reshape(R, 256)).astype(BF).reshape(4, D // 4, 256)
    red[3].begin()
    advance(len(todo))
    load.wait()
    gain = vec[GAIN1 : GAIN1 + 1, :]
    for b in range(images):
        xhat, rstd = xhat_of(pad_rows(tok[b].astype(F32)))
        g = dot_nt(gqkv[b], qkv[...].reshape(D, 3 * D))
        small[2:3, :] += colsum(g * xhat)
        small[3:4, :] += colsum(g)
        gg = g * gain
        gi = (gg - rowmean(gg) - xhat * rowmean(gg * xhat)) * rstd
        tgrad[b] = (gres[b] + gi)[:SEQ]
        if b == 1:
            steps[3][0]()
        if b == 3:
            steps[3][1]()
    table_back(gtab, index, tab)
    steps[3][2]()
    sm[...] = jnp.zeros_like(sm)
    order = [small[2:3, :], small[3:4, :], small[0:1, :], small[1:2, :], small_mlp[5:6, :], small_mlp[4:5, :], small_mlp[2:3, :], small_mlp[3:4, :], small_mlp[1:2, :], small_mlp[0:1, :]]
    vectors = jnp.concatenate(order + [jnp.zeros((6, D), F32)], axis=0)
    flat = jnp.concatenate([tab[c * 16 : c * 16 + 16, :] for c in range(6)], axis=1)
    for z in range(4):
        sm[z, 0:16, 0:192] = vectors[:, z * 192 : z * 192 + 192]
        for i in range(4):
            sm[z, 10 + i : 11 + i, 0:192] = small_up[:, z * 768 + i * 192 : z * 768 + i * 192 + 192]
        sm[z, 16:32, 0:183] = flat[:, z * 183 : z * 183 + 183]

    def exchange(i, peer):
        return pltpu.make_async_remote_copy(src_ref=sm.at[pl.ds(4 * i, 4)], dst_ref=sm_got.at[i], send_sem=ssend.at[i], recv_sem=srecv.at[i], device_id=peer, device_id_type=MESH)

    swaps = [exchange(i, peer) for i, peer in enumerate((p.twin, p.x, p.y))]
    for i in range(3):
        swaps[i].start()
        swaps[i].wait_recv()
        sm[4 * i + 4 : 4 * i + 8] = sm[4 * i : 4 * i + 4] + sm_got[i]
        if i == 1:
            steps[3][3]()
    last = [pltpu.make_async_remote_copy(src_ref=sm.at[12 + (p.z + d) % 4], dst_ref=sm_piece.at[d - 1], send_sem=ssend.at[2 + d], recv_sem=srecv.at[2 + d], device_id=p.up(d), device_id_type=MESH) for d in (1, 2, 3)]
    for s in last:
        s.start()
    steps[3][4]()
    for s in last:
        s.wait_recv()
    sm_out[...] = sm[12 + p.z] + sm_piece[0] + sm_piece[1] + sm_piece[2]
    steps[3][5]()
    for s in steps:
        s[6]()
    for s in swaps + last:
        s.wait_send()
    for r in red:
        r.drain()


def backward(tok, norm_one, qkv, vec, index, q, k, v, attend, gctx, gres, small_mlp, small_up, dout, dup, ddown):
    n = tok.shape[0]
    grads = (ddown, dup, dout, S((4, D // 4, 3 * D), BF))
    outs = tuple(S(g.shape[1:], BF) for g in grads)
    bufs = []
    for g in grads:
        _, rows, cols = g.shape
        h = cols // 2
        bufs += [pltpu.VMEM((4, rows, h), BF), pltpu.VMEM((4, rows, h), BF), pltpu.VMEM((2, 4, rows // 4, h), BF), pltpu.VMEM((4, rows // 4, h), BF), pltpu.VMEM((3, rows // 4, h), BF)]
    return pl.pallas_call(
        backward_kernel,
        out_shape=(S((n, SEQ, D), F32), S((32, 256), F32), outs[3], outs[2], outs[1], outs[0]),
        in_specs=[VMEM, VMEM, ANY] + [VMEM] * 10 + [ANY] * 3, out_specs=(VMEM,) * 6,
        scratch_shapes=[pltpu.VMEM((16, SP, KP), F32), pltpu.VMEM((n, SP, 3 * D), BF), pltpu.VMEM((4, D // 4, 3 * D), BF), pltpu.VMEM((4, D // 4, 3 * D), BF),
                        pltpu.VMEM((8, D), F32), pltpu.VMEM((96, 128), F32), pltpu.VMEM((16, 32, 256), F32), pltpu.VMEM((3, 4, 32, 256), F32), pltpu.VMEM((3, 32, 256), F32)] + bufs + [
                            pltpu.SemaphoreType.DMA(()), pltpu.SemaphoreType.DMA((4, 14)), pltpu.SemaphoreType.DMA((4, 14)), pltpu.SemaphoreType.DMA((4,)),
                            pltpu.SemaphoreType.DMA((6,)), pltpu.SemaphoreType.DMA((6,))],
        compiler_params=params(collective_id=1, has_side_effects=True), name="backward")(
            tok, norm_one, qkv, vec, index, q, k, v, attend, gctx, gres, small_mlp, small_up, dout, dup, ddown)


def wide_body(tokens, first_gain, first_shift, qkv_weight, query_bias, value_bias, bias_table, bias_index, out_weight, out_bias, first_scale,
              second_gain, second_shift, up_weight, up_bias, down_weight, down_bias, second_scale, patch_mask, upstream):
    n = tokens.shape[0]

    def whole(v):
        return lax.all_gather(v, "fsdp", axis=0, tiled=True)

    vectors = (first_gain, first_shift, query_bias, value_bias, out_bias, first_scale, second_gain, second_shift, down_bias, second_scale)
    vec = jnp.pad(lax.all_gather(jnp.stack(vectors), "fsdp", axis=1, tiled=True).astype(F32), ((0, 6), (0, 0)))
    upb = whole(up_bias).astype(F32).reshape(1, FF)
    table = jnp.pad(whole(bias_table).T.astype(F32), ((0, 4), (0, 768 - RELS)))
    qkv, outw, upw, downw = whole(qkv_weight), whole(out_weight), whole(up_weight), whole(down_weight)
    index = pad_index(bias_index)
    mask = jnp.pad(patch_mask.astype(F32), ((0, 8 - n), (0, KP - SEQ)))
    norm_one, relative = front(tokens, vec, table, index)
    q, k, v, attend, context = attention(norm_one, qkv, vec, relative)
    layer_out, dout, dup, ddown, gctx, gres, small_mlp, small_up = mlp(tokens, context, outw, upw, downw, vec, upb, mask, upstream)
    tgrad, dqkv, small, tab = back(tokens, norm_one, qkv, vec, index, q, k, v, attend, gctx, gres)
    tab = tab.reshape(6, 16, 128)[:, :HEADS].transpose(1, 0, 2).reshape(HEADS, 768)[:, :RELS].T

    def summed(g):
        part = lax.psum_scatter(g.astype(BF), "fsdp", scatter_dimension=0, tiled=True)
        return lax.psum(part.astype(F32), "dp")

    rows = lax.psum(lax.psum_scatter(jnp.concatenate([small[2:4], small[0:2], small_mlp[::-1][2:]]), "fsdp", scatter_dimension=1, tiled=True), "dp")
    g1, s1, qb, vb, ob, sc1, s2, g2, db, sc2 = rows
    return (layer_out, tgrad, g1, s1, summed(dqkv), qb, vb, summed(tab), summed(dout), ob, sc1, g2, s2, summed(dup), summed(small_up.reshape(FF)), summed(ddown), db, sc2)


def body(wide, tokens, first_gain, first_shift, qkv_weight, query_bias, value_bias, bias_table, bias_index, out_weight, out_bias, first_scale,
         second_gain, second_shift, up_weight, up_bias, down_weight, down_bias, second_scale, patch_mask, upstream):
    if wide:
        return wide_body(tokens, first_gain, first_shift, qkv_weight, query_bias, value_bias, bias_table, bias_index, out_weight, out_bias, first_scale,
                         second_gain, second_shift, up_weight, up_bias, down_weight, down_bias, second_scale, patch_mask, upstream)
    n = tokens.shape[0]
    vectors = (first_gain, first_shift, query_bias, value_bias, out_bias, first_scale, second_gain, second_shift, down_bias, second_scale)
    small = stack_small(vectors, up_bias, bias_table)
    index = pad_index(bias_index)
    mask = jnp.pad(patch_mask.astype(F32), ((0, 8 - n), (0, KP - SEQ)))
    norm_one, q, k, v, attend, context, vec, upb, qkv_f, out_f, up_f, down_f = forward(tokens, small, index, qkv_weight, out_weight, up_weight, down_weight)
    layer_out, dout, dup, ddown, gctx, gres, small_mlp, small_up = mlp(
        tokens, context, out_f.reshape(D, D), up_f.reshape(D, FF), down_f.reshape(FF, D), vec, upb, mask, upstream)
    tgrad, sm, rqkv, rout, rup, rdown = backward(tokens, norm_one, qkv_f, vec, index, q, k, v, attend, gctx, gres, small_mlp, small_up,
                                                 dout.reshape(4, D // 4, D), dup.reshape(4, D // 4, FF), ddown.reshape(4, FF // 4, D))
    rows = [sm[i, :192] for i in range(10)]
    gub = sm[10:14, :192].reshape(768)
    gtab = sm[16:28, :183].T
    f = lambda t: t.astype(F32)
    g1, s1, qb, vb, ob, sc1, g2, s2, db, sc2 = rows
    return (layer_out, tgrad, g1, s1, f(rqkv), qb, vb, gtab, f(rout), ob, sc1, g2, s2, f(rup), gub, f(rdown), db, sc2)


def solution(mesh):
    vector, matrix, batch = P("fsdp"), P("fsdp", None), P(("dp", "fsdp"), None, None)
    in_specs = (batch, vector, vector, matrix, vector, vector, matrix, P(), matrix, vector, vector, vector, vector, matrix, vector, matrix, vector, vector,
                P(("dp", "fsdp"), None), batch)
    out_specs = (batch, batch, vector, vector, matrix, vector, vector, matrix, matrix, vector, vector, vector, vector, matrix, vector, matrix, vector, vector)
    wide = mesh.shape["dp"] != 8 or mesh.shape["fsdp"] != 4
    return jax.shard_map(functools.partial(body, wide), mesh=mesh, in_specs=in_specs, out_specs=out_specs, check_vma=False)
```

```python
import functools
import jax
import jax.numpy as jnp
from jax import lax
from jax.experimental import pallas as pl
from jax.experimental.pallas import tpu as pltpu
from jax.sharding import PartitionSpec as P

D = 768
HEADS = 12
HEAD_DIM = 64
FF = 3072
SEQ = 197
RELS = 732
SP = 208
KP = 256
HALF = SP * KP
EPS = 1e-06
BF = jnp.bfloat16
F32 = jnp.float32
VMEM = pl.BlockSpec(memory_space=pltpu.VMEM)
ANY = pl.BlockSpec(memory_space=pl.ANY)
LIMIT = 62 * 2**20


def dot(a, b):
    return lax.dot_general(a, b, (((1,), (0,)), ((), ())), preferred_element_type=F32)


def dot_nt(a, b):
    return lax.dot_general(a, b, (((1,), (1,)), ((), ())), preferred_element_type=F32)


def dot_tn(a, b):
    return lax.dot_general(a, b, (((0,), (0,)), ((), ())), preferred_element_type=F32)


def rowmean(v):
    return jnp.sum(v, axis=-1, keepdims=True) * (1.0 / D)


def colsum(v):
    return jnp.sum(v, axis=0, keepdims=True)


def xhat_of(v):
    centred = v - rowmean(v)
    rstd = lax.rsqrt(rowmean(centred * centred) + EPS)
    return centred * rstd, rstd


def pad_rows(v):
    return jnp.concatenate([v, jnp.zeros((SP - SEQ, v.shape[1]), v.dtype)], axis=0)


GAIN1, SHIFT1, QBIAS, VBIAS, OBIAS, SCALE1, GAIN2, SHIFT2, DBIAS, SCALE2 = range(10)


def front_kernel(tok, vec, table, index, norm_one, relative):
    images = tok.shape[0]
    gain, shift = vec[GAIN1 : GAIN1 + 1, :], vec[SHIFT1 : SHIFT1 + 1, :]
    for b in range(images):
        xhat, _ = xhat_of(pad_rows(tok[b].astype(F32)))
        norm_one[b] = (xhat * gain + shift).astype(BF)
    lookup(table, index, [relative.at[h] for h in range(HEADS)])


def lookup(table, index, relative):
    lanes = lax.broadcasted_iota(jnp.int32, (16, 128), 1)

    def rows(r, carry):
        at = pl.ds(pl.multiple_of(r * 16, 16), 16)
        for half in range(2):
            idx = index[at, half * 128 : half * 128 + 128]
            low = idx & 127
            high = idx >> 7
            for h in range(HEADS):
                out = jnp.zeros((16, 128), F32)
                for c in range(6):
                    part = jnp.broadcast_to(table[h : h + 1, c * 128 : c * 128 + 128], (16, 128))
                    got = jnp.take_along_axis(part, low, axis=1, mode="promise_in_bounds")
                    out = jnp.where(high == c, got, out)
                if half == 1:
                    out = jnp.where(lanes < SEQ - 128, out, -1e30)
                relative[h][at, half * 128 : half * 128 + 128] = out.astype(BF)
        return carry

    lax.fori_loop(0, SP // 16, rows, 0)


def lane_masks(rows):
    lane = lax.broadcasted_iota(jnp.int32, (rows, 128), 1)
    return lane < HEAD_DIM


def split_heads(v, first):
    zero = jnp.zeros_like(v)
    return jnp.where(first, v, zero), jnp.where(first, zero, v)


def project(norm_one, qkv, vec, q, k, v):
    images = norm_one.shape[0]
    k[:, SP:, :] = jnp.zeros((images, KP - SP, D), BF)
    v[:, SP:, :] = jnp.zeros((images, KP - SP, D), BF)

    def chunk(i, carry):
        at = pl.ds(pl.multiple_of(i * 256, 256), 256)
        rows = norm_one[...].reshape(images * SP, D)
        pq = dot(rows, qkv[:, at])
        q[:, :, at] = ((pq + vec[QBIAS : QBIAS + 1, at]) * 0.125).astype(BF).reshape(images, SP, 256)
        pk = dot(rows, qkv[:, pl.ds(pl.multiple_of(D + i * 256, 256), 256)])
        k[:, :SP, at] = pk.astype(BF).reshape(images, SP, 256)
        pv = dot(rows, qkv[:, pl.ds(pl.multiple_of(2 * D + i * 256, 256), 256)])
        v[:, :SP, at] = (pv + vec[VBIAS : VBIAS + 1, at]).astype(BF).reshape(images, SP, 256)
        return carry

    lax.fori_loop(0, D // 256, chunk, 0)


def attend_pair(b, hp, at, q, k, v, relative, attend, context):
    first = lane_masks(KP)
    q2 = q[b, :, at]
    ks = split_heads(k[b, :, at], first)
    vs = split_heads(v[b, :, at], first)
    probs = []
    for e in range(2):
        h = 2 * hp + e
        s = dot_nt(q2, ks[e]) + relative[h][...].astype(F32)
        s = jnp.exp(s - jnp.max(s, axis=-1, keepdims=True))
        p = (s * (1.0 / jnp.sum(s, axis=-1, keepdims=True))).astype(BF)
        attend[b, h] = p
        probs.append(p)
    context[b, :, at] = (dot(probs[0], vs[0]) + dot(probs[1], vs[1])).astype(BF)


def attention_kernel(norm_one, qkv, vec, relative, q, k, v, attend, context):
    images = norm_one.shape[0]
    relative = [relative.at[h] for h in range(HEADS)]
    project(norm_one, qkv, vec, q, k, v)

    def image(b, carry):
        for hp in range(HEADS // 2):
            attend_pair(b, hp, slice(hp * 128, hp * 128 + 128), q, k, v, relative, attend, context)
        return carry

    lax.fori_loop(0, images, image, 0)


def gelu_both(v):
    cdf = 0.5 * (1.0 + lax.erf(v * 0.7071067811865476))
    pdf = jnp.exp(v * v * -0.5) * 0.3989422804014327
    return v * cdf, cdf + v * pdf


def mlp_kernel(tok, ctx, out_hbm, up_hbm, down_hbm, vec, upb, mask, ups,
               layer_out, dout, dup, ddown, gctx, gres, small, small_up,
               outw, upw, downw, hid, att, n2, act, slope, acc, gd, gy_s, sems):
    images = tok.shape[0]
    R = images * SP
    loads = [pltpu.make_async_copy(s, d, sems.at[i]) for i, (s, d) in enumerate(
        ((out_hbm, outw), (up_hbm, upw), (down_hbm, downw)))]
    for l in loads:
        l.start()
    obias, scale1 = vec[OBIAS : OBIAS + 1, :], vec[SCALE1 : SCALE1 + 1, :]
    gain2, shift2 = vec[GAIN2 : GAIN2 + 1, :], vec[SHIFT2 : SHIFT2 + 1, :]
    dbias, scale2 = vec[DBIAS : DBIAS + 1, :], vec[SCALE2 : SCALE2 + 1, :]
    maskt = jnp.transpose(mask[...], (1, 0))
    loads[0].wait()
    for b in range(images):
        attn = dot(ctx[b], outw[...]) + obias
        att[b] = attn
        h = pad_rows(tok[b].astype(F32)) + scale1 * attn
        hid[b] = h
        xhat, _ = xhat_of(h)
        n2[b] = (xhat * gain2 + shift2).astype(BF)
    loads[1].wait()
    loads[2].wait()
    acc[...] = jnp.zeros_like(acc)
    W = 256

    def forward(f, carry):
        at = pl.ds(pl.multiple_of(f * W, W), W)
        for b in range(images):
            u = dot(n2[b], upw[:, at]) + upb[:, at]
            g, s = gelu_both(u)
            g = g.astype(BF)
            act[b, :, at] = g
            slope[b, :, at] = s.astype(BF)
            acc[b] += dot(g, downw[at, :])
        return carry

    lax.fori_loop(0, FF // W, forward, 0)
    sums = [jnp.zeros((1, D), F32) for _ in range(6)]
    for b in range(images):
        down = acc[b] + dbias
        layer_out[b] = (hid[b] + scale2 * down).astype(BF)[:SEQ]
        gy = pad_rows(ups[b].astype(F32)) * maskt[:SP, b : b + 1]
        gy_s[b] = gy.astype(BF)
        sums[0] += colsum(gy * down)
        full = gy * scale2
        sums[1] += colsum(full)
        gd[b] = full.astype(BF)
    acc[...] = jnp.zeros_like(acc)

    def backward(f, carry):
        at = pl.ds(pl.multiple_of(f * W, W), W)
        total = jnp.zeros((1, W), F32)
        lows = []
        for b in range(images):
            gg = dot_nt(gd[b], downw[at, :]) * slope[b, :, at].astype(F32)
            total += colsum(gg)
            low = gg.astype(BF)
            lows.append(low)
            acc[b] += dot_nt(low, upw[:, at])
        small_up[:, at] = total
        low = jnp.concatenate(lows, axis=0)
        dup[:, at] = dot_tn(n2[...].reshape(R, D), low).astype(BF)
        ddown[at, :] = dot_tn(act[:, :, at].reshape(R, W), gd[...].reshape(R, D)).astype(BF)
        return carry

    lax.fori_loop(0, FF // W, backward, 0)
    for b in range(images):
        xhat, rstd = xhat_of(hid[b])
        g = acc[b]
        sums[2] += colsum(g * xhat)
        sums[3] += colsum(g)
        gg = g * gain2
        gh = (gg - rowmean(gg) - xhat * rowmean(gg * xhat)) * rstd
        res = gy_s[b].astype(F32) + gh
        gres[b] = res
        sums[4] += colsum(res * att[b])
        full = res * scale1
        sums[5] += colsum(full)
        n2[b] = full.astype(BF)
    dout[...] = dot_tn(ctx[...].reshape(R, D), n2[...].reshape(R, D)).astype(BF)
    for b in range(images):
        gctx[b] = dot_nt(n2[b], outw[...]).astype(BF)
    small[...] = jnp.concatenate(sums + [jnp.zeros((2, D), F32)], axis=0)


def attend_back(b, hp, at, q, k, v, attend, gctx, gtab, gq, gk, gv, qsum, vsum):
    first = lane_masks(KP)
    firsts = first[:SP]
    v2 = split_heads(v[b, :, at], first)
    k2 = split_heads(k[b, :, at], first)
    q2 = split_heads(q[b, :, at], firsts)
    g2 = gctx[b, :, at]
    gs2 = split_heads(g2, firsts)
    dq = jnp.zeros((SP, 128), F32)
    dk = jnp.zeros((KP, 128), F32)
    dv = jnp.zeros((KP, 128), F32)
    for e in range(2):
        h = 2 * hp + e
        a = attend[b, h]
        af = a.astype(F32)
        ga = dot_nt(g2, v2[e])
        w = af * ga
        inner = jnp.sum(w, axis=-1, keepdims=True)
        gs = w - af * inner
        gtab[h][...] += gs
        low = gs.astype(BF)
        dq += dot(low, k2[e])
        dk += dot_tn(low, q2[e])
        dv += dot_tn(a, gs2[e])
    dq = dq * 0.125
    qsum[:, at] += colsum(dq)
    vsum[:, at] += colsum(dv)
    gq[b, :, at] = dq.astype(BF)
    gk[b, :, at] = dk[:SP].astype(BF)
    gv[b, :, at] = dv[:SP].astype(BF)


def table_back(gtab, index, out):
    ids = lax.broadcasted_iota(jnp.int32, (128, KP), 0)

    def row(i, acc):
        idx = index[pl.ds(i, 1), :]
        low, high = idx & 127, idx >> 7
        hot = jnp.where(ids == low, 1.0, 0.0).astype(BF)
        g = jnp.concatenate([t[pl.ds(i, 1), :] for t in gtab] + [jnp.zeros((4, KP), F32)], axis=0)
        g1 = g.astype(BF).astype(F32)
        g2 = g - g1
        parts = []
        for src in (g1, g2):
            for c in range(6):
                parts.append(jnp.where(high == c, src, 0.0).astype(BF))
        return acc + dot_nt(jnp.concatenate(parts, axis=0), hot)

    acc = lax.fori_loop(0, SEQ, row, jnp.zeros((192, 128), F32))
    out[...] = acc[:96] + acc[96:]


def back_kernel(tok, norm_one, qkv_hbm, vec, index, q, k, v, attend, gctx, gres,
                tgrad, dqkv, small, tab, gtab, gqkv, qkv, sem):
    images = tok.shape[0]
    R = images * SP
    load = pltpu.make_async_copy(qkv_hbm, qkv, sem)
    load.start()
    gtab[...] = jnp.zeros_like(gtab)
    gtab = [gtab.at[h] for h in range(HEADS)]
    small[...] = jnp.zeros_like(small)
    gq, gk, gv = (gqkv.at[:, :, i * D : (i + 1) * D] for i in range(3))
    qsum, vsum = small.at[0:1, :], small.at[1:2, :]

    for hp in range(HEADS // 2):

        def one(b, carry, hp=hp):
            attend_back(b, hp, slice(hp * 128, hp * 128 + 128), q, k, v, attend, gctx, gtab, gq, gk, gv, qsum, vsum)
            return carry

        lax.fori_loop(0, images, one, 0)
    table_back(gtab, index, tab)

    def chunk(i, carry):
        at = pl.ds(pl.multiple_of(i * 256, 256), 256)
        dqkv[:, at] = dot_tn(norm_one[...].reshape(R, D), gqkv[:, :, at].reshape(R, 256)).astype(BF)
        return carry

    lax.fori_loop(0, 3 * D // 256, chunk, 0)
    load.wait()
    gain = vec[GAIN1 : GAIN1 + 1, :]
    for b in range(images):
        xhat, rstd = xhat_of(pad_rows(tok[b].astype(F32)))
        g = dot_nt(gqkv[b], qkv[...])
        small[2:3, :] += colsum(g * xhat)
        small[3:4, :] += colsum(g)
        gg = g * gain
        gi = (gg - rowmean(gg) - xhat * rowmean(gg * xhat)) * rstd
        tgrad[b] = (gres[b] + gi)[:SEQ]


def params(**kw):
    return pltpu.CompilerParams(vmem_limit_bytes=LIMIT, **kw)


def S(shape, dtype):
    return jax.ShapeDtypeStruct(shape, dtype)


def front(tok, vec, table, index):
    n = tok.shape[0]
    return pl.pallas_call(front_kernel, out_shape=(S((n, SP, D), BF), S((HEADS, SP, KP), BF)),
                          in_specs=[VMEM] * 4, out_specs=(VMEM, VMEM), compiler_params=params(), name="front")(tok, vec, table, index)


def attention(norm_one, qkv, vec, relative):
    n = norm_one.shape[0]
    return pl.pallas_call(attention_kernel,
                          out_shape=(S((n, SP, D), BF), S((n, KP, D), BF), S((n, KP, D), BF), S((n, HEADS, SP, KP), BF), S((n, SP, D), BF)),
                          in_specs=[VMEM] * 4, out_specs=(VMEM,) * 5, compiler_params=params(), name="attention")(norm_one, qkv, vec, relative)


def mlp(tok, ctx, outw, upw, downw, vec, upb, mask, ups):
    n = tok.shape[0]
    return pl.pallas_call(
        mlp_kernel,
        out_shape=(S((n, SEQ, D), BF), S((D, D), BF), S((D, FF), BF), S((FF, D), BF), S((n, SP, D), BF), S((n, SP, D), F32), S((8, D), F32), S((1, FF), F32)),
        in_specs=[VMEM, VMEM, ANY, ANY, ANY, VMEM, VMEM, VMEM, VMEM], out_specs=(VMEM,) * 8,
        scratch_shapes=[pltpu.VMEM((D, D), BF), pltpu.VMEM((D, FF), BF), pltpu.VMEM((FF, D), BF),
                        pltpu.VMEM((n, SP, D), F32), pltpu.VMEM((n, SP, D), F32), pltpu.VMEM((n, SP, D), BF),
                        pltpu.VMEM((n, SP, FF), BF), pltpu.VMEM((n, SP, FF), BF), pltpu.VMEM((n, SP, D), F32),
                        pltpu.VMEM((n, SP, D), BF), pltpu.VMEM((n, SP, D), BF), pltpu.SemaphoreType.DMA((3,))],
        compiler_params=params(), name="mlp")(tok, ctx, outw, upw, downw, vec, upb, mask, ups)


def back(tok, norm_one, qkv, vec, index, q, k, v, attend, gctx, gres):
    n = tok.shape[0]
    return pl.pallas_call(
        back_kernel,
        out_shape=(S((n, SEQ, D), F32), S((D, 3 * D), BF), S((8, D), F32), S((96, 128), F32)),
        in_specs=[VMEM, VMEM, ANY] + [VMEM] * 8, out_specs=(VMEM,) * 4,
        scratch_shapes=[pltpu.VMEM((16, SP, KP), F32), pltpu.VMEM((n, SP, 3 * D), BF), pltpu.VMEM((D, 3 * D), BF), pltpu.SemaphoreType.DMA(())],
        compiler_params=params(), name="back")(tok, norm_one, qkv, vec, index, q, k, v, attend, gctx, gres)


def pad_index(bias_index):
    return jnp.pad(bias_index, ((0, SP - SEQ), (0, KP - SEQ)))
MESH = pl.DeviceIdType.MESH


class Place:
    def __init__(self):
        dp, z = lax.axis_index("dp"), lax.axis_index("fsdp")
        y, x, c = dp // 4, (dp // 2) % 2, dp % 2
        xn, yn = dp + 2 - 4 * x, dp + 4 - 8 * y
        q = dp // 2
        qx, qy = q + 1 - 2 * x, q + 2 - 4 * y
        self.dp, self.z, self.c, self.q = dp, z, c, q
        self.near = (xn * (1 - c) + yn * c, z)
        self.far = (yn * (1 - c) + xn * c, z)
        self.x, self.y = (xn, z), (yn, z)
        self.twin = (dp + 1 - 2 * c, z)
        self.q_near = qx * (1 - c) + qy * c
        self.q_far = qy * (1 - c) + qx * c
        self.q_both = 3 - q

    def up(self, d):
        return (self.dp, (self.z + d) % 4)

    def barrier(self):
        sem = pltpu.get_barrier_semaphore()
        peers = [self.near, self.far, self.twin] + [self.up(d) for d in (1, 2, 3)]
        for peer in peers:
            pl.semaphore_signal(sem, inc=1, device_id=peer, device_id_type=MESH)
        pl.semaphore_wait(sem, len(peers))


def aligned(i, size):
    return pl.ds(pl.multiple_of(i * size, size), size)


class Gather:
    def __init__(self, place, shard, full, send, recv, local):
        self.p, self.shard, self.full, self.send, self.recv, self.local = place, shard, full, send, recv, local
        self.rows, self.cols = shard.shape[0] // 4, shard.shape[1] // 2

    def region(self, zb, q, c):
        return self.full.at[zb, aligned(q, self.rows), aligned(c, self.cols)]

    def copy(self, d, slot, src, dst, peer):
        return pltpu.make_async_remote_copy(src_ref=src, dst_ref=dst, send_sem=self.send.at[d - 1, slot], recv_sem=self.recv.at[d - 1, slot],
                                            device_id=peer, device_id_type=MESH)

    def over_z(self, d):
        p = self.p
        src = self.shard.at[aligned(p.q, self.rows), aligned(p.c, self.cols)]
        return self.copy(d, 0, src, self.region(p.z, p.q, p.c), p.up(d))

    def passed(self, d, slot, q, peer):
        p = self.p
        r = self.region((p.z + 4 - d) % 4, q, p.c)
        return self.copy(d, slot, r, r, peer)

    def own(self):
        return pltpu.make_async_copy(self.shard, self.full.at[self.p.z], self.local)

    def begin(self):
        for d in (1, 2, 3):
            self.over_z(d).start()
        self.own().start()

    def part(self, d, i):
        p = self.p
        slot, q, peer = ((1, p.q, p.near), (2, p.q, p.far), (4, p.q, p.twin), (3, p.q_near, p.far), (5, p.q_near, p.twin),
                         (6, p.q_far, p.twin), (7, p.q_both, p.twin))[i]
        return self.passed(d, slot, q, peer)

    def spread(self, d):
        self.over_z(d).wait_recv()
        for i in (0, 1, 2):
            self.part(d, i).start()

    def relay(self, d):
        self.part(d, 0).wait_recv()
        for i in (3, 4):
            self.part(d, i).start()

    def close(self, d):
        self.part(d, 1).wait_recv()
        self.part(d, 5).start()
        self.part(d, 3).wait_recv()
        self.part(d, 6).start()

    def finish(self):
        self.own().wait()
        for d in (1, 2, 3):
            for i in (2, 4, 5, 6):
                self.part(d, i).wait_recv()

    def drain(self):
        for d in (1, 2, 3):
            self.over_z(d).wait_send()
            for i in range(7):
                self.part(d, i).wait_send()

    def steps(self):
        return [lambda d=d: self.spread(d) for d in (1, 2, 3)] + [lambda d=d: self.relay(d) for d in (1, 2, 3)] + [
            lambda d=d: self.close(d) for d in (1, 2, 3)] + [self.finish]


class Reduce:
    def __init__(self, place, grad, got, half, quarter, pieces, out, send, recv, local):
        self.p, self.grad, self.got, self.half, self.quarter, self.pieces, self.out = place, grad, got, half, quarter, pieces, out
        self.send, self.recv, self.local = send, recv, local
        self.rows, self.cols = grad.shape[1] // 4, grad.shape[2] // 2

    def copy(self, slot, src, dst, peer):
        return pltpu.make_async_remote_copy(src_ref=src, dst_ref=dst, send_sem=self.send.at[slot], recv_sem=self.recv.at[slot], device_id=peer, device_id_type=MESH)

    def twin(self, i):
        q = self.quarters()[i]
        return self.copy(14 + i, self.grad.at[:, aligned(q, self.rows), aligned(1 - self.p.c, self.cols)], self.got(q), self.p.twin)

    def quarters(self):
        p = self.p
        return (p.q_far, p.q_both, p.q, p.q_near)

    def mine(self, q):
        return self.grad.at[:, aligned(q, self.rows), aligned(self.p.c, self.cols)]

    def near(self, i):
        q = (self.p.q_near, self.p.q_both)[i]
        return self.copy(1 + i, self.mine(q), self.half.at[i], self.p.near)

    def far(self):
        return self.copy(3, self.half.at[1], self.quarter, self.p.far)

    def over_z(self, d):
        return self.copy(3 + d, self.quarter.at[(self.p.z + d) % 4], self.pieces.at[d - 1], self.p.up(d))

    def region(self, q):
        return self.out.at[aligned(q, self.rows), aligned(self.p.c, self.cols)]

    def passed(self, i):
        p = self.p
        q, peer = ((p.q, p.near), (p.q, p.far), (p.q, p.twin), (p.q_near, p.far), (p.q_near, p.twin), (p.q_far, p.twin), (p.q_both, p.twin))[i]
        src = self.quarter.at[p.z] if i < 3 else self.region(q)
        return self.copy(7 + i, src, self.region(q), peer)

    def own(self):
        return pltpu.make_async_copy(self.quarter.at[self.p.z], self.region(self.p.q), self.local)

    def begin(self):
        for i in range(4):
            self.twin(i).start()

    def add(self, dst, src):
        def one(i, carry):
            dst[i] = (dst[i].astype(F32) + src[i].astype(F32)).astype(BF)
            return carry

        lax.fori_loop(0, 4, one, 0)

    def fold(self, q):
        self.add(self.mine(q), self.got(q))

    def first_a(self):
        self.twin(0).wait_recv()
        self.fold(self.p.q_near)
        self.near(0).start()

    def first_b(self):
        self.twin(1).wait_recv()
        self.fold(self.p.q_both)
        self.near(1).start()

    def first_c(self):
        self.twin(2).wait_recv()
        self.fold(self.p.q)
        self.twin(3).wait_recv()
        self.fold(self.p.q_far)

    def second(self):
        self.near(1).wait_recv()
        self.add(self.half.at[1], self.mine(self.p.q_far))
        self.far().start()
        self.near(0).wait_recv()
        self.add(self.half.at[0], self.mine(self.p.q))

    def third(self):
        self.far().wait_recv()
        self.add(self.quarter, self.half.at[0])
        for d in (1, 2, 3):
            self.over_z(d).start()

    def fourth(self):
        for d in (1, 2, 3):
            self.over_z(d).wait_recv()
        total = self.quarter[self.p.z].astype(F32)
        for d in (1, 2, 3):
            total += self.pieces[d - 1].astype(F32)
        self.quarter[self.p.z] = total.astype(BF)
        for i in (0, 1, 2):
            self.passed(i).start()
        self.own().start()

    def fifth(self):
        self.passed(0).wait_recv()
        self.passed(3).start()
        self.passed(4).start()

    def sixth(self):
        self.passed(1).wait_recv()
        self.passed(5).start()
        self.passed(3).wait_recv()
        self.passed(6).start()

    def finish(self):
        for i in (2, 4, 5, 6):
            self.passed(i).wait_recv()
        self.own().wait()

    def drain(self):
        for i in range(4):
            self.twin(i).wait_send()
        self.near(0).wait_send()
        self.near(1).wait_send()
        self.far().wait_send()
        for d in (1, 2, 3):
            self.over_z(d).wait_send()
        for i in range(7):
            self.passed(i).wait_send()
def stack_small(vectors, up_bias, table):
    k = vectors[0].shape[0]
    rows = jnp.concatenate([jnp.stack(vectors), up_bias.reshape(-1, k), jnp.zeros((2, k), BF)], axis=0)
    rows = jnp.pad(rows, ((0, 0), (0, 256 - k)))
    table = jnp.pad(table.T, ((0, 4), (0, 256 - table.shape[0])))
    return jnp.concatenate([rows, table], axis=0)


def unstack_small(block, vec, upb, table):
    vec[...] = jnp.zeros_like(vec)
    table[...] = jnp.zeros_like(table)
    for z in range(4):
        part = block[z].astype(F32)
        vec[:, z * 192 : z * 192 + 192] = part[:16, :192]
        for k in range(4):
            upb[:, z * 768 + k * 192 : z * 768 + k * 192 + 192] = part[10 + k : 11 + k, :192]
        table[:, z * 183 : z * 183 + 183] = part[16:32, :183]


def head_view(ref, h):
    return ref.at[h // 3, :, (h % 3) * 256 : (h % 3) * 256 + 256]


def layer_kernel(tok, ups, small_in, index, mask, qkv_s, out_s, up_s, down_s,
                 lo_hbm, tg_hbm, sm_out, rqkv, rout, rup, rdown,
                 qkv, outw, upw, downw, A, B, hid, att, acc, n1, q, k, v, ctx, n2, gd, lo, attend, vec, upb, table, block,
                 sums, upsum, tab, sm, sm_got, sm_piece,
                 half0, quart0, piece0, half1, quart1, piece1, got2, half2, quart2, piece2, got3, half3, quart3, piece3,
                 gsend, grecv, rsend, rrecv, local, ssend, srecv, free):
    p = Place()
    p.barrier()
    images = tok.shape[0]
    R = images * SP

    gathers = [Gather(p, s, f, gsend.at[i], grecv.at[i], local.at[i]) for i, (s, f) in enumerate(((qkv_s, qkv), (out_s, outw), (up_s, upw), (down_s, downw)))]
    block[p.z] = small_in[...]
    smalls = [pltpu.make_async_remote_copy(src_ref=small_in, dst_ref=block.at[p.z], send_sem=ssend.at[d - 1], recv_sem=srecv.at[d - 1], device_id=p.up(d), device_id_type=MESH) for d in (1, 2, 3)]
    for s in smalls:
        s.start()
    for g in gathers:
        g.begin()
    for s in smalls:
        s.wait_recv()
    unstack_small(block, vec, upb, table)
    row = lambda i: vec[i : i + 1, :]
    todo = []

    def advance(n):
        for _ in range(min(n, len(todo))):
            todo.pop(0)()

    g0, g1, g2, g3 = (g.steps() for g in gathers)
    todo += g0[:9]
    for b in range(images):
        xhat, _ = xhat_of(pad_rows(tok[b].astype(F32)))
        n1[b] = (xhat * row(GAIN1) + row(SHIFT1)).astype(BF)
        advance(1)
    relative = [head_view(gd, h) for h in range(HEADS)]
    lookup(table, index, relative)
    advance(len(todo))
    todo += g1[:6]
    advance(3)
    g0[9]()
    todo += g1[6:9] + g2[:6] + g1[9:] + g3[:3] + g2[6:9] + g3[3:6] + g2[9:] + g3[6:]

    k[:, SP:, :] = jnp.zeros((images, KP - SP, D), BF)
    v[:, SP:, :] = jnp.zeros((images, KP - SP, D), BF)
    for i in range(D // 256):
        at = slice(i * 256, i * 256 + 256)

        def weight(j):
            return qkv[:, :, j * D + i * 256 : j * D + i * 256 + 256].reshape(D, 256)

        rows = n1[...].reshape(R, D)
        q[:, :, at] = ((dot(rows, weight(0)) + vec[QBIAS : QBIAS + 1, at]) * 0.125).astype(BF).reshape(images, SP, 256)
        k[:, :SP, at] = dot(rows, weight(1)).astype(BF).reshape(images, SP, 256)
        v[:, :SP, at] = (dot(rows, weight(2)) + vec[VBIAS : VBIAS + 1, at]).astype(BF).reshape(images, SP, 256)
        advance(2)
    for hp in range(HEADS // 2):

        def one(b, carry, hp=hp):
            attend_pair(b, hp, slice(hp * 128, hp * 128 + 128), q, k, v, relative, attend, ctx)
            return carry

        lax.fori_loop(0, images, one, 0)
        advance(1)

    while todo and g1[9] in todo:
        advance(1)
    for b in range(images):
        attn = dot(ctx[b], outw[...].reshape(D, D)) + row(OBIAS)
        att[b] = attn
        h = pad_rows(tok[b].astype(F32)) + row(SCALE1) * attn
        hid[b] = h
        xhat, _ = xhat_of(h)
        n2[b] = (xhat * row(GAIN2) + row(SHIFT2)).astype(BF)
    while todo and g2[9] in todo:
        advance(1)
    W = 256

    def expand(f, carry):
        at = aligned(f, W)
        for b in range(images):
            u = dot(n2[b], upw[:, :, at].reshape(D, W)) + upb[:, at]
            g, s = gelu_both(u)
            A[b, :, at] = g.astype(BF)
            B[b, :, at] = s.astype(BF)
        return carry

    for part in range(4):
        lax.fori_loop(part * 3, part * 3 + 3, expand, 0)
        advance(1)
    advance(len(todo))
    for i in range(D // 256):
        at = slice(i * 256, i * 256 + 256)
        acc[:, :, at] = dot(A[...].reshape(R, FF), downw[:, :, at].reshape(FF, 256)).reshape(images, SP, 256)
    maskt = jnp.transpose(mask[...], (1, 0))
    sums[...] = jnp.zeros_like(sums)

    def add_sum(i, value):
        sums[i : i + 1, :] += colsum(value)

    def grad_y(b):
        return pad_rows(ups[b].astype(F32)) * maskt[:SP, b : b + 1]

    for b in range(images):
        down = acc[b] + row(DBIAS)
        lo[b] = (hid[b] + row(SCALE2) * down).astype(BF)
        gy = grad_y(b)
        add_sum(SCALE2, gy * down)
        full = gy * row(SCALE2)
        add_sum(DBIAS, full)
        gd[b] = full.astype(BF)
    lo_copy = pltpu.make_async_copy(lo, lo_hbm, local.at[8])
    lo_copy.start()

    for g in gathers:
        g.drain()

    def contract(f, carry):
        at = aligned(f, W)
        z, r = f // 3, f % 3
        rows = aligned(r, W)
        total = jnp.zeros((1, W), F32)
        for b in range(images):
            gg = dot_nt(gd[b], downw[z, rows, :]) * B[b, :, at].astype(F32)
            total += colsum(gg)
            B[b, :, at] = gg.astype(BF)
        upsum[:, at] = total
        downw[z, rows, :] = dot_tn(A[:, :, at].reshape(R, W), gd[...].reshape(R, D)).astype(BF)
        return carry

    lax.fori_loop(0, FF // W, contract, 0)
    pl.semaphore_signal(free, inc=1, device_id=p.twin, device_id_type=MESH)

    def got_down(q):
        return A.at[:, :192, pl.ds(pl.multiple_of(1536 + q * 384, 128), 384)]

    def got_up(q):
        return A.at[:, aligned(q, 48), :1536]

    def got_of(ref, rows):
        return lambda q: ref.at[:, aligned(q, rows), :]

    parts = ((downw, got_down, half0, quart0, piece0, rdown), (upw, got_up, half1, quart1, piece1, rup),
             (outw, got_of(got2, 48), half2, quart2, piece2, rout), (qkv, got_of(got3, 48), half3, quart3, piece3, rqkv))
    red = [Reduce(p, *part, rsend.at[i], rrecv.at[i], local.at[4 + i]) for i, part in enumerate(parts)]
    r0, r1, r2, r3 = red
    pl.semaphore_wait(free, 1)
    r0.begin()
    todo += [r0.first_a, r0.first_b, r0.first_c]
    for i in range(4):
        acc[:, :, i * 192 : i * 192 + 192] = dot_nt(B[...].reshape(R, FF), upw[i]).reshape(images, SP, 192)
        if i:
            advance(1)

    def widen(f, carry):
        at = aligned(f, W)
        upw[:, :, at] = dot_tn(n2[...].reshape(R, D), B[:, :, at].reshape(R, W)).astype(BF).reshape(4, D // 4, W)
        return carry

    lax.fori_loop(0, FF // W, widen, 0)
    r1.begin()
    todo += [r1.first_a, r1.first_b, r1.first_c, r0.second]
    for b in range(images):
        xhat, rstd = xhat_of(hid[b])
        g = acc[b]
        add_sum(GAIN2, g * xhat)
        add_sum(SHIFT2, g)
        gg = g * row(GAIN2)
        res = grad_y(b) + (gg - rowmean(gg) - xhat * rowmean(gg * xhat)) * rstd
        hid[b] = res
        add_sum(SCALE1, res * att[b])
        full = res * row(SCALE1)
        add_sum(OBIAS, full)
        n2[b] = full.astype(BF)
        if b:
            advance(1)
    gctx = B.at[:, :, 3 * D :]
    for b in range(images):
        gctx[b] = dot_nt(n2[b], outw[...].reshape(D, D)).astype(BF)
    for i in range(3):
        at = slice(i * 256, i * 256 + 256)
        outw[:, :, at] = dot_tn(ctx[...].reshape(R, D), n2[:, :, at].reshape(R, 256)).astype(BF).reshape(4, D // 4, 256)
    r2.begin()
    todo += [r2.first_a, r2.first_b, r2.first_c, r0.third, r1.second, r0.fourth, r1.third, r0.fifth, r2.second, r0.sixth, r1.fourth, r2.third,
             r1.fifth, r1.sixth, r2.fourth, r2.fifth, r2.sixth]

    acc[...] = jnp.zeros_like(acc)
    gtab = [head_view(acc, h) for h in range(HEADS)]
    gq, gk, gv = (B.at[:, :, i * D : (i + 1) * D] for i in range(3))
    qsum, vsum = sums.at[QBIAS : QBIAS + 1, :], sums.at[VBIAS : VBIAS + 1, :]
    for hp in range(HEADS // 2):
        for part in range(2):

            def one(i, carry, hp=hp, part=part):
                attend_back(part * (images // 2) + i, hp, slice(hp * 128, hp * 128 + 128), q, k, v, attend, gctx, gtab, gq, gk, gv, qsum, vsum)
                return carry

            lax.fori_loop(0, images // 2, one, 0)
            advance(1)
    for b in range(images):
        att[b] = dot_nt(B[b, :, : 3 * D], qkv[...].reshape(D, 3 * D))
        advance(1)
    for i in range(9):
        at = slice(i * 256, i * 256 + 256)
        qkv[:, :, at] = dot_tn(n1[...].reshape(R, D), B[:, :, at].reshape(R, 256)).astype(BF).reshape(4, D // 4, 256)
    r3.begin()
    advance(len(todo))
    for b in range(images):
        xhat, rstd = xhat_of(pad_rows(tok[b].astype(F32)))
        g = att[b]
        add_sum(GAIN1, g * xhat)
        add_sum(SHIFT1, g)
        gg = g * row(GAIN1)
        att[b] = hid[b] + (gg - rowmean(gg) - xhat * rowmean(gg * xhat)) * rstd
        if b:
            (r3.first_a, r3.first_b, r3.first_c)[b - 1]()
    tg_copy = pltpu.make_async_copy(att, tg_hbm, local.at[9])
    tg_copy.start()
    table_back(gtab, index, tab)
    r3.second()
    sm[...] = jnp.zeros_like(sm)
    flat = jnp.concatenate([tab[c * 16 : c * 16 + 16, :] for c in range(6)], axis=1)
    for z in range(4):
        sm[z, 0:16, 0:192] = sums[:, z * 192 : z * 192 + 192]
        for i in range(4):
            sm[z, 10 + i : 11 + i, 0:192] = upsum[:, z * 768 + i * 192 : z * 768 + i * 192 + 192]
        sm[z, 16:32, 0:183] = flat[:, z * 183 : z * 183 + 183]

    def exchange(i, peer):
        return pltpu.make_async_remote_copy(src_ref=sm.at[pl.ds(4 * i, 4)], dst_ref=sm_got.at[i], send_sem=ssend.at[3 + i], recv_sem=srecv.at[3 + i], device_id=peer, device_id_type=MESH)

    swaps = [exchange(i, peer) for i, peer in enumerate((p.twin, p.x, p.y))]
    for i in range(3):
        swaps[i].start()
        if i == 1:
            r3.third()
        swaps[i].wait_recv()
        sm[4 * i + 4 : 4 * i + 8] = sm[4 * i : 4 * i + 4] + sm_got[i]
    last = [pltpu.make_async_remote_copy(src_ref=sm.at[12 + (p.z + d) % 4], dst_ref=sm_piece.at[d - 1], send_sem=ssend.at[5 + d], recv_sem=srecv.at[5 + d], device_id=p.up(d), device_id_type=MESH) for d in (1, 2, 3)]
    for s in last:
        s.start()
    r3.fourth()
    for s in last:
        s.wait_recv()
    sm_out[...] = sm[12 + p.z] + sm_piece[0] + sm_piece[1] + sm_piece[2]
    r3.fifth()
    r3.sixth()
    for r in red:
        r.finish()
    lo_copy.wait()
    tg_copy.wait()
    for s in smalls + swaps + last:
        s.wait_send()
    for r in red:
        r.drain()


def layer(tok, ups, small, index, mask, qkv_s, out_s, up_s, down_s):
    n = tok.shape[0]
    shards = (qkv_s, out_s, up_s, down_s)

    def vm(shape, dtype=BF):
        return pltpu.VMEM(shape, dtype)

    row3, bufs = (n, SP, D), []
    for i, s in enumerate((down_s, up_s, out_s, qkv_s)):
        rows, h = s.shape[0], s.shape[1] // 2
        bufs += [vm((4, rows, h))] * (i > 1) + [vm((2, 4, rows // 4, h)), vm((4, rows // 4, h)), vm((3, rows // 4, h))]
    dma = pltpu.SemaphoreType.DMA
    scratch = [vm((4,) + s.shape) for s in shards] + [vm((n, SP, FF)), vm((n, SP, FF)), vm(row3, F32), vm(row3, F32), vm(row3, F32),
               vm(row3), vm(row3), vm((n, KP, D)), vm((n, KP, D)), vm(row3), vm(row3), vm(row3), vm(row3), vm((n, HEADS, SP, KP)),
               vm((16, D), F32), vm((1, FF), F32), vm((16, D), F32), vm((4, 32, 256)),
               vm((16, D), F32), vm((1, FF), F32), vm((96, 128), F32), vm((16, 32, 256), F32), vm((3, 4, 32, 256), F32), vm((3, 32, 256), F32)]
    return pl.pallas_call(
        layer_kernel,
        out_shape=(S(row3, BF), S(row3, F32), S((32, 256), F32)) + tuple(S(s.shape, BF) for s in shards),
        in_specs=[VMEM] * 5 + [ANY] * 4, out_specs=(ANY, ANY, VMEM, ANY, ANY, ANY, ANY),
        scratch_shapes=scratch + bufs + [dma((4, 3, 8)), dma((4, 3, 8)), dma((4, 18)), dma((4, 18)), dma((10,)), dma((9,)), dma((9,)), pltpu.SemaphoreType.REGULAR],
        compiler_params=params(collective_id=0, has_side_effects=True), name="layer")(tok, ups, small, index, mask, *shards)


def wide_body(tokens, first_gain, first_shift, qkv_weight, query_bias, value_bias, bias_table, bias_index, out_weight, out_bias, first_scale,
              second_gain, second_shift, up_weight, up_bias, down_weight, down_bias, second_scale, patch_mask, upstream):
    n = tokens.shape[0]

    def whole(v):
        return lax.all_gather(v, "fsdp", axis=0, tiled=True)

    vectors = (first_gain, first_shift, query_bias, value_bias, out_bias, first_scale, second_gain, second_shift, down_bias, second_scale)
    vec = jnp.pad(lax.all_gather(jnp.stack(vectors), "fsdp", axis=1, tiled=True).astype(F32), ((0, 6), (0, 0)))
    upb = whole(up_bias).astype(F32).reshape(1, FF)
    table = jnp.pad(whole(bias_table).T.astype(F32), ((0, 4), (0, 768 - RELS)))
    qkv, outw, upw, downw = whole(qkv_weight), whole(out_weight), whole(up_weight), whole(down_weight)
    index = pad_index(bias_index)
    mask = jnp.pad(patch_mask.astype(F32), ((0, 8 - n), (0, KP - SEQ)))
    norm_one, relative = front(tokens, vec, table, index)
    q, k, v, attend, context = attention(norm_one, qkv, vec, relative)
    layer_out, dout, dup, ddown, gctx, gres, small_mlp, small_up = mlp(tokens, context, outw, upw, downw, vec, upb, mask, upstream)
    tgrad, dqkv, small, tab = back(tokens, norm_one, qkv, vec, index, q, k, v, attend, gctx, gres)
    tab = tab.reshape(6, 16, 128)[:, :HEADS].transpose(1, 0, 2).reshape(HEADS, 768)[:, :RELS].T

    def summed(g):
        part = lax.psum_scatter(g.astype(BF), "fsdp", scatter_dimension=0, tiled=True)
        return lax.psum(part.astype(F32), "dp")

    rows = lax.psum(lax.psum_scatter(jnp.concatenate([small[2:4], small[0:2], small_mlp[::-1][2:]]), "fsdp", scatter_dimension=1, tiled=True), "dp")
    g1, s1, qb, vb, ob, sc1, s2, g2, db, sc2 = rows
    return (layer_out, tgrad, g1, s1, summed(dqkv), qb, vb, summed(tab), summed(dout), ob, sc1, g2, s2, summed(dup), summed(small_up.reshape(FF)), summed(ddown), db, sc2)


def body(wide, tokens, first_gain, first_shift, qkv_weight, query_bias, value_bias, bias_table, bias_index, out_weight, out_bias, first_scale,
         second_gain, second_shift, up_weight, up_bias, down_weight, down_bias, second_scale, patch_mask, upstream):
    if wide:
        return wide_body(tokens, first_gain, first_shift, qkv_weight, query_bias, value_bias, bias_table, bias_index, out_weight, out_bias, first_scale,
                         second_gain, second_shift, up_weight, up_bias, down_weight, down_bias, second_scale, patch_mask, upstream)
    n = tokens.shape[0]
    vectors = (first_gain, first_shift, query_bias, value_bias, out_bias, first_scale, second_gain, second_shift, down_bias, second_scale)
    small = stack_small(vectors, up_bias, bias_table)
    index = pad_index(bias_index)
    mask = jnp.pad(patch_mask.astype(F32), ((0, 8 - n), (0, KP - SEQ)))
    lo, tg, sm, rqkv, rout, rup, rdown = layer(tokens, upstream, small, index, mask, qkv_weight, out_weight, up_weight, down_weight)
    layer_out, tgrad = lo[:, :SEQ], tg[:, :SEQ]
    rows = [sm[i, :192] for i in range(10)]
    gub = sm[10:14, :192].reshape(768)
    gtab = sm[16:28, :183].T
    f = lambda t: t.astype(F32)
    g1, s1, qb, vb, ob, sc1, g2, s2, db, sc2 = rows
    return (layer_out, tgrad, g1, s1, f(rqkv), qb, vb, gtab, f(rout), ob, sc1, g2, s2, f(rup), gub, f(rdown), db, sc2)


def solution(mesh):
    vector, matrix, batch = P("fsdp"), P("fsdp", None), P(("dp", "fsdp"), None, None)
    in_specs = (batch, vector, vector, matrix, vector, vector, matrix, P(), matrix, vector, vector, vector, vector, matrix, vector, matrix, vector, vector,
                P(("dp", "fsdp"), None), batch)
    out_specs = (batch, batch, vector, vector, matrix, vector, vector, matrix, matrix, vector, vector, vector, vector, matrix, vector, matrix, vector, vector)
    wide = mesh.shape["dp"] != 8 or mesh.shape["fsdp"] != 4
    return jax.shard_map(functools.partial(body, wide), mesh=mesh, in_specs=in_specs, out_specs=out_specs, check_vma=False)
```

```python
import functools
import jax
import jax.numpy as jnp
from jax import lax
from jax.experimental import pallas as pl
from jax.experimental.pallas import tpu as pltpu
from jax.sharding import PartitionSpec as P

D = 768
HEADS = 12
HEAD_DIM = 64
FF = 3072
SEQ = 197
RELS = 732
SP = 208
KP = 256
HALF = SP * KP
EPS = 1e-06
BF = jnp.bfloat16
F32 = jnp.float32
VMEM = pl.BlockSpec(memory_space=pltpu.VMEM)
ANY = pl.BlockSpec(memory_space=pl.ANY)
LIMIT = 63 * 2**20


def dot(a, b):
    return lax.dot_general(a, b, (((1,), (0,)), ((), ())), preferred_element_type=F32)


def dot_nt(a, b):
    return lax.dot_general(a, b, (((1,), (1,)), ((), ())), preferred_element_type=F32)


def dot_tn(a, b):
    return lax.dot_general(a, b, (((0,), (0,)), ((), ())), preferred_element_type=F32)


def rowmean(v):
    return jnp.sum(v, axis=-1, keepdims=True) * (1.0 / D)


def colsum(v):
    return jnp.sum(v, axis=0, keepdims=True)


def xhat_of(v):
    centred = v - rowmean(v)
    rstd = lax.rsqrt(rowmean(centred * centred) + EPS)
    return centred * rstd, rstd


def pad_rows(v):
    return jnp.concatenate([v, jnp.zeros((SP - SEQ, v.shape[1]), v.dtype)], axis=0)


GAIN1, SHIFT1, QBIAS, VBIAS, OBIAS, SCALE1, GAIN2, SHIFT2, DBIAS, SCALE2 = range(10)


def front_kernel(tok, vec, table, index, norm_one, relative):
    images = tok.shape[0]
    gain, shift = vec[GAIN1 : GAIN1 + 1, :], vec[SHIFT1 : SHIFT1 + 1, :]
    for b in range(images):
        xhat, _ = xhat_of(pad_rows(tok[b].astype(F32)))
        norm_one[b] = (xhat * gain + shift).astype(BF)
    lookup(table, index, [relative.at[h] for h in range(HEADS)])


def lookup(table, index, relative):
    lanes = lax.broadcasted_iota(jnp.int32, (16, 128), 1)

    def rows(r, carry):
        at = pl.ds(pl.multiple_of(r * 16, 16), 16)
        for half in range(2):
            idx = index[at, half * 128 : half * 128 + 128]
            low = idx & 127
            high = idx >> 7
            for h in range(HEADS):
                out = jnp.zeros((16, 128), F32)
                for c in range(6):
                    part = jnp.broadcast_to(table[h : h + 1, c * 128 : c * 128 + 128], (16, 128))
                    got = jnp.take_along_axis(part, low, axis=1, mode="promise_in_bounds")
                    out = jnp.where(high == c, got, out)
                if half == 1:
                    out = jnp.where(lanes < SEQ - 128, out, -1e30)
                relative[h][at, half * 128 : half * 128 + 128] = out.astype(BF)
        return carry

    lax.fori_loop(0, SP // 16, rows, 0)


def lane_masks(rows):
    lane = lax.broadcasted_iota(jnp.int32, (rows, 128), 1)
    return lane < HEAD_DIM


def split_heads(v, first):
    zero = jnp.zeros_like(v)
    return jnp.where(first, v, zero), jnp.where(first, zero, v)


def project(norm_one, qkv, vec, q, k, v):
    images = norm_one.shape[0]
    k[:, SP:, :] = jnp.zeros((images, KP - SP, D), BF)
    v[:, SP:, :] = jnp.zeros((images, KP - SP, D), BF)

    def chunk(i, carry):
        at = pl.ds(pl.multiple_of(i * 256, 256), 256)
        rows = norm_one[...].reshape(images * SP, D)
        pq = dot(rows, qkv[:, at])
        q[:, :, at] = ((pq + vec[QBIAS : QBIAS + 1, at]) * 0.125).astype(BF).reshape(images, SP, 256)
        pk = dot(rows, qkv[:, pl.ds(pl.multiple_of(D + i * 256, 256), 256)])
        k[:, :SP, at] = pk.astype(BF).reshape(images, SP, 256)
        pv = dot(rows, qkv[:, pl.ds(pl.multiple_of(2 * D + i * 256, 256), 256)])
        v[:, :SP, at] = (pv + vec[VBIAS : VBIAS + 1, at]).astype(BF).reshape(images, SP, 256)
        return carry

    lax.fori_loop(0, D // 256, chunk, 0)


def attend_pair(b, hp, at, q, k, v, relative, attend, context):
    first = lane_masks(KP)
    q2 = q[b, :, at]
    ks = split_heads(k[b, :, at], first)
    vs = split_heads(v[b, :, at], first)
    probs = []
    for e in range(2):
        h = 2 * hp + e
        s = dot_nt(q2, ks[e]) + relative[h][...].astype(F32)
        s = jnp.exp(s - jnp.max(s, axis=-1, keepdims=True))
        p = (s * (1.0 / jnp.sum(s, axis=-1, keepdims=True))).astype(BF)
        attend[b, h] = p
        probs.append(p)
    context[b, :, at] = (dot(probs[0], vs[0]) + dot(probs[1], vs[1])).astype(BF)


def attention_kernel(norm_one, qkv, vec, relative, q, k, v, attend, context):
    images = norm_one.shape[0]
    relative = [relative.at[h] for h in range(HEADS)]
    project(norm_one, qkv, vec, q, k, v)

    def image(b, carry):
        for hp in range(HEADS // 2):
            attend_pair(b, hp, slice(hp * 128, hp * 128 + 128), q, k, v, relative, attend, context)
        return carry

    lax.fori_loop(0, images, image, 0)


def gelu_both(v):
    cdf = 0.5 * (1.0 + lax.erf(v * 0.7071067811865476))
    pdf = jnp.exp(v * v * -0.5) * 0.3989422804014327
    return v * cdf, cdf + v * pdf


def mlp_kernel(tok, ctx, out_hbm, up_hbm, down_hbm, vec, upb, mask, ups,
               layer_out, dout, dup, ddown, gctx, gres, small, small_up,
               outw, upw, downw, hid, att, n2, act, slope, acc, gd, gy_s, sems):
    images = tok.shape[0]
    R = images * SP
    loads = [pltpu.make_async_copy(s, d, sems.at[i]) for i, (s, d) in enumerate(
        ((out_hbm, outw), (up_hbm, upw), (down_hbm, downw)))]
    for l in loads:
        l.start()
    obias, scale1 = vec[OBIAS : OBIAS + 1, :], vec[SCALE1 : SCALE1 + 1, :]
    gain2, shift2 = vec[GAIN2 : GAIN2 + 1, :], vec[SHIFT2 : SHIFT2 + 1, :]
    dbias, scale2 = vec[DBIAS : DBIAS + 1, :], vec[SCALE2 : SCALE2 + 1, :]
    maskt = jnp.transpose(mask[...], (1, 0))
    loads[0].wait()
    for b in range(images):
        attn = dot(ctx[b], outw[...]) + obias
        att[b] = attn
        h = pad_rows(tok[b].astype(F32)) + scale1 * attn
        hid[b] = h
        xhat, _ = xhat_of(h)
        n2[b] = (xhat * gain2 + shift2).astype(BF)
    loads[1].wait()
    loads[2].wait()
    acc[...] = jnp.zeros_like(acc)
    W = 256

    def forward(f, carry):
        at = pl.ds(pl.multiple_of(f * W, W), W)
        for b in range(images):
            u = dot(n2[b], upw[:, at]) + upb[:, at]
            g, s = gelu_both(u)
            g = g.astype(BF)
            act[b, :, at] = g
            slope[b, :, at] = s.astype(BF)
            acc[b] += dot(g, downw[at, :])
        return carry

    lax.fori_loop(0, FF // W, forward, 0)
    sums = [jnp.zeros((1, D), F32) for _ in range(6)]
    for b in range(images):
        down = acc[b] + dbias
        layer_out[b] = (hid[b] + scale2 * down).astype(BF)[:SEQ]
        gy = pad_rows(ups[b].astype(F32)) * maskt[:SP, b : b + 1]
        gy_s[b] = gy.astype(BF)
        sums[0] += colsum(gy * down)
        full = gy * scale2
        sums[1] += colsum(full)
        gd[b] = full.astype(BF)
    acc[...] = jnp.zeros_like(acc)

    def backward(f, carry):
        at = pl.ds(pl.multiple_of(f * W, W), W)
        total = jnp.zeros((1, W), F32)
        lows = []
        for b in range(images):
            gg = dot_nt(gd[b], downw[at, :]) * slope[b, :, at].astype(F32)
            total += colsum(gg)
            low = gg.astype(BF)
            lows.append(low)
            acc[b] += dot_nt(low, upw[:, at])
        small_up[:, at] = total
        low = jnp.concatenate(lows, axis=0)
        dup[:, at] = dot_tn(n2[...].reshape(R, D), low).astype(BF)
        ddown[at, :] = dot_tn(act[:, :, at].reshape(R, W), gd[...].reshape(R, D)).astype(BF)
        return carry

    lax.fori_loop(0, FF // W, backward, 0)
    for b in range(images):
        xhat, rstd = xhat_of(hid[b])
        g = acc[b]
        sums[2] += colsum(g * xhat)
        sums[3] += colsum(g)
        gg = g * gain2
        gh = (gg - rowmean(gg) - xhat * rowmean(gg * xhat)) * rstd
        res = gy_s[b].astype(F32) + gh
        gres[b] = res
        sums[4] += colsum(res * att[b])
        full = res * scale1
        sums[5] += colsum(full)
        n2[b] = full.astype(BF)
    dout[...] = dot_tn(ctx[...].reshape(R, D), n2[...].reshape(R, D)).astype(BF)
    for b in range(images):
        gctx[b] = dot_nt(n2[b], outw[...]).astype(BF)
    small[...] = jnp.concatenate(sums + [jnp.zeros((2, D), F32)], axis=0)


def attend_back(b, hp, at, q, k, v, attend, gctx, gtab, gq, gk, gv, qsum, vsum):
    first = lane_masks(KP)
    firsts = first[:SP]
    v2 = split_heads(v[b, :, at], first)
    k2 = split_heads(k[b, :, at], first)
    q2 = split_heads(q[b, :, at], firsts)
    g2 = gctx[b, :, at]
    gs2 = split_heads(g2, firsts)
    dq = jnp.zeros((SP, 128), F32)
    dk = jnp.zeros((KP, 128), F32)
    dv = jnp.zeros((KP, 128), F32)
    for e in range(2):
        h = 2 * hp + e
        a = attend[b, h]
        af = a.astype(F32)
        ga = dot_nt(g2, v2[e])
        w = af * ga
        inner = jnp.sum(w, axis=-1, keepdims=True)
        gs = w - af * inner
        gtab[h][...] += gs
        low = gs.astype(BF)
        dq += dot(low, k2[e])
        dk += dot_tn(low, q2[e])
        dv += dot_tn(a, gs2[e])
    dq = dq * 0.125
    qsum[:, at] += colsum(dq)
    vsum[:, at] += colsum(dv)
    gq[b, :, at] = dq.astype(BF)
    gk[b, :, at] = dk[:SP].astype(BF)
    gv[b, :, at] = dv[:SP].astype(BF)


def table_rows(gtab, index, total, start, stop):
    ids = lax.broadcasted_iota(jnp.int32, (128, KP), 0).astype(F32).astype(BF)
    one, zero = jnp.ones((128, KP), BF), jnp.zeros((128, KP), BF)
    none = jnp.zeros((16, KP), BF)

    def row(i, acc):
        idx = index[pl.ds(i, 1), :]
        low = (idx & 127).astype(F32).astype(BF)
        high = jnp.broadcast_to((idx >> 7).astype(F32).astype(BF), (16, KP))
        hot = jnp.where(ids == low, one, zero)
        g = jnp.concatenate([t[pl.ds(i, 1), :] for t in gtab] + [jnp.zeros((4, KP), F32)], axis=0)
        g1 = g.astype(BF)
        g2 = (g - g1.astype(F32)).astype(BF)
        parts = [jnp.where(high == c, src, none) for src in (g1, g2) for c in range(6)]
        return acc + dot_nt(jnp.concatenate(parts, axis=0), hot)

    return lax.fori_loop(start, stop, row, total)


def table_back(gtab, index, out):
    total = table_rows(gtab, index, jnp.zeros((192, 128), F32), 0, SEQ)
    out[...] = total[:96] + total[96:]


def back_kernel(tok, norm_one, qkv_hbm, vec, index, q, k, v, attend, gctx, gres,
                tgrad, dqkv, small, tab, gtab, gqkv, qkv, sem):
    images = tok.shape[0]
    R = images * SP
    load = pltpu.make_async_copy(qkv_hbm, qkv, sem)
    load.start()
    gtab[...] = jnp.zeros_like(gtab)
    gtab = [gtab.at[h] for h in range(HEADS)]
    small[...] = jnp.zeros_like(small)
    gq, gk, gv = (gqkv.at[:, :, i * D : (i + 1) * D] for i in range(3))
    qsum, vsum = small.at[0:1, :], small.at[1:2, :]

    for hp in range(HEADS // 2):

        def one(b, carry, hp=hp):
            attend_back(b, hp, slice(hp * 128, hp * 128 + 128), q, k, v, attend, gctx, gtab, gq, gk, gv, qsum, vsum)
            return carry

        lax.fori_loop(0, images, one, 0)
    table_back(gtab, index, tab)

    def chunk(i, carry):
        at = pl.ds(pl.multiple_of(i * 256, 256), 256)
        dqkv[:, at] = dot_tn(norm_one[...].reshape(R, D), gqkv[:, :, at].reshape(R, 256)).astype(BF)
        return carry

    lax.fori_loop(0, 3 * D // 256, chunk, 0)
    load.wait()
    gain = vec[GAIN1 : GAIN1 + 1, :]
    for b in range(images):
        xhat, rstd = xhat_of(pad_rows(tok[b].astype(F32)))
        g = dot_nt(gqkv[b], qkv[...])
        small[2:3, :] += colsum(g * xhat)
        small[3:4, :] += colsum(g)
        gg = g * gain
        gi = (gg - rowmean(gg) - xhat * rowmean(gg * xhat)) * rstd
        tgrad[b] = (gres[b] + gi)[:SEQ]


def params(**kw):
    return pltpu.CompilerParams(vmem_limit_bytes=LIMIT, **kw)


def S(shape, dtype):
    return jax.ShapeDtypeStruct(shape, dtype)


def front(tok, vec, table, index):
    n = tok.shape[0]
    return pl.pallas_call(front_kernel, out_shape=(S((n, SP, D), BF), S((HEADS, SP, KP), BF)),
                          in_specs=[VMEM] * 4, out_specs=(VMEM, VMEM), compiler_params=params(), name="front")(tok, vec, table, index)


def attention(norm_one, qkv, vec, relative):
    n = norm_one.shape[0]
    return pl.pallas_call(attention_kernel,
                          out_shape=(S((n, SP, D), BF), S((n, KP, D), BF), S((n, KP, D), BF), S((n, HEADS, SP, KP), BF), S((n, SP, D), BF)),
                          in_specs=[VMEM] * 4, out_specs=(VMEM,) * 5, compiler_params=params(), name="attention")(norm_one, qkv, vec, relative)


def mlp(tok, ctx, outw, upw, downw, vec, upb, mask, ups):
    n = tok.shape[0]
    return pl.pallas_call(
        mlp_kernel,
        out_shape=(S((n, SEQ, D), BF), S((D, D), BF), S((D, FF), BF), S((FF, D), BF), S((n, SP, D), BF), S((n, SP, D), F32), S((8, D), F32), S((1, FF), F32)),
        in_specs=[VMEM, VMEM, ANY, ANY, ANY, VMEM, VMEM, VMEM, VMEM], out_specs=(VMEM,) * 8,
        scratch_shapes=[pltpu.VMEM((D, D), BF), pltpu.VMEM((D, FF), BF), pltpu.VMEM((FF, D), BF),
                        pltpu.VMEM((n, SP, D), F32), pltpu.VMEM((n, SP, D), F32), pltpu.VMEM((n, SP, D), BF),
                        pltpu.VMEM((n, SP, FF), BF), pltpu.VMEM((n, SP, FF), BF), pltpu.VMEM((n, SP, D), F32),
                        pltpu.VMEM((n, SP, D), BF), pltpu.VMEM((n, SP, D), BF), pltpu.SemaphoreType.DMA((3,))],
        compiler_params=params(), name="mlp")(tok, ctx, outw, upw, downw, vec, upb, mask, ups)


def back(tok, norm_one, qkv, vec, index, q, k, v, attend, gctx, gres):
    n = tok.shape[0]
    return pl.pallas_call(
        back_kernel,
        out_shape=(S((n, SEQ, D), F32), S((D, 3 * D), BF), S((8, D), F32), S((96, 128), F32)),
        in_specs=[VMEM, VMEM, ANY] + [VMEM] * 8, out_specs=(VMEM,) * 4,
        scratch_shapes=[pltpu.VMEM((16, SP, KP), F32), pltpu.VMEM((n, SP, 3 * D), BF), pltpu.VMEM((D, 3 * D), BF), pltpu.SemaphoreType.DMA(())],
        compiler_params=params(), name="back")(tok, norm_one, qkv, vec, index, q, k, v, attend, gctx, gres)


def pad_index(bias_index):
    return jnp.pad(bias_index, ((0, SP - SEQ), (0, KP - SEQ)))
MESH = pl.DeviceIdType.MESH


class Place:
    def __init__(self):
        dp, z = lax.axis_index("dp"), lax.axis_index("fsdp")
        y, x, c = dp // 4, (dp // 2) % 2, dp % 2
        xn, yn = dp + 2 - 4 * x, dp + 4 - 8 * y
        q = dp // 2
        qx, qy = q + 1 - 2 * x, q + 2 - 4 * y
        self.dp, self.z, self.c, self.q = dp, z, c, q
        self.near = (xn * (1 - c) + yn * c, z)
        self.far = (yn * (1 - c) + xn * c, z)
        self.x, self.y = (xn, z), (yn, z)
        self.twin = (dp + 1 - 2 * c, z)
        self.q_near = qx * (1 - c) + qy * c
        self.q_far = qy * (1 - c) + qx * c
        self.q_both = 3 - q

    def up(self, d):
        return (self.dp, (self.z + d) % 4)

    def barrier(self):
        sem = pltpu.get_barrier_semaphore()
        peers = [self.near, self.far, self.twin] + [self.up(d) for d in (1, 2, 3)]
        for peer in peers:
            pl.semaphore_signal(sem, inc=1, device_id=peer, device_id_type=MESH)
        pl.semaphore_wait(sem, len(peers))


def aligned(i, size):
    return pl.ds(pl.multiple_of(i * size, size), size)


class Gather:
    def __init__(self, place, shard, full, send, recv, local):
        self.p, self.shard, self.full, self.send, self.recv, self.local = place, shard, full, send, recv, local
        self.rows, self.cols = full.shape[1] // 4, full.shape[2] // 2

    def region(self, zb, q, c):
        return self.full.at[zb, aligned(q, self.rows), aligned(c, self.cols)]

    def copy(self, d, slot, src, dst, peer):
        return pltpu.make_async_remote_copy(src_ref=src, dst_ref=dst, send_sem=self.send.at[d - 1, slot], recv_sem=self.recv.at[d - 1, slot],
                                            device_id=peer, device_id_type=MESH)

    def over_z(self, d):
        p = self.p
        if self.shard is None:
            src = self.region(p.z, p.q, p.c)
        else:
            src = self.shard.at[aligned(p.q, self.rows), aligned(p.c, self.cols)]
        return self.copy(d, 0, src, self.region(p.z, p.q, p.c), p.up(d))

    def passed(self, d, slot, q, peer):
        p = self.p
        r = self.region((p.z + 4 - d) % 4, q, p.c)
        return self.copy(d, slot, r, r, peer)

    def own(self):
        return pltpu.make_async_copy(self.shard, self.full.at[self.p.z], self.local)

    def begin(self):
        for d in (1, 2, 3):
            self.over_z(d).start()
        if self.shard is not None:
            self.own().start()

    def part(self, d, i):
        p = self.p
        slot, q, peer = ((1, p.q, p.near), (2, p.q, p.far), (4, p.q, p.twin), (3, p.q_near, p.far), (5, p.q_near, p.twin),
                         (6, p.q_far, p.twin), (7, p.q_both, p.twin))[i]
        return self.passed(d, slot, q, peer)

    def spread(self, d):
        self.over_z(d).wait_recv()
        for i in (0, 1, 2):
            self.part(d, i).start()

    def relay(self, d):
        self.part(d, 0).wait_recv()
        for i in (3, 4):
            self.part(d, i).start()

    def close(self, d):
        self.part(d, 1).wait_recv()
        self.part(d, 5).start()
        self.part(d, 3).wait_recv()
        self.part(d, 6).start()

    def finish(self):
        if self.shard is not None:
            self.own().wait()
        for d in (1, 2, 3):
            for i in (2, 4, 5, 6):
                self.part(d, i).wait_recv()

    def drain(self):
        for d in (1, 2, 3):
            self.over_z(d).wait_send()
            for i in range(7):
                self.part(d, i).wait_send()

    def steps(self):
        return [lambda d=d: self.spread(d) for d in (1, 2, 3)] + [lambda d=d: self.relay(d) for d in (1, 2, 3)] + [
            lambda d=d: self.close(d) for d in (1, 2, 3)] + [self.finish]


class Reduce:
    def __init__(self, place, grad, got, half, quarter, pieces, out, send, recv, local):
        self.p, self.grad, self.got, self.half, self.quarter, self.pieces, self.out = place, grad, got, half, quarter, pieces, out
        self.send, self.recv, self.local = send, recv, local
        self.rows, self.cols = grad.shape[1] // 4, grad.shape[2] // 2

    def copy(self, slot, src, dst, peer):
        return pltpu.make_async_remote_copy(src_ref=src, dst_ref=dst, send_sem=self.send.at[slot], recv_sem=self.recv.at[slot], device_id=peer, device_id_type=MESH)

    def twin(self, i):
        q = self.quarters()[i]
        return self.copy(14 + i, self.grad.at[:, aligned(q, self.rows), aligned(1 - self.p.c, self.cols)], self.got(q), self.p.twin)

    def quarters(self):
        p = self.p
        return (p.q_far, p.q_both, p.q, p.q_near)

    def mine(self, q):
        return self.grad.at[:, aligned(q, self.rows), aligned(self.p.c, self.cols)]

    def near(self, i):
        q = (self.p.q_near, self.p.q_both)[i]
        return self.copy(1 + i, self.mine(q), self.half.at[i], self.p.near)

    def far(self):
        return self.copy(3, self.half.at[1], self.quarter, self.p.far)

    def over_z(self, d):
        return self.copy(3 + d, self.quarter.at[(self.p.z + d) % 4], self.pieces.at[d - 1], self.p.up(d))

    def region(self, q):
        return self.out.at[aligned(q, self.rows), aligned(self.p.c, self.cols)]

    def passed(self, i):
        p = self.p
        q, peer = ((p.q, p.near), (p.q, p.far), (p.q, p.twin), (p.q_near, p.far), (p.q_near, p.twin), (p.q_far, p.twin), (p.q_both, p.twin))[i]
        src = self.quarter.at[p.z] if i < 3 else self.region(q)
        return self.copy(7 + i, src, self.region(q), peer)

    def own(self):
        return pltpu.make_async_copy(self.quarter.at[self.p.z], self.region(self.p.q), self.local)

    def begin(self):
        for i in range(4):
            self.twin(i).start()

    def add(self, dst, src):
        def one(i, carry):
            dst[i] = (dst[i].astype(F32) + src[i].astype(F32)).astype(BF)
            return carry

        lax.fori_loop(0, 4, one, 0)

    def fold(self, q):
        self.add(self.mine(q), self.got(q))

    def first_a(self):
        self.twin(0).wait_recv()
        self.fold(self.p.q_near)
        self.near(0).start()

    def first_b(self):
        self.twin(1).wait_recv()
        self.fold(self.p.q_both)
        self.near(1).start()

    def first_c(self):
        self.twin(2).wait_recv()
        self.fold(self.p.q)
        self.twin(3).wait_recv()
        self.fold(self.p.q_far)

    def second(self):
        self.near(1).wait_recv()
        self.add(self.half.at[1], self.mine(self.p.q_far))
        self.far().start()
        self.near(0).wait_recv()
        self.add(self.half.at[0], self.mine(self.p.q))

    def third(self):
        self.far().wait_recv()
        self.add(self.quarter, self.half.at[0])
        for d in (1, 2, 3):
            self.over_z(d).start()

    def fourth(self):
        for d in (1, 2, 3):
            self.over_z(d).wait_recv()
        total = self.quarter[self.p.z].astype(F32)
        for d in (1, 2, 3):
            total += self.pieces[d - 1].astype(F32)
        self.quarter[self.p.z] = total.astype(BF)
        for i in (0, 1, 2):
            self.passed(i).start()
        self.own().start()

    def fifth(self):
        self.passed(0).wait_recv()
        self.passed(3).start()
        self.passed(4).start()

    def sixth(self):
        self.passed(1).wait_recv()
        self.passed(5).start()
        self.passed(3).wait_recv()
        self.passed(6).start()

    def finish(self):
        for i in (2, 4, 5, 6):
            self.passed(i).wait_recv()
        self.own().wait()

    def drain(self):
        for i in range(4):
            self.twin(i).wait_send()
        self.near(0).wait_send()
        self.near(1).wait_send()
        self.far().wait_send()
        for d in (1, 2, 3):
            self.over_z(d).wait_send()
        for i in range(7):
            self.passed(i).wait_send()

    def steps(self):
        return [self.first_a, self.first_b, self.first_c, self.second, self.third, self.fourth, self.fifth, self.sixth]
def unstack_small(block, vec, upb, table):
    vec[...] = jnp.zeros_like(vec)
    table[...] = jnp.zeros_like(table)
    for z in range(4):
        part = block[z].astype(F32)
        vec[:, z * 192 : z * 192 + 192] = part[:16, :192]
        upb[:, z * 768 : z * 768 + 768] = part[10:11, :]
        table[:, z * 183 : z * 183 + 183] = part[16:32, :183]


def head_view(ref, h):
    return ref.at[h // 3, :, (h % 3) * 256 : (h % 3) * 256 + 256]


def layer_kernel(tok, ups, idx_in, mask_in, table_in, ub_in, v0, v1, v2, v3, v4, v5, v6, v7, v8, v9, qkv_s, out_s, up_s, down_s,
                 lo_hbm, tg_hbm, sm_out, rqkv, rout, rup, rdown,
                 qw0, qw1, qw2, outw, upw, downw, A, B, hid, att, acc, n1, q, k, v, ctx, n2, gd, lo, attend, vec, upb, table, block, small_in, small_f, index, mask,
                 sums, upsum, tab, sm, sm_got, sm_piece,
                 half0, quart0, piece0, half1, quart1, piece1, got2, half2, quart2, piece2, got3, half3, quart3, piece3,
                 got4, half4, quart4, piece4, got5, half5, quart5, piece5,
                 gsend, grecv, rsend, rrecv, local, ssend, srecv, qsem, free):
    p = Place()
    images = tok.shape[0]
    R = images * SP
    qw = (qw0, qw1, qw2)
    groups = [[pltpu.make_async_copy(qkv_s.at[:, j * D + g * 256 : j * D + g * 256 + 256], qw[g].at[p.z, :, j * 256 : j * 256 + 256], qsem.at[g, j])
               for j in range(3)] for g in range(3)]
    for group in groups:
        for c in group:
            c.start()
    small_f[...] = jnp.zeros_like(small_f)
    for i, vector in enumerate((v0, v1, v2, v3, v4, v5, v6, v7, v8, v9)):
        small_f[i, :192] = vector[...].astype(F32)
    small_f[10, :] = ub_in[...].astype(F32)
    small_f[16:28, :183] = table_in[...].astype(F32)
    small_in[...] = small_f[...].astype(BF)
    p.barrier()

    units = [(None, qw[g]) for g in range(3)] + [(out_s, outw), (up_s, upw), (down_s, downw)]
    gathers = [Gather(p, s, f, gsend.at[i], grecv.at[i], local.at[i]) for i, (s, f) in enumerate(units)]
    block[p.z] = small_in[...]
    smalls = [pltpu.make_async_remote_copy(src_ref=small_in, dst_ref=block.at[p.z], send_sem=ssend.at[d - 1], recv_sem=srecv.at[d - 1], device_id=p.up(d), device_id_type=MESH) for d in (1, 2, 3)]
    for s in smalls:
        s.start()
    for g in range(4):
        if g < 3:
            for c in groups[g]:
                c.wait()
        gathers[g].begin()
    index[...] = jnp.zeros_like(index)
    index[:SEQ, :SEQ] = idx_in[...]
    mask[...] = jnp.zeros_like(mask)
    mask[:images, :SEQ] = mask_in[...].astype(F32)
    for s in smalls:
        s.wait_recv()
    unstack_small(block, vec, upb, table)
    row = lambda i: vec[i : i + 1, :]
    todo = []

    def plan(steps, times):
        todo.extend(zip(times, steps))
        todo.sort(key=lambda e: e[0])

    def advance(now):
        while todo and todo[0][0] <= now:
            todo.pop(0)[1]()

    for g, (spread, relay, close, finish) in zip(gathers, GATHER_PLAN):
        plan(g.steps(), (spread, spread + 0.5, spread + 1, relay, relay + 0.5, relay + 1, close, close + 0.5, close + 1, finish))
    plan([gathers[4].begin, gathers[5].begin], BEGIN_PLAN)
    for b in range(images):
        xhat, _ = xhat_of(pad_rows(tok[b].astype(F32)))
        n1[b] = (xhat * row(GAIN1) + row(SHIFT1)).astype(BF)
        advance(5 + b)
    relative = [head_view(gd, h) for h in range(HEADS)]
    lookup(table, index, relative)

    k[:, SP:, :] = jnp.zeros((images, KP - SP, D), BF)
    v[:, SP:, :] = jnp.zeros((images, KP - SP, D), BF)
    for g in range(3):
        at = slice(g * 256, g * 256 + 256)
        advance(GATHER_PLAN[g][3])

        def weight(j, g=g):
            return qw[g][:, :, j * 256 : j * 256 + 256].reshape(D, 256)

        rows = n1[...].reshape(R, D)
        q[:, :, at] = ((dot(rows, weight(0)) + vec[QBIAS : QBIAS + 1, at]) * 0.125).astype(BF).reshape(images, SP, 256)
        k[:, :SP, at] = dot(rows, weight(1)).astype(BF).reshape(images, SP, 256)
        v[:, :SP, at] = (dot(rows, weight(2)) + vec[VBIAS : VBIAS + 1, at]).astype(BF).reshape(images, SP, 256)
        advance(17 + 8 * g)
        for hp in (2 * g, 2 * g + 1):

            def one(b, carry, hp=hp):
                attend_pair(b, hp, slice(hp * 128, hp * 128 + 128), q, k, v, relative, attend, ctx)
                return carry

            lax.fori_loop(0, images, one, 0)
            advance(20 + 8 * g + 3 * (hp - 2 * g))

    advance(GATHER_PLAN[3][3])
    for b in range(images):
        attn = dot(ctx[b], outw[...].reshape(D, D)) + row(OBIAS)
        att[b] = attn
        h = pad_rows(tok[b].astype(F32)) + row(SCALE1) * attn
        hid[b] = h
        xhat, _ = xhat_of(h)
        n2[b] = (xhat * row(GAIN2) + row(SHIFT2)).astype(BF)
    advance(GATHER_PLAN[4][3])
    W = 256

    def expand(f, carry):
        at = aligned(f, W)
        for b in range(images):
            u = dot(n2[b], upw[:, :, at].reshape(D, W)) + upb[:, at]
            g, s = gelu_both(u)
            A[b, :, at] = g.astype(BF)
            B[b, :, at] = s.astype(BF)
        return carry

    for part in range(4):
        lax.fori_loop(part * 3, part * 3 + 3, expand, 0)
        advance(46 + 3 * part)
    advance(1000)
    for i in range(D // 256):
        at = slice(i * 256, i * 256 + 256)
        acc[:, :, at] = dot(A[...].reshape(R, FF), downw[:, :, at].reshape(FF, 256)).reshape(images, SP, 256)
    maskt = jnp.transpose(mask[...], (1, 0))
    sums[...] = jnp.zeros_like(sums)

    def add_sum(i, value):
        sums[i : i + 1, :] += colsum(value)

    def grad_y(b):
        return pad_rows(ups[b].astype(F32)) * maskt[:SP, b : b + 1]

    for b in range(images):
        down = acc[b] + row(DBIAS)
        lo[b] = (hid[b] + row(SCALE2) * down).astype(BF)
        gy = grad_y(b)
        add_sum(SCALE2, gy * down)
        full = gy * row(SCALE2)
        add_sum(DBIAS, full)
        gd[b] = full.astype(BF)
    lo_copy = pltpu.make_async_copy(lo, lo_hbm, local.at[12])
    lo_copy.start()

    for g in gathers:
        g.drain()

    def contract(f, carry):
        at = aligned(f, W)
        z, r = f // 3, f % 3
        rows = aligned(r, W)
        total = jnp.zeros((1, W), F32)
        for b in range(images):
            gg = dot_nt(gd[b], downw[z, rows, :]) * B[b, :, at].astype(F32)
            total += colsum(gg)
            B[b, :, at] = gg.astype(BF)
        upsum[:, at] = total
        downw[z, rows, :] = dot_tn(A[:, :, at].reshape(R, W), gd[...].reshape(R, D)).astype(BF)
        return carry

    lax.fori_loop(0, FF // W, contract, 0)
    pl.semaphore_signal(free, inc=1, device_id=p.twin, device_id_type=MESH)

    def got_down(q):
        return A.at[:, :192, pl.ds(pl.multiple_of(1536 + q * 384, 128), 384)]

    def got_up(q):
        return A.at[:, aligned(q, 48), :1536]

    def got_of(ref, rows):
        return lambda q: ref.at[:, aligned(q, rows), :]

    parts = ((downw, got_down, half0, quart0, piece0, rdown), (upw, got_up, half1, quart1, piece1, rup),
             (outw, got_of(got2, 48), half2, quart2, piece2, rout), (qw0, got_of(got3, 48), half3, quart3, piece3, rqkv.at[0]),
             (qw1, got_of(got4, 48), half4, quart4, piece4, rqkv.at[1]), (qw2, got_of(got5, 48), half5, quart5, piece5, rqkv.at[2]))
    red = [Reduce(p, *part, rsend.at[i], rrecv.at[i], local.at[6 + i]) for i, part in enumerate(parts)]

    def launch(i):
        red[i].begin()
        plan(red[i].steps(), REDUCE_PLAN[i])

    pl.semaphore_wait(free, 1)
    launch(0)
    for i in range(4):
        acc[:, :, i * 192 : i * 192 + 192] = dot_nt(B[...].reshape(R, FF), upw[i]).reshape(images, SP, 192)
        advance(13.5 + 1.5 * i)

    def widen(f, carry):
        at = aligned(f, W)
        upw[:, :, at] = dot_tn(n2[...].reshape(R, D), B[:, :, at].reshape(R, W)).astype(BF).reshape(4, D // 4, W)
        return carry

    for i in range(4):
        lax.fori_loop(3 * i, 3 * i + 3, widen, 0)
        advance(20 + 2 * i)
    launch(1)
    for b in range(images):
        xhat, rstd = xhat_of(hid[b])
        g = acc[b]
        add_sum(GAIN2, g * xhat)
        add_sum(SHIFT2, g)
        gg = g * row(GAIN2)
        res = grad_y(b) + (gg - rowmean(gg) - xhat * rowmean(gg * xhat)) * rstd
        hid[b] = res
        add_sum(SCALE1, res * att[b])
        full = res * row(SCALE1)
        add_sum(OBIAS, full)
        n2[b] = full.astype(BF)
        advance(27 + b)
    gctx = B.at[:, :, 3 * D :]
    for b in range(images):
        gctx[b] = dot_nt(n2[b], outw[...].reshape(D, D)).astype(BF)
    for i in range(3):
        at = slice(i * 256, i * 256 + 256)
        outw[:, :, at] = dot_tn(ctx[...].reshape(R, D), n2[:, :, at].reshape(R, 256)).astype(BF).reshape(4, D // 4, 256)
    launch(2)
    advance(33)

    acc[...] = jnp.zeros_like(acc)
    gtab = [head_view(acc, h) for h in range(HEADS)]
    gq, gk, gv = (B.at[:, :, i * D : (i + 1) * D] for i in range(3))
    qsum, vsum = sums.at[QBIAS : QBIAS + 1, :], sums.at[VBIAS : VBIAS + 1, :]
    for g in range(3):
        now = 33 + 11 * g
        for hp in (2 * g, 2 * g + 1):
            for part in range(2):

                def one(i, carry, hp=hp, part=part):
                    attend_back(part * (images // 2) + i, hp, slice(hp * 128, hp * 128 + 128), q, k, v, attend, gctx, gtab, gq, gk, gv, qsum, vsum)
                    return carry

                lax.fori_loop(0, images // 2, one, 0)
                now += 2
                advance(now)
        grads = [B.at[:, :, j * D + g * 256 : j * D + g * 256 + 256] for j in range(3)]
        for b in range(images):
            term = sum(dot_nt(grads[j][b], qw[g][:, :, j * 256 : j * 256 + 256].reshape(D, 256)) for j in range(3))
            att[b] = term if g == 0 else att[b] + term
        for j in range(3):
            qw[g][:, :, j * 256 : j * 256 + 256] = dot_tn(n1[...].reshape(R, D), grads[j][...].reshape(R, 256)).astype(BF).reshape(4, D // 4, 256)
        launch(3 + g)
        advance(now + 3)
    for b in range(images):
        xhat, rstd = xhat_of(pad_rows(tok[b].astype(F32)))
        g = att[b]
        add_sum(GAIN1, g * xhat)
        add_sum(SHIFT1, g)
        gg = g * row(GAIN1)
        att[b] = hid[b] + (gg - rowmean(gg) - xhat * rowmean(gg * xhat)) * rstd
        advance(67 + b)
    tg_copy = pltpu.make_async_copy(att, tg_hbm, local.at[13])
    tg_copy.start()
    total = jnp.zeros((192, 128), F32)
    for i in range(7):
        total = table_rows(gtab, index, total, 29 * i, min(29 * i + 29, SEQ))
        advance(71 + 2 * (i + 1))
    tab[...] = total[:96] + total[96:]
    sm[...] = jnp.zeros_like(sm)
    flat = jnp.concatenate([tab[c * 16 : c * 16 + 16, :] for c in range(6)], axis=1)
    for z in range(4):
        sm[z, 0:16, 0:192] = sums[:, z * 192 : z * 192 + 192]
        for i in range(4):
            sm[z, 10 + i : 11 + i, 0:192] = upsum[:, z * 768 + i * 192 : z * 768 + i * 192 + 192]
        sm[z, 16:32, 0:183] = flat[:, z * 183 : z * 183 + 183]

    def exchange(i, peer):
        return pltpu.make_async_remote_copy(src_ref=sm.at[pl.ds(4 * i, 4)], dst_ref=sm_got.at[i], send_sem=ssend.at[3 + i], recv_sem=srecv.at[3 + i], device_id=peer, device_id_type=MESH)

    swaps = [exchange(i, peer) for i, peer in enumerate((p.twin, p.x, p.y))]
    for i in range(3):
        swaps[i].start()
        advance(85 + i)
        swaps[i].wait_recv()
        sm[4 * i + 4 : 4 * i + 8] = sm[4 * i : 4 * i + 4] + sm_got[i]
    last = [pltpu.make_async_remote_copy(src_ref=sm.at[12 + (p.z + d) % 4], dst_ref=sm_piece.at[d - 1], send_sem=ssend.at[5 + d], recv_sem=srecv.at[5 + d], device_id=p.up(d), device_id_type=MESH) for d in (1, 2, 3)]
    for s in last:
        s.start()
    advance(88)
    for s in last:
        s.wait_recv()
    sm_out[...] = sm[12 + p.z] + sm_piece[0] + sm_piece[1] + sm_piece[2]
    advance(1000)
    for r in red:
        r.finish()
    lo_copy.wait()
    tg_copy.wait()
    for s in smalls + swaps + last:
        s.wait_send()
    for r in red:
        r.drain()


GATHER_PLAN = ((5, 8, 10, 13), (8.2, 11, 13.2, 16), (11.2, 14, 17, 20), (14.2, 18, 20.2, 23), (24, 30, 35, 38), (36, 44, 49, 52))
BEGIN_PLAN = (8, 20)
REDUCE_PLAN = ((15, 17, 19, 30, 37, 50, 53, 56), (28, 30, 32, 45, 52, 65, 68, 71), (35, 35.5, 36, 47, 50.5, 56, 58, 61),
               (46, 47, 48, 52.5, 56.5, 62, 65, 68), (57, 58, 59, 63, 66, 71, 74, 77), (68, 69, 70, 74, 77, 82, 85, 88))


def layer(tok, ups, index, mask, table, up_bias, vectors, qkv_s, out_s, up_s, down_s):
    n = tok.shape[0]
    shards = (qkv_s, out_s, up_s, down_s)

    def vm(shape, dtype=BF):
        return pltpu.VMEM(shape, dtype)

    row3, bufs = (n, SP, D), []
    for i, s in enumerate((down_s, up_s, out_s, out_s, out_s, out_s)):
        rows, h = s.shape[0], s.shape[1] // 2
        bufs += [vm((4, rows, h))] * (i > 1) + [vm((2, 4, rows // 4, h)), vm((4, rows // 4, h)), vm((3, rows // 4, h))]
    dma = pltpu.SemaphoreType.DMA
    scratch = [vm((4,) + s.shape) for s in (out_s, out_s, out_s, out_s, up_s, down_s)] + [vm((n, SP, FF)), vm((n, SP, FF)), vm(row3, F32), vm(row3, F32), vm(row3, F32),
               vm(row3), vm(row3), vm((n, KP, D)), vm((n, KP, D)), vm(row3), vm(row3), vm(row3), vm(row3), vm((n, HEADS, SP, KP)),
               vm((16, D), F32), vm((1, FF), F32), vm((16, D), F32), vm((4, 32, D)), vm((32, D)), vm((32, D), F32), vm((SP, KP), jnp.int32), vm((8, KP), F32),
               vm((16, D), F32), vm((1, FF), F32), vm((96, 128), F32), vm((16, 32, 256), F32), vm((3, 4, 32, 256), F32), vm((3, 32, 256), F32)]
    return pl.pallas_call(
        layer_kernel,
        out_shape=(S(row3, BF), S(row3, F32), S((32, 256), F32)) + (S((3, qkv_s.shape[0], D), BF),) + tuple(S(s.shape, BF) for s in shards[1:]),
        in_specs=[VMEM] * 16 + [ANY] * 4, out_specs=(ANY, ANY, VMEM, ANY, ANY, ANY, ANY),
        scratch_shapes=scratch + bufs + [dma((6, 3, 8)), dma((6, 3, 8)), dma((6, 18)), dma((6, 18)), dma((14,)), dma((9,)), dma((9,)), dma((3, 3)), pltpu.SemaphoreType.REGULAR],
        compiler_params=params(collective_id=0, has_side_effects=True), name="layer")(tok, ups, index, mask, table, up_bias, *vectors, *shards)


def finish_kernel(sm, rq, ro, ru, rd, dq, do, du, dd, gub, tab, *vectors):
    for g in range(3):
        for j in range(3):
            dq[:, j * D + g * 256 : j * D + g * 256 + 256] = rq[g, :, j * 256 : j * 256 + 256].astype(F32)
    do[...] = ro[...].astype(F32)
    du[...] = ru[...].astype(F32)
    dd[...] = rd[...].astype(F32)
    for i, v in enumerate(vectors):
        v[...] = sm[i, :192]
    gub[...] = sm[10:14, :192]
    tab[...] = sm[16:28, :183]


def finish(sm, rq, ro, ru, rd):
    outs = (S((192, 3 * D), F32), S(ro.shape, F32), S(ru.shape, F32), S(rd.shape, F32), S((4, 192), F32), S((HEADS, 183), F32)) + (S((192,), F32),) * 10
    return pl.pallas_call(finish_kernel, out_shape=outs, in_specs=[VMEM] * 5, out_specs=(VMEM,) * 16, compiler_params=params(), name="finish")(sm, rq, ro, ru, rd)


def wide_body(tokens, first_gain, first_shift, qkv_weight, query_bias, value_bias, bias_table, bias_index, out_weight, out_bias, first_scale,
              second_gain, second_shift, up_weight, up_bias, down_weight, down_bias, second_scale, patch_mask, upstream):
    n = tokens.shape[0]

    def whole(v):
        return lax.all_gather(v, "fsdp", axis=0, tiled=True)

    vectors = (first_gain, first_shift, query_bias, value_bias, out_bias, first_scale, second_gain, second_shift, down_bias, second_scale)
    vec = jnp.pad(lax.all_gather(jnp.stack(vectors), "fsdp", axis=1, tiled=True).astype(F32), ((0, 6), (0, 0)))
    upb = whole(up_bias).astype(F32).reshape(1, FF)
    table = jnp.pad(whole(bias_table).T.astype(F32), ((0, 4), (0, 768 - RELS)))
    qkv, outw, upw, downw = whole(qkv_weight), whole(out_weight), whole(up_weight), whole(down_weight)
    index = pad_index(bias_index)
    mask = jnp.pad(patch_mask.astype(F32), ((0, 8 - n), (0, KP - SEQ)))
    norm_one, relative = front(tokens, vec, table, index)
    q, k, v, attend, context = attention(norm_one, qkv, vec, relative)
    layer_out, dout, dup, ddown, gctx, gres, small_mlp, small_up = mlp(tokens, context, outw, upw, downw, vec, upb, mask, upstream)
    tgrad, dqkv, small, tab = back(tokens, norm_one, qkv, vec, index, q, k, v, attend, gctx, gres)
    tab = tab.reshape(6, 16, 128)[:, :HEADS].transpose(1, 0, 2).reshape(HEADS, 768)[:, :RELS].T

    def summed(g):
        part = lax.psum_scatter(g.astype(BF), "fsdp", scatter_dimension=0, tiled=True)
        return lax.psum(part.astype(F32), "dp")

    rows = lax.psum(lax.psum_scatter(jnp.concatenate([small[2:4], small[0:2], small_mlp[::-1][2:]]), "fsdp", scatter_dimension=1, tiled=True), "dp")
    g1, s1, qb, vb, ob, sc1, s2, g2, db, sc2 = rows
    return (layer_out, tgrad, g1, s1, summed(dqkv), qb, vb, summed(tab), summed(dout), ob, sc1, g2, s2, summed(dup), summed(small_up.reshape(FF)), summed(ddown), db, sc2)


def body(wide, tokens, first_gain, first_shift, qkv_weight, query_bias, value_bias, bias_table, bias_index, out_weight, out_bias, first_scale,
         second_gain, second_shift, up_weight, up_bias, down_weight, down_bias, second_scale, patch_mask, upstream):
    if wide:
        return wide_body(tokens, first_gain, first_shift, qkv_weight, query_bias, value_bias, bias_table, bias_index, out_weight, out_bias, first_scale,
                         second_gain, second_shift, up_weight, up_bias, down_weight, down_bias, second_scale, patch_mask, upstream)
    n = tokens.shape[0]
    vectors = (first_gain, first_shift, query_bias, value_bias, out_bias, first_scale, second_gain, second_shift, down_bias, second_scale)
    lo, tg, sm, rqkv, rout, rup, rdown = layer(tokens, upstream, bias_index, patch_mask, bias_table.T, up_bias, vectors,
                                               qkv_weight, out_weight, up_weight, down_weight)
    layer_out, tgrad = lo[:, :SEQ], tg[:, :SEQ]
    dq, do, du, dd, gub, gtab, g1, s1, qb, vb, ob, sc1, g2, s2, db, sc2 = finish(sm, rqkv, rout, rup, rdown)
    return (layer_out, tgrad, g1, s1, dq, qb, vb, gtab.T, do, ob, sc1, g2, s2, du, gub.reshape(FF // 4), dd, db, sc2)


def solution(mesh):
    vector, matrix, batch = P("fsdp"), P("fsdp", None), P(("dp", "fsdp"), None, None)
    in_specs = (batch, vector, vector, matrix, vector, vector, matrix, P(), matrix, vector, vector, vector, vector, matrix, vector, matrix, vector, vector,
                P(("dp", "fsdp"), None), batch)
    out_specs = (batch, batch, vector, vector, matrix, vector, vector, matrix, matrix, vector, vector, vector, vector, matrix, vector, matrix, vector, vector)
    wide = mesh.shape["dp"] != 8 or mesh.shape["fsdp"] != 4
    return jax.shard_map(functools.partial(body, wide), mesh=mesh, in_specs=in_specs, out_specs=out_specs, check_vma=False)
```

```python
import functools
import jax
import jax.numpy as jnp
from jax import lax
from jax.experimental import pallas as pl
from jax.experimental.pallas import tpu as pltpu
from jax.sharding import PartitionSpec as P

D = 768
HEADS = 12
HEAD_DIM = 64
FF = 3072
SEQ = 197
RELS = 732
SP = 208
KP = 256
HALF = SP * KP
EPS = 1e-06
BF = jnp.bfloat16
F32 = jnp.float32
VMEM = pl.BlockSpec(memory_space=pltpu.VMEM)
ANY = pl.BlockSpec(memory_space=pl.ANY)
LIMIT = 63 * 2**20


def dot(a, b):
    return lax.dot_general(a, b, (((1,), (0,)), ((), ())), preferred_element_type=F32)


def dot_nt(a, b):
    return lax.dot_general(a, b, (((1,), (1,)), ((), ())), preferred_element_type=F32)


def dot_tn(a, b):
    return lax.dot_general(a, b, (((0,), (0,)), ((), ())), preferred_element_type=F32)


def rowmean(v):
    return jnp.sum(v, axis=-1, keepdims=True) * (1.0 / D)


def colsum(v):
    return jnp.sum(v, axis=0, keepdims=True)


def xhat_of(v):
    centred = v - rowmean(v)
    rstd = lax.rsqrt(rowmean(centred * centred) + EPS)
    return centred * rstd, rstd


def pad_rows(v):
    return jnp.concatenate([v, jnp.zeros((SP - SEQ, v.shape[1]), v.dtype)], axis=0)


GAIN1, SHIFT1, QBIAS, VBIAS, OBIAS, SCALE1, GAIN2, SHIFT2, DBIAS, SCALE2 = range(10)


def front_kernel(tok, vec, table, index, norm_one, relative):
    images = tok.shape[0]
    gain, shift = vec[GAIN1 : GAIN1 + 1, :], vec[SHIFT1 : SHIFT1 + 1, :]
    for b in range(images):
        xhat, _ = xhat_of(pad_rows(tok[b].astype(F32)))
        norm_one[b] = (xhat * gain + shift).astype(BF)
    lookup(table, index, [relative.at[h] for h in range(HEADS)])


def lookup(table, index, relative):
    lanes = lax.broadcasted_iota(jnp.int32, (16, 128), 1)

    def rows(r, carry):
        at = pl.ds(pl.multiple_of(r * 16, 16), 16)
        for half in range(2):
            idx = index[at, half * 128 : half * 128 + 128]
            low = idx & 127
            high = idx >> 7
            for h in range(HEADS):
                out = jnp.zeros((16, 128), F32)
                for c in range(6):
                    part = jnp.broadcast_to(table[h : h + 1, c * 128 : c * 128 + 128], (16, 128))
                    got = jnp.take_along_axis(part, low, axis=1, mode="promise_in_bounds")
                    out = jnp.where(high == c, got, out)
                if half == 1:
                    out = jnp.where(lanes < SEQ - 128, out, -1e30)
                relative[h][at, half * 128 : half * 128 + 128] = out.astype(BF)
        return carry

    lax.fori_loop(0, SP // 16, rows, 0)


def lane_masks(rows):
    lane = lax.broadcasted_iota(jnp.int32, (rows, 128), 1)
    return lane < HEAD_DIM


def split_heads(v, first):
    zero = jnp.zeros_like(v)
    return jnp.where(first, v, zero), jnp.where(first, zero, v)


def project(norm_one, qkv, vec, q, k, v):
    images = norm_one.shape[0]
    k[:, SP:, :] = jnp.zeros((images, KP - SP, D), BF)
    v[:, SP:, :] = jnp.zeros((images, KP - SP, D), BF)

    def chunk(i, carry):
        at = pl.ds(pl.multiple_of(i * 256, 256), 256)
        rows = norm_one[...].reshape(images * SP, D)
        pq = dot(rows, qkv[:, at])
        q[:, :, at] = ((pq + vec[QBIAS : QBIAS + 1, at]) * 0.125).astype(BF).reshape(images, SP, 256)
        pk = dot(rows, qkv[:, pl.ds(pl.multiple_of(D + i * 256, 256), 256)])
        k[:, :SP, at] = pk.astype(BF).reshape(images, SP, 256)
        pv = dot(rows, qkv[:, pl.ds(pl.multiple_of(2 * D + i * 256, 256), 256)])
        v[:, :SP, at] = (pv + vec[VBIAS : VBIAS + 1, at]).astype(BF).reshape(images, SP, 256)
        return carry

    lax.fori_loop(0, D // 256, chunk, 0)


def attend_pair(b, hp, at, q, k, v, relative, attend, context):
    first = lane_masks(KP)
    q2 = q[b, :, at]
    ks = split_heads(k[b, :, at], first)
    vs = split_heads(v[b, :, at], first)
    probs = []
    for e in range(2):
        h = 2 * hp + e
        s = dot_nt(q2, ks[e]) + relative[h][...].astype(F32)
        s = jnp.exp(s - jnp.max(s, axis=-1, keepdims=True))
        p = (s * (1.0 / jnp.sum(s, axis=-1, keepdims=True))).astype(BF)
        attend[b, h] = p
        probs.append(p)
    context[b, :, at] = (dot(probs[0], vs[0]) + dot(probs[1], vs[1])).astype(BF)


def attention_kernel(norm_one, qkv, vec, relative, q, k, v, attend, context):
    images = norm_one.shape[0]
    relative = [relative.at[h] for h in range(HEADS)]
    project(norm_one, qkv, vec, q, k, v)

    def image(b, carry):
        for hp in range(HEADS // 2):
            attend_pair(b, hp, slice(hp * 128, hp * 128 + 128), q, k, v, relative, attend, context)
        return carry

    lax.fori_loop(0, images, image, 0)


def gelu_both(v):
    cdf = 0.5 * (1.0 + lax.erf(v * 0.7071067811865476))
    pdf = jnp.exp(v * v * -0.5) * 0.3989422804014327
    return v * cdf, cdf + v * pdf


def mlp_kernel(tok, ctx, out_hbm, up_hbm, down_hbm, vec, upb, mask, ups,
               layer_out, dout, dup, ddown, gctx, gres, small, small_up,
               outw, upw, downw, hid, att, n2, act, slope, acc, gd, gy_s, sems):
    images = tok.shape[0]
    R = images * SP
    loads = [pltpu.make_async_copy(s, d, sems.at[i]) for i, (s, d) in enumerate(
        ((out_hbm, outw), (up_hbm, upw), (down_hbm, downw)))]
    for l in loads:
        l.start()
    obias, scale1 = vec[OBIAS : OBIAS + 1, :], vec[SCALE1 : SCALE1 + 1, :]
    gain2, shift2 = vec[GAIN2 : GAIN2 + 1, :], vec[SHIFT2 : SHIFT2 + 1, :]
    dbias, scale2 = vec[DBIAS : DBIAS + 1, :], vec[SCALE2 : SCALE2 + 1, :]
    maskt = jnp.transpose(mask[...], (1, 0))
    loads[0].wait()
    for b in range(images):
        attn = dot(ctx[b], outw[...]) + obias
        att[b] = attn
        h = pad_rows(tok[b].astype(F32)) + scale1 * attn
        hid[b] = h
        xhat, _ = xhat_of(h)
        n2[b] = (xhat * gain2 + shift2).astype(BF)
    loads[1].wait()
    loads[2].wait()
    acc[...] = jnp.zeros_like(acc)
    W = 256

    def forward(f, carry):
        at = pl.ds(pl.multiple_of(f * W, W), W)
        for b in range(images):
            u = dot(n2[b], upw[:, at]) + upb[:, at]
            g, s = gelu_both(u)
            g = g.astype(BF)
            act[b, :, at] = g
            slope[b, :, at] = s.astype(BF)
            acc[b] += dot(g, downw[at, :])
        return carry

    lax.fori_loop(0, FF // W, forward, 0)
    sums = [jnp.zeros((1, D), F32) for _ in range(6)]
    for b in range(images):
        down = acc[b] + dbias
        layer_out[b] = (hid[b] + scale2 * down).astype(BF)[:SEQ]
        gy = pad_rows(ups[b].astype(F32)) * maskt[:SP, b : b + 1]
        gy_s[b] = gy.astype(BF)
        sums[0] += colsum(gy * down)
        full = gy * scale2
        sums[1] += colsum(full)
        gd[b] = full.astype(BF)
    acc[...] = jnp.zeros_like(acc)

    def backward(f, carry):
        at = pl.ds(pl.multiple_of(f * W, W), W)
        total = jnp.zeros((1, W), F32)
        lows = []
        for b in range(images):
            gg = dot_nt(gd[b], downw[at, :]) * slope[b, :, at].astype(F32)
            total += colsum(gg)
            low = gg.astype(BF)
            lows.append(low)
            acc[b] += dot_nt(low, upw[:, at])
        small_up[:, at] = total
        low = jnp.concatenate(lows, axis=0)
        dup[:, at] = dot_tn(n2[...].reshape(R, D), low).astype(BF)
        ddown[at, :] = dot_tn(act[:, :, at].reshape(R, W), gd[...].reshape(R, D)).astype(BF)
        return carry

    lax.fori_loop(0, FF // W, backward, 0)
    for b in range(images):
        xhat, rstd = xhat_of(hid[b])
        g = acc[b]
        sums[2] += colsum(g * xhat)
        sums[3] += colsum(g)
        gg = g * gain2
        gh = (gg - rowmean(gg) - xhat * rowmean(gg * xhat)) * rstd
        res = gy_s[b].astype(F32) + gh
        gres[b] = res
        sums[4] += colsum(res * att[b])
        full = res * scale1
        sums[5] += colsum(full)
        n2[b] = full.astype(BF)
    dout[...] = dot_tn(ctx[...].reshape(R, D), n2[...].reshape(R, D)).astype(BF)
    for b in range(images):
        gctx[b] = dot_nt(n2[b], outw[...]).astype(BF)
    small[...] = jnp.concatenate(sums + [jnp.zeros((2, D), F32)], axis=0)


def attend_back(b, hp, at, q, k, v, attend, gctx, gtab, gq, gk, gv, qsum, vsum):
    first = lane_masks(KP)
    firsts = first[:SP]
    v2 = split_heads(v[b, :, at], first)
    k2 = split_heads(k[b, :, at], first)
    q2 = split_heads(q[b, :, at], firsts)
    g2 = gctx[b, :, at]
    gs2 = split_heads(g2, firsts)
    dq = jnp.zeros((SP, 128), F32)
    dk = jnp.zeros((KP, 128), F32)
    dv = jnp.zeros((KP, 128), F32)
    for e in range(2):
        h = 2 * hp + e
        a = attend[b, h]
        af = a.astype(F32)
        ga = dot_nt(g2, v2[e])
        w = af * ga
        inner = jnp.sum(w, axis=-1, keepdims=True)
        gs = w - af * inner
        gtab[h][...] += gs
        low = gs.astype(BF)
        dq += dot(low, k2[e])
        dk += dot_tn(low, q2[e])
        dv += dot_tn(a, gs2[e])
    dq = dq * 0.125
    qsum[:, at] += colsum(dq)
    vsum[:, at] += colsum(dv)
    gq[b, :, at] = dq.astype(BF)
    gk[b, :, at] = dk[:SP].astype(BF)
    gv[b, :, at] = dv[:SP].astype(BF)


def table_rows(gtab, index, total, start, stop):
    ids = lax.broadcasted_iota(jnp.int32, (128, KP), 0).astype(F32).astype(BF)
    ones, zeros = jnp.ones((128, KP), BF), jnp.zeros((128, KP), BF)
    highs = lax.broadcasted_iota(jnp.int32, (8, KP), 0)

    def block(i, acc):
        idx = index[pl.ds(pl.multiple_of(i * 8, 8), 8), :]
        lows = (idx & 127).astype(F32)
        for r in range(8):
            hot = jnp.where(ids == lows[r : r + 1, :].astype(BF), ones, zeros)
            mask = highs == (idx[r : r + 1, :] >> 7)
            g = jnp.concatenate([jnp.where(mask, jnp.broadcast_to(t[pl.ds(i * 8 + r, 1), :], (8, KP)), 0.0) for t in gtab], axis=0)
            g1 = g.astype(BF)
            g2 = (g - g1.astype(F32)).astype(BF)
            acc = acc + dot_nt(jnp.concatenate([g1, g2], axis=0), hot)
        return acc

    return lax.fori_loop(start, stop, block, total)


def table_back(gtab, index, out):
    total = table_rows(gtab, index, jnp.zeros((192, 128), F32), 0, SP // 8)
    out[...] = total[:96] + total[96:]


def back_kernel(tok, norm_one, qkv_hbm, vec, index, q, k, v, attend, gctx, gres,
                tgrad, dqkv, small, tab, gtab, gqkv, qkv, sem):
    images = tok.shape[0]
    R = images * SP
    load = pltpu.make_async_copy(qkv_hbm, qkv, sem)
    load.start()
    gtab[...] = jnp.zeros_like(gtab)
    gtab = [gtab.at[h] for h in range(HEADS)]
    small[...] = jnp.zeros_like(small)
    gq, gk, gv = (gqkv.at[:, :, i * D : (i + 1) * D] for i in range(3))
    qsum, vsum = small.at[0:1, :], small.at[1:2, :]

    for hp in range(HEADS // 2):

        def one(b, carry, hp=hp):
            attend_back(b, hp, slice(hp * 128, hp * 128 + 128), q, k, v, attend, gctx, gtab, gq, gk, gv, qsum, vsum)
            return carry

        lax.fori_loop(0, images, one, 0)
    table_back(gtab, index, tab)

    def chunk(i, carry):
        at = pl.ds(pl.multiple_of(i * 256, 256), 256)
        dqkv[:, at] = dot_tn(norm_one[...].reshape(R, D), gqkv[:, :, at].reshape(R, 256)).astype(BF)
        return carry

    lax.fori_loop(0, 3 * D // 256, chunk, 0)
    load.wait()
    gain = vec[GAIN1 : GAIN1 + 1, :]
    for b in range(images):
        xhat, rstd = xhat_of(pad_rows(tok[b].astype(F32)))
        g = dot_nt(gqkv[b], qkv[...])
        small[2:3, :] += colsum(g * xhat)
        small[3:4, :] += colsum(g)
        gg = g * gain
        gi = (gg - rowmean(gg) - xhat * rowmean(gg * xhat)) * rstd
        tgrad[b] = (gres[b] + gi)[:SEQ]


def params(**kw):
    return pltpu.CompilerParams(vmem_limit_bytes=LIMIT, **kw)


def S(shape, dtype):
    return jax.ShapeDtypeStruct(shape, dtype)


def front(tok, vec, table, index):
    n = tok.shape[0]
    return pl.pallas_call(front_kernel, out_shape=(S((n, SP, D), BF), S((HEADS, SP, KP), BF)),
                          in_specs=[VMEM] * 4, out_specs=(VMEM, VMEM), compiler_params=params(), name="front")(tok, vec, table, index)


def attention(norm_one, qkv, vec, relative):
    n = norm_one.shape[0]
    return pl.pallas_call(attention_kernel,
                          out_shape=(S((n, SP, D), BF), S((n, KP, D), BF), S((n, KP, D), BF), S((n, HEADS, SP, KP), BF), S((n, SP, D), BF)),
                          in_specs=[VMEM] * 4, out_specs=(VMEM,) * 5, compiler_params=params(), name="attention")(norm_one, qkv, vec, relative)


def mlp(tok, ctx, outw, upw, downw, vec, upb, mask, ups):
    n = tok.shape[0]
    return pl.pallas_call(
        mlp_kernel,
        out_shape=(S((n, SEQ, D), BF), S((D, D), BF), S((D, FF), BF), S((FF, D), BF), S((n, SP, D), BF), S((n, SP, D), F32), S((8, D), F32), S((1, FF), F32)),
        in_specs=[VMEM, VMEM, ANY, ANY, ANY, VMEM, VMEM, VMEM, VMEM], out_specs=(VMEM,) * 8,
        scratch_shapes=[pltpu.VMEM((D, D), BF), pltpu.VMEM((D, FF), BF), pltpu.VMEM((FF, D), BF),
                        pltpu.VMEM((n, SP, D), F32), pltpu.VMEM((n, SP, D), F32), pltpu.VMEM((n, SP, D), BF),
                        pltpu.VMEM((n, SP, FF), BF), pltpu.VMEM((n, SP, FF), BF), pltpu.VMEM((n, SP, D), F32),
                        pltpu.VMEM((n, SP, D), BF), pltpu.VMEM((n, SP, D), BF), pltpu.SemaphoreType.DMA((3,))],
        compiler_params=params(), name="mlp")(tok, ctx, outw, upw, downw, vec, upb, mask, ups)


def back(tok, norm_one, qkv, vec, index, q, k, v, attend, gctx, gres):
    n = tok.shape[0]
    return pl.pallas_call(
        back_kernel,
        out_shape=(S((n, SEQ, D), F32), S((D, 3 * D), BF), S((8, D), F32), S((96, 128), F32)),
        in_specs=[VMEM, VMEM, ANY] + [VMEM] * 8, out_specs=(VMEM,) * 4,
        scratch_shapes=[pltpu.VMEM((16, SP, KP), F32), pltpu.VMEM((n, SP, 3 * D), BF), pltpu.VMEM((D, 3 * D), BF), pltpu.SemaphoreType.DMA(())],
        compiler_params=params(), name="back")(tok, norm_one, qkv, vec, index, q, k, v, attend, gctx, gres)


def pad_index(bias_index):
    return jnp.pad(bias_index, ((0, SP - SEQ), (0, KP - SEQ)))
MESH = pl.DeviceIdType.MESH


class Place:
    def __init__(self):
        dp, z = lax.axis_index("dp"), lax.axis_index("fsdp")
        y, x, c = dp // 4, (dp // 2) % 2, dp % 2
        xn, yn = dp + 2 - 4 * x, dp + 4 - 8 * y
        q = dp // 2
        qx, qy = q + 1 - 2 * x, q + 2 - 4 * y
        self.dp, self.z, self.c, self.q = dp, z, c, q
        self.near = (xn * (1 - c) + yn * c, z)
        self.far = (yn * (1 - c) + xn * c, z)
        self.x, self.y = (xn, z), (yn, z)
        self.twin = (dp + 1 - 2 * c, z)
        self.q_near = qx * (1 - c) + qy * c
        self.q_far = qy * (1 - c) + qx * c
        self.q_both = 3 - q

    def up(self, d):
        return (self.dp, (self.z + d) % 4)

    def barrier(self):
        sem = pltpu.get_barrier_semaphore()
        peers = [self.near, self.far, self.twin] + [self.up(d) for d in (1, 2, 3)]
        for peer in peers:
            pl.semaphore_signal(sem, inc=1, device_id=peer, device_id_type=MESH)
        pl.semaphore_wait(sem, len(peers))


def aligned(i, size):
    return pl.ds(pl.multiple_of(i * size, size), size)


class Gather:
    def __init__(self, place, shard, full, send, recv, local):
        self.p, self.shard, self.full, self.send, self.recv, self.local = place, shard, full, send, recv, local
        self.rows, self.cols = full.shape[1] // 4, full.shape[2] // 2

    def region(self, zb, q, c):
        return self.full.at[zb, aligned(q, self.rows), aligned(c, self.cols)]

    def copy(self, d, slot, src, dst, peer):
        return pltpu.make_async_remote_copy(src_ref=src, dst_ref=dst, send_sem=self.send.at[d - 1, slot], recv_sem=self.recv.at[d - 1, slot],
                                            device_id=peer, device_id_type=MESH)

    def over_z(self, d):
        p = self.p
        if self.shard is None:
            src = self.region(p.z, p.q, p.c)
        else:
            src = self.shard.at[aligned(p.q, self.rows), aligned(p.c, self.cols)]
        return self.copy(d, 0, src, self.region(p.z, p.q, p.c), p.up(d))

    def passed(self, d, slot, q, peer):
        p = self.p
        r = self.region((p.z + 4 - d) % 4, q, p.c)
        return self.copy(d, slot, r, r, peer)

    def own(self):
        return pltpu.make_async_copy(self.shard, self.full.at[self.p.z], self.local)

    def begin(self):
        for d in (1, 2, 3):
            self.over_z(d).start()
        if self.shard is not None:
            self.own().start()

    def part(self, d, i):
        p = self.p
        slot, q, peer = ((1, p.q, p.near), (2, p.q, p.far), (4, p.q, p.twin), (3, p.q_near, p.far), (5, p.q_near, p.twin),
                         (6, p.q_far, p.twin), (7, p.q_both, p.twin))[i]
        return self.passed(d, slot, q, peer)

    def spread(self, d):
        self.over_z(d).wait_recv()
        for i in (0, 1, 2):
            self.part(d, i).start()

    def relay(self, d):
        self.part(d, 0).wait_recv()
        for i in (3, 4):
            self.part(d, i).start()

    def close(self, d):
        self.part(d, 1).wait_recv()
        self.part(d, 5).start()
        self.part(d, 3).wait_recv()
        self.part(d, 6).start()

    def finish(self):
        if self.shard is not None:
            self.own().wait()
        for d in (1, 2, 3):
            for i in (2, 4, 5, 6):
                self.part(d, i).wait_recv()

    def drain(self):
        for d in (1, 2, 3):
            self.over_z(d).wait_send()
            for i in range(7):
                self.part(d, i).wait_send()

    def steps(self):
        return [lambda d=d: self.spread(d) for d in (1, 2, 3)] + [lambda d=d: self.relay(d) for d in (1, 2, 3)] + [
            lambda d=d: self.close(d) for d in (1, 2, 3)] + [self.finish]


class Reduce:
    def __init__(self, place, grad, got, half, quarter, pieces, out, send, recv, local):
        self.p, self.grad, self.got, self.half, self.quarter, self.pieces, self.out = place, grad, got, half, quarter, pieces, out
        self.send, self.recv, self.local = send, recv, local
        self.rows, self.cols = grad.shape[1] // 4, grad.shape[2] // 2

    def copy(self, slot, src, dst, peer):
        return pltpu.make_async_remote_copy(src_ref=src, dst_ref=dst, send_sem=self.send.at[slot], recv_sem=self.recv.at[slot], device_id=peer, device_id_type=MESH)

    def twin(self, i):
        q = self.quarters()[i]
        return self.copy(14 + i, self.grad.at[:, aligned(q, self.rows), aligned(1 - self.p.c, self.cols)], self.got(q), self.p.twin)

    def quarters(self):
        p = self.p
        return (p.q_far, p.q_both, p.q, p.q_near)

    def mine(self, q):
        return self.grad.at[:, aligned(q, self.rows), aligned(self.p.c, self.cols)]

    def near(self, i):
        q = (self.p.q_near, self.p.q_both)[i]
        return self.copy(1 + i, self.mine(q), self.half.at[i], self.p.near)

    def far(self):
        return self.copy(3, self.half.at[1], self.quarter, self.p.far)

    def over_z(self, d):
        return self.copy(3 + d, self.quarter.at[(self.p.z + d) % 4], self.pieces.at[d - 1], self.p.up(d))

    def region(self, q):
        return self.out.at[aligned(q, self.rows), aligned(self.p.c, self.cols)]

    def passed(self, i):
        p = self.p
        q, peer = ((p.q, p.near), (p.q, p.far), (p.q, p.twin), (p.q_near, p.far), (p.q_near, p.twin), (p.q_far, p.twin), (p.q_both, p.twin))[i]
        src = self.quarter.at[p.z] if i < 3 else self.region(q)
        return self.copy(7 + i, src, self.region(q), peer)

    def own(self):
        return pltpu.make_async_copy(self.quarter.at[self.p.z], self.region(self.p.q), self.local)

    def begin(self):
        for i in range(4):
            self.twin(i).start()

    def add(self, dst, src):
        def one(i, carry):
            dst[i] = (dst[i].astype(F32) + src[i].astype(F32)).astype(BF)
            return carry

        lax.fori_loop(0, 4, one, 0)

    def fold(self, q):
        self.add(self.mine(q), self.got(q))

    def first_a(self):
        self.twin(0).wait_recv()
        self.fold(self.p.q_near)
        self.near(0).start()

    def first_b(self):
        self.twin(1).wait_recv()
        self.fold(self.p.q_both)
        self.near(1).start()

    def first_c(self):
        self.twin(2).wait_recv()
        self.fold(self.p.q)
        self.twin(3).wait_recv()
        self.fold(self.p.q_far)

    def second(self):
        self.near(1).wait_recv()
        self.add(self.half.at[1], self.mine(self.p.q_far))
        self.far().start()
        self.near(0).wait_recv()
        self.add(self.half.at[0], self.mine(self.p.q))

    def third(self):
        self.far().wait_recv()
        self.add(self.quarter, self.half.at[0])
        for d in (1, 2, 3):
            self.over_z(d).start()

    def fourth(self):
        for d in (1, 2, 3):
            self.over_z(d).wait_recv()
        total = self.quarter[self.p.z].astype(F32)
        for d in (1, 2, 3):
            total += self.pieces[d - 1].astype(F32)
        self.quarter[self.p.z] = total.astype(BF)
        for i in (0, 1, 2):
            self.passed(i).start()
        self.own().start()

    def fifth(self):
        self.passed(0).wait_recv()
        self.passed(3).start()
        self.passed(4).start()

    def sixth(self):
        self.passed(1).wait_recv()
        self.passed(5).start()
        self.passed(3).wait_recv()
        self.passed(6).start()

    def finish(self):
        for i in (2, 4, 5, 6):
            self.passed(i).wait_recv()
        self.own().wait()

    def drain(self):
        for i in range(4):
            self.twin(i).wait_send()
        self.near(0).wait_send()
        self.near(1).wait_send()
        self.far().wait_send()
        for d in (1, 2, 3):
            self.over_z(d).wait_send()
        for i in range(7):
            self.passed(i).wait_send()

    def steps(self):
        return [self.first_a, self.first_b, self.first_c, self.second, self.third, self.fourth, self.fifth, self.sixth]
def unstack_small(block, vec, upb, table):
    vec[...] = jnp.zeros_like(vec)
    table[...] = jnp.zeros_like(table)
    for z in range(4):
        part = block[z].astype(F32)
        vec[:, z * 192 : z * 192 + 192] = part[:16, :192]
        upb[:, z * 768 : z * 768 + 768] = part[10:11, :]
        table[:, z * 183 : z * 183 + 183] = part[16:32, :183]


def head_view(ref, h):
    return ref.at[h // 3, :, (h % 3) * 256 : (h % 3) * 256 + 256]


def layer_kernel(tok, ups, idx_in, mask_in, table_in, ub_in, v0, v1, v2, v3, v4, v5, v6, v7, v8, v9, qkv_s, out_s, up_s, down_s,
                 lo_hbm, tg_hbm, sm_out, rqkv, rout, rup, rdown,
                 qw0, qw1, qw2, outw, upw, downw, A, B, hid, att, acc, n1, q, k, v, ctx, n2, gd, lo, attend, vec, upb, table, block, small_in, small_f, index, mask,
                 sums, upsum, tab, sm, sm_got, sm_piece,
                 half0, quart0, piece0, half1, quart1, piece1, got2, half2, quart2, piece2, got3, half3, quart3, piece3,
                 got4, half4, quart4, piece4, got5, half5, quart5, piece5,
                 gsend, grecv, rsend, rrecv, local, ssend, srecv, qsem, free):
    p = Place()
    images = tok.shape[0]
    R = images * SP
    qw = (qw0, qw1, qw2)
    groups = [[pltpu.make_async_copy(qkv_s.at[:, j * D + g * 256 : j * D + g * 256 + 256], qw[g].at[p.z, :, j * 256 : j * 256 + 256], qsem.at[g, j])
               for j in range(3)] for g in range(3)]
    for group in groups:
        for c in group:
            c.start()
    small_f[...] = jnp.zeros_like(small_f)
    for i, vector in enumerate((v0, v1, v2, v3, v4, v5, v6, v7, v8, v9)):
        small_f[i, :192] = vector[...].astype(F32)
    small_f[10, :] = ub_in[...].astype(F32)
    small_f[16:28, :183] = table_in[...].astype(F32)
    small_in[...] = small_f[...].astype(BF)
    p.barrier()

    units = [(None, qw[g]) for g in range(3)] + [(out_s, outw), (up_s, upw), (down_s, downw)]
    gathers = [Gather(p, s, f, gsend.at[i], grecv.at[i], local.at[i]) for i, (s, f) in enumerate(units)]
    block[p.z] = small_in[...]
    smalls = [pltpu.make_async_remote_copy(src_ref=small_in, dst_ref=block.at[p.z], send_sem=ssend.at[d - 1], recv_sem=srecv.at[d - 1], device_id=p.up(d), device_id_type=MESH) for d in (1, 2, 3)]
    for s in smalls:
        s.start()
    for g in range(4):
        if g < 3:
            for c in groups[g]:
                c.wait()
        gathers[g].begin()
    index[...] = jnp.zeros_like(index)
    index[:SEQ, :SEQ] = idx_in[...]
    mask[...] = jnp.zeros_like(mask)
    mask[:images, :SEQ] = mask_in[...].astype(F32)
    for s in smalls:
        s.wait_recv()
    unstack_small(block, vec, upb, table)
    row = lambda i: vec[i : i + 1, :]
    todo = []

    def plan(steps, times):
        todo.extend(zip(times, steps))
        todo.sort(key=lambda e: e[0])

    def advance(now):
        while todo and todo[0][0] <= now:
            todo.pop(0)[1]()

    for g, (spread, relay, close, finish) in zip(gathers, GATHER_PLAN):
        plan(g.steps(), (spread, spread + 0.5, spread + 1, relay, relay + 0.5, relay + 1, close, close + 0.5, close + 1, finish))
    plan([gathers[4].begin, gathers[5].begin], BEGIN_PLAN)
    for b in range(images):
        xhat, _ = xhat_of(pad_rows(tok[b].astype(F32)))
        n1[b] = (xhat * row(GAIN1) + row(SHIFT1)).astype(BF)
        advance(5 + b)
    relative = [head_view(gd, h) for h in range(HEADS)]
    lookup(table, index, relative)

    k[:, SP:, :] = jnp.zeros((images, KP - SP, D), BF)
    v[:, SP:, :] = jnp.zeros((images, KP - SP, D), BF)
    for g in range(3):
        at = slice(g * 256, g * 256 + 256)
        advance(GATHER_PLAN[g][3])

        def weight(j, g=g):
            return qw[g][:, :, j * 256 : j * 256 + 256].reshape(D, 256)

        rows = n1[...].reshape(R, D)
        q[:, :, at] = ((dot(rows, weight(0)) + vec[QBIAS : QBIAS + 1, at]) * 0.125).astype(BF).reshape(images, SP, 256)
        k[:, :SP, at] = dot(rows, weight(1)).astype(BF).reshape(images, SP, 256)
        v[:, :SP, at] = (dot(rows, weight(2)) + vec[VBIAS : VBIAS + 1, at]).astype(BF).reshape(images, SP, 256)
        advance(17 + 8 * g)
        for hp in (2 * g, 2 * g + 1):

            def one(b, carry, hp=hp):
                attend_pair(b, hp, slice(hp * 128, hp * 128 + 128), q, k, v, relative, attend, ctx)
                return carry

            lax.fori_loop(0, images, one, 0)
            advance(20 + 8 * g + 3 * (hp - 2 * g))

    advance(GATHER_PLAN[3][3])
    for b in range(images):
        attn = dot(ctx[b], outw[...].reshape(D, D)) + row(OBIAS)
        att[b] = attn
        h = pad_rows(tok[b].astype(F32)) + row(SCALE1) * attn
        hid[b] = h
        xhat, _ = xhat_of(h)
        n2[b] = (xhat * row(GAIN2) + row(SHIFT2)).astype(BF)
    advance(GATHER_PLAN[4][3])
    W = 256

    def expand(f, carry):
        at = aligned(f, W)
        u = dot(n2[...].reshape(R, D), upw[:, :, at].reshape(D, W)) + upb[:, at]
        g, s = gelu_both(u)
        A[:, :, at] = g.astype(BF).reshape(images, SP, W)
        B[:, :, at] = s.astype(BF).reshape(images, SP, W)
        return carry

    for part in range(4):
        lax.fori_loop(part * 3, part * 3 + 3, expand, 0)
        advance(46 + 3 * part)
    advance(1000)
    for i in range(D // 256):
        at = slice(i * 256, i * 256 + 256)
        acc[:, :, at] = dot(A[...].reshape(R, FF), downw[:, :, at].reshape(FF, 256)).reshape(images, SP, 256)
    maskt = jnp.transpose(mask[...], (1, 0))
    sums[...] = jnp.zeros_like(sums)

    def add_sum(i, value):
        sums[i : i + 1, :] += colsum(value)

    def grad_y(b):
        return pad_rows(ups[b].astype(F32)) * maskt[:SP, b : b + 1]

    for b in range(images):
        down = acc[b] + row(DBIAS)
        lo[b] = (hid[b] + row(SCALE2) * down).astype(BF)
        gy = grad_y(b)
        add_sum(SCALE2, gy * down)
        full = gy * row(SCALE2)
        add_sum(DBIAS, full)
        gd[b] = full.astype(BF)
    lo_copy = pltpu.make_async_copy(lo, lo_hbm, local.at[12])
    lo_copy.start()

    for g in gathers:
        g.drain()

    def contract(f, carry):
        at = aligned(f, W)
        z, r = f // 3, f % 3
        rows = aligned(r, W)
        gg = dot_nt(gd[...].reshape(R, D), downw[z, rows, :]) * B[:, :, at].reshape(R, W).astype(F32)
        upsum[:, at] = colsum(gg)
        B[:, :, at] = gg.astype(BF).reshape(images, SP, W)
        downw[z, rows, :] = dot_tn(A[:, :, at].reshape(R, W), gd[...].reshape(R, D)).astype(BF)
        return carry

    lax.fori_loop(0, FF // W, contract, 0)
    pl.semaphore_signal(free, inc=1, device_id=p.twin, device_id_type=MESH)

    def got_down(q):
        return A.at[:, :192, pl.ds(pl.multiple_of(1536 + q * 384, 128), 384)]

    def got_up(q):
        return A.at[:, aligned(q, 48), :1536]

    def got_of(ref, rows):
        return lambda q: ref.at[:, aligned(q, rows), :]

    parts = ((downw, got_down, half0, quart0, piece0, rdown), (upw, got_up, half1, quart1, piece1, rup),
             (outw, got_of(got2, 48), half2, quart2, piece2, rout), (qw0, got_of(got3, 48), half3, quart3, piece3, rqkv.at[0]),
             (qw1, got_of(got4, 48), half4, quart4, piece4, rqkv.at[1]), (qw2, got_of(got5, 48), half5, quart5, piece5, rqkv.at[2]))
    red = [Reduce(p, *part, rsend.at[i], rrecv.at[i], local.at[6 + i]) for i, part in enumerate(parts)]

    def launch(i):
        red[i].begin()
        plan(red[i].steps(), REDUCE_PLAN[i])

    pl.semaphore_wait(free, 1)
    launch(0)
    for i in range(4):
        acc[:, :, i * 192 : i * 192 + 192] = dot_nt(B[...].reshape(R, FF), upw[i]).reshape(images, SP, 192)
        advance(13.5 + 1.5 * i)

    def widen(f, carry):
        at = aligned(f, W)
        upw[:, :, at] = dot_tn(n2[...].reshape(R, D), B[:, :, at].reshape(R, W)).astype(BF).reshape(4, D // 4, W)
        return carry

    for i in range(4):
        lax.fori_loop(3 * i, 3 * i + 3, widen, 0)
        advance(20 + 2 * i)
    launch(1)
    for b in range(images):
        xhat, rstd = xhat_of(hid[b])
        g = acc[b]
        add_sum(GAIN2, g * xhat)
        add_sum(SHIFT2, g)
        gg = g * row(GAIN2)
        res = grad_y(b) + (gg - rowmean(gg) - xhat * rowmean(gg * xhat)) * rstd
        hid[b] = res
        add_sum(SCALE1, res * att[b])
        full = res * row(SCALE1)
        add_sum(OBIAS, full)
        n2[b] = full.astype(BF)
        advance(27 + b)
    gctx = B.at[:, :, 3 * D :]
    for b in range(images):
        gctx[b] = dot_nt(n2[b], outw[...].reshape(D, D)).astype(BF)
    for i in range(3):
        at = slice(i * 256, i * 256 + 256)
        outw[:, :, at] = dot_tn(ctx[...].reshape(R, D), n2[:, :, at].reshape(R, 256)).astype(BF).reshape(4, D // 4, 256)
    launch(2)
    advance(33)

    acc[...] = jnp.zeros_like(acc)
    gtab = [head_view(acc, h) for h in range(HEADS)]
    gq, gk, gv = (B.at[:, :, i * D : (i + 1) * D] for i in range(3))
    qsum, vsum = sums.at[QBIAS : QBIAS + 1, :], sums.at[VBIAS : VBIAS + 1, :]
    for g in range(3):
        now = 33 + 11 * g
        for hp in (2 * g, 2 * g + 1):
            for part in range(2):

                def one(i, carry, hp=hp, part=part):
                    attend_back(part * (images // 2) + i, hp, slice(hp * 128, hp * 128 + 128), q, k, v, attend, gctx, gtab, gq, gk, gv, qsum, vsum)
                    return carry

                lax.fori_loop(0, images // 2, one, 0)
                now += 2
                advance(now)
        grads = [B.at[:, :, j * D + g * 256 : j * D + g * 256 + 256] for j in range(3)]
        term = sum(dot_nt(grads[j][...].reshape(R, 256), qw[g][:, :, j * 256 : j * 256 + 256].reshape(D, 256)) for j in range(3)).reshape(images, SP, D)
        att[...] = term if g == 0 else att[...] + term
        for j in range(3):
            qw[g][:, :, j * 256 : j * 256 + 256] = dot_tn(n1[...].reshape(R, D), grads[j][...].reshape(R, 256)).astype(BF).reshape(4, D // 4, 256)
        launch(3 + g)
        advance(now + 3)
    for b in range(images):
        xhat, rstd = xhat_of(pad_rows(tok[b].astype(F32)))
        g = att[b]
        add_sum(GAIN1, g * xhat)
        add_sum(SHIFT1, g)
        gg = g * row(GAIN1)
        att[b] = hid[b] + (gg - rowmean(gg) - xhat * rowmean(gg * xhat)) * rstd
        advance(67 + b)
    tg_copy = pltpu.make_async_copy(att, tg_hbm, local.at[13])
    tg_copy.start()
    total = jnp.zeros((192, 128), F32)
    for i in range(5):
        total = table_rows(gtab, index, total, 5 * i, 5 * i + 5)
        advance(72 + 2 * (i + 1))
    tab[...] = total[:96] + total[96:]
    sm[...] = jnp.zeros_like(sm)
    flat = table
    for h in range(HEADS):
        for c in range(6):
            flat[h : h + 1, c * 128 : c * 128 + 128] = tab[h * 8 + c : h * 8 + c + 1, :]
    for z in range(4):
        sm[z, 0:16, 0:192] = sums[:, z * 192 : z * 192 + 192]
        for i in range(4):
            sm[z, 10 + i : 11 + i, 0:192] = upsum[:, z * 768 + i * 192 : z * 768 + i * 192 + 192]
        sm[z, 16:32, 0:183] = flat[:, z * 183 : z * 183 + 183]

    def exchange(i, peer):
        return pltpu.make_async_remote_copy(src_ref=sm.at[pl.ds(4 * i, 4)], dst_ref=sm_got.at[i], send_sem=ssend.at[3 + i], recv_sem=srecv.at[3 + i], device_id=peer, device_id_type=MESH)

    swaps = [exchange(i, peer) for i, peer in enumerate((p.twin, p.x, p.y))]
    for i in range(3):
        swaps[i].start()
        advance(85 + i)
        swaps[i].wait_recv()
        sm[4 * i + 4 : 4 * i + 8] = sm[4 * i : 4 * i + 4] + sm_got[i]
    last = [pltpu.make_async_remote_copy(src_ref=sm.at[12 + (p.z + d) % 4], dst_ref=sm_piece.at[d - 1], send_sem=ssend.at[5 + d], recv_sem=srecv.at[5 + d], device_id=p.up(d), device_id_type=MESH) for d in (1, 2, 3)]
    for s in last:
        s.start()
    advance(88)
    for s in last:
        s.wait_recv()
    sm_out[...] = sm[12 + p.z] + sm_piece[0] + sm_piece[1] + sm_piece[2]
    advance(1000)
    for r in red:
        r.finish()
    lo_copy.wait()
    tg_copy.wait()
    for s in smalls + swaps + last:
        s.wait_send()
    for r in red:
        r.drain()


GATHER_PLAN = ((5, 8, 10, 13), (8.2, 11, 13.2, 16), (11.2, 14, 17, 20), (14.2, 18, 20.2, 23), (24, 30, 35, 38), (36, 44, 49, 52))
BEGIN_PLAN = (5, 9)
REDUCE_PLAN = ((15, 17, 19, 30, 37, 50, 53, 56), (28, 30, 32, 45, 52, 65, 68, 71), (35, 35.5, 36, 47, 50.5, 56, 58, 61),
               (46, 47, 48, 52.5, 56.5, 62, 65, 68), (57, 58, 59, 63, 66, 71, 74, 77), (68, 69, 70, 74, 77, 82, 85, 88))


def layer(tok, ups, index, mask, table, up_bias, vectors, qkv_s, out_s, up_s, down_s):
    n = tok.shape[0]
    shards = (qkv_s, out_s, up_s, down_s)

    def vm(shape, dtype=BF):
        return pltpu.VMEM(shape, dtype)

    row3, bufs = (n, SP, D), []
    for i, s in enumerate((down_s, up_s, out_s, out_s, out_s, out_s)):
        rows, h = s.shape[0], s.shape[1] // 2
        bufs += [vm((4, rows, h))] * (i > 1) + [vm((2, 4, rows // 4, h)), vm((4, rows // 4, h)), vm((3, rows // 4, h))]
    dma = pltpu.SemaphoreType.DMA
    scratch = [vm((4,) + s.shape) for s in (out_s, out_s, out_s, out_s, up_s, down_s)] + [vm((n, SP, FF)), vm((n, SP, FF)), vm(row3, F32), vm(row3, F32), vm(row3, F32),
               vm(row3), vm(row3), vm((n, KP, D)), vm((n, KP, D)), vm(row3), vm(row3), vm(row3), vm(row3), vm((n, HEADS, SP, KP)),
               vm((16, D), F32), vm((1, FF), F32), vm((16, D), F32), vm((4, 32, D)), vm((32, D)), vm((32, D), F32), vm((SP, KP), jnp.int32), vm((8, KP), F32),
               vm((16, D), F32), vm((1, FF), F32), vm((96, 128), F32), vm((16, 32, 256), F32), vm((3, 4, 32, 256), F32), vm((3, 32, 256), F32)]
    return pl.pallas_call(
        layer_kernel,
        out_shape=(S(row3, BF), S(row3, F32), S((32, 256), F32)) + (S((3, qkv_s.shape[0], D), BF),) + tuple(S(s.shape, BF) for s in shards[1:]),
        in_specs=[VMEM] * 16 + [ANY] * 4, out_specs=(ANY, ANY, VMEM, ANY, ANY, ANY, ANY),
        scratch_shapes=scratch + bufs + [dma((6, 3, 8)), dma((6, 3, 8)), dma((6, 18)), dma((6, 18)), dma((14,)), dma((9,)), dma((9,)), dma((3, 3)), pltpu.SemaphoreType.REGULAR],
        compiler_params=params(collective_id=0, has_side_effects=True), name="layer")(tok, ups, index, mask, table, up_bias, *vectors, *shards)


def finish_kernel(sm, rq, ro, ru, rd, dq, do, du, dd, gub, tab, *vectors):
    for g in range(3):
        for j in range(3):
            dq[:, j * D + g * 256 : j * D + g * 256 + 256] = rq[g, :, j * 256 : j * 256 + 256].astype(F32)
    do[...] = ro[...].astype(F32)
    du[...] = ru[...].astype(F32)
    dd[...] = rd[...].astype(F32)
    for i, v in enumerate(vectors):
        v[...] = sm[i, :192]
    gub[...] = sm[10:14, :192]
    tab[...] = sm[16:28, :183]


def finish(sm, rq, ro, ru, rd):
    outs = (S((192, 3 * D), F32), S(ro.shape, F32), S(ru.shape, F32), S(rd.shape, F32), S((4, 192), F32), S((HEADS, 183), F32)) + (S((192,), F32),) * 10
    return pl.pallas_call(finish_kernel, out_shape=outs, in_specs=[VMEM] * 5, out_specs=(VMEM,) * 16, compiler_params=params(), name="finish")(sm, rq, ro, ru, rd)


def wide_body(tokens, first_gain, first_shift, qkv_weight, query_bias, value_bias, bias_table, bias_index, out_weight, out_bias, first_scale,
              second_gain, second_shift, up_weight, up_bias, down_weight, down_bias, second_scale, patch_mask, upstream):
    n = tokens.shape[0]

    def whole(v):
        return lax.all_gather(v, "fsdp", axis=0, tiled=True)

    vectors = (first_gain, first_shift, query_bias, value_bias, out_bias, first_scale, second_gain, second_shift, down_bias, second_scale)
    vec = jnp.pad(lax.all_gather(jnp.stack(vectors), "fsdp", axis=1, tiled=True).astype(F32), ((0, 6), (0, 0)))
    upb = whole(up_bias).astype(F32).reshape(1, FF)
    table = jnp.pad(whole(bias_table).T.astype(F32), ((0, 4), (0, 768 - RELS)))
    qkv, outw, upw, downw = whole(qkv_weight), whole(out_weight), whole(up_weight), whole(down_weight)
    index = pad_index(bias_index)
    mask = jnp.pad(patch_mask.astype(F32), ((0, 8 - n), (0, KP - SEQ)))
    norm_one, relative = front(tokens, vec, table, index)
    q, k, v, attend, context = attention(norm_one, qkv, vec, relative)
    layer_out, dout, dup, ddown, gctx, gres, small_mlp, small_up = mlp(tokens, context, outw, upw, downw, vec, upb, mask, upstream)
    tgrad, dqkv, small, tab = back(tokens, norm_one, qkv, vec, index, q, k, v, attend, gctx, gres)
    tab = tab.reshape(HEADS, 8, 128)[:, :6].reshape(HEADS, 768)[:, :RELS].T

    def summed(g):
        part = lax.psum_scatter(g.astype(BF), "fsdp", scatter_dimension=0, tiled=True)
        return lax.psum(part.astype(F32), "dp")

    rows = lax.psum(lax.psum_scatter(jnp.concatenate([small[2:4], small[0:2], small_mlp[::-1][2:]]), "fsdp", scatter_dimension=1, tiled=True), "dp")
    g1, s1, qb, vb, ob, sc1, s2, g2, db, sc2 = rows
    return (layer_out, tgrad, g1, s1, summed(dqkv), qb, vb, summed(tab), summed(dout), ob, sc1, g2, s2, summed(dup), summed(small_up.reshape(FF)), summed(ddown), db, sc2)


def body(wide, tokens, first_gain, first_shift, qkv_weight, query_bias, value_bias, bias_table, bias_index, out_weight, out_bias, first_scale,
         second_gain, second_shift, up_weight, up_bias, down_weight, down_bias, second_scale, patch_mask, upstream):
    if wide:
        return wide_body(tokens, first_gain, first_shift, qkv_weight, query_bias, value_bias, bias_table, bias_index, out_weight, out_bias, first_scale,
                         second_gain, second_shift, up_weight, up_bias, down_weight, down_bias, second_scale, patch_mask, upstream)
    n = tokens.shape[0]
    vectors = (first_gain, first_shift, query_bias, value_bias, out_bias, first_scale, second_gain, second_shift, down_bias, second_scale)
    lo, tg, sm, rqkv, rout, rup, rdown = layer(tokens, upstream, bias_index, patch_mask, bias_table.T, up_bias, vectors,
                                               qkv_weight, out_weight, up_weight, down_weight)
    layer_out, tgrad = lo[:, :SEQ], tg[:, :SEQ]
    dq, do, du, dd, gub, gtab, g1, s1, qb, vb, ob, sc1, g2, s2, db, sc2 = finish(sm, rqkv, rout, rup, rdown)
    return (layer_out, tgrad, g1, s1, dq, qb, vb, gtab.T, do, ob, sc1, g2, s2, du, gub.reshape(FF // 4), dd, db, sc2)


def solution(mesh):
    vector, matrix, batch = P("fsdp"), P("fsdp", None), P(("dp", "fsdp"), None, None)
    in_specs = (batch, vector, vector, matrix, vector, vector, matrix, P(), matrix, vector, vector, vector, vector, matrix, vector, matrix, vector, vector,
                P(("dp", "fsdp"), None), batch)
    out_specs = (batch, batch, vector, vector, matrix, vector, vector, matrix, matrix, vector, vector, vector, vector, matrix, vector, matrix, vector, vector)
    wide = mesh.shape["dp"] != 8 or mesh.shape["fsdp"] != 4
    return jax.shard_map(functools.partial(body, wide), mesh=mesh, in_specs=in_specs, out_specs=out_specs, check_vma=False)
```

```python
import functools
import jax
import jax.numpy as jnp
from jax import lax
from jax.experimental import pallas as pl
from jax.experimental.pallas import tpu as pltpu
from jax.sharding import PartitionSpec as P

D = 768
HEADS = 12
HEAD_DIM = 64
FF = 3072
SEQ = 197
RELS = 732
SP = 208
KP = 256
HALF = SP * KP
EPS = 1e-06
BF = jnp.bfloat16
F32 = jnp.float32
VMEM = pl.BlockSpec(memory_space=pltpu.VMEM)
ANY = pl.BlockSpec(memory_space=pl.ANY)
LIMIT = 63 * 2**20


def dot(a, b):
    return lax.dot_general(a, b, (((1,), (0,)), ((), ())), preferred_element_type=F32)


def dot_nt(a, b):
    return lax.dot_general(a, b, (((1,), (1,)), ((), ())), preferred_element_type=F32)


def dot_tn(a, b):
    return lax.dot_general(a, b, (((0,), (0,)), ((), ())), preferred_element_type=F32)


def rowmean(v):
    return jnp.sum(v, axis=-1, keepdims=True) * (1.0 / D)


def colsum(v):
    return jnp.sum(v, axis=0, keepdims=True)


def xhat_of(v):
    centred = v - rowmean(v)
    rstd = lax.rsqrt(rowmean(centred * centred) + EPS)
    return centred * rstd, rstd


def pad_rows(v):
    return jnp.concatenate([v, jnp.zeros((SP - SEQ, v.shape[1]), v.dtype)], axis=0)


GAIN1, SHIFT1, QBIAS, VBIAS, OBIAS, SCALE1, GAIN2, SHIFT2, DBIAS, SCALE2 = range(10)


def front_kernel(tok, vec, table, index, norm_one, relative):
    images = tok.shape[0]
    gain, shift = vec[GAIN1 : GAIN1 + 1, :], vec[SHIFT1 : SHIFT1 + 1, :]
    for b in range(images):
        xhat, _ = xhat_of(pad_rows(tok[b].astype(F32)))
        norm_one[b] = (xhat * gain + shift).astype(BF)
    lookup(table, index, [relative.at[h] for h in range(HEADS)])


def lookup(table, index, relative):
    lanes = lax.broadcasted_iota(jnp.int32, (16, 128), 1)

    def rows(r, carry):
        at = pl.ds(pl.multiple_of(r * 16, 16), 16)
        for half in range(2):
            idx = index[at, half * 128 : half * 128 + 128]
            low = idx & 127
            high = idx >> 7
            for h in range(HEADS):
                out = jnp.zeros((16, 128), F32)
                for c in range(6):
                    part = jnp.broadcast_to(table[h : h + 1, c * 128 : c * 128 + 128], (16, 128))
                    got = jnp.take_along_axis(part, low, axis=1, mode="promise_in_bounds")
                    out = jnp.where(high == c, got, out)
                if half == 1:
                    out = jnp.where(lanes < SEQ - 128, out, -1e30)
                relative[h][at, half * 128 : half * 128 + 128] = out.astype(BF)
        return carry

    lax.fori_loop(0, SP // 16, rows, 0)


def lane_masks(rows):
    lane = lax.broadcasted_iota(jnp.int32, (rows, 128), 1)
    return lane < HEAD_DIM


def split_heads(v, first):
    zero = jnp.zeros_like(v)
    return jnp.where(first, v, zero), jnp.where(first, zero, v)


def project(norm_one, qkv, vec, q, k, v):
    images = norm_one.shape[0]
    k[:, SP:, :] = jnp.zeros((images, KP - SP, D), BF)
    v[:, SP:, :] = jnp.zeros((images, KP - SP, D), BF)

    def chunk(i, carry):
        at = pl.ds(pl.multiple_of(i * 256, 256), 256)
        rows = norm_one[...].reshape(images * SP, D)
        pq = dot(rows, qkv[:, at])
        q[:, :, at] = ((pq + vec[QBIAS : QBIAS + 1, at]) * 0.125).astype(BF).reshape(images, SP, 256)
        pk = dot(rows, qkv[:, pl.ds(pl.multiple_of(D + i * 256, 256), 256)])
        k[:, :SP, at] = pk.astype(BF).reshape(images, SP, 256)
        pv = dot(rows, qkv[:, pl.ds(pl.multiple_of(2 * D + i * 256, 256), 256)])
        v[:, :SP, at] = (pv + vec[VBIAS : VBIAS + 1, at]).astype(BF).reshape(images, SP, 256)
        return carry

    lax.fori_loop(0, D // 256, chunk, 0)


def attend_pair(b, hp, at, q, k, v, relative, attend, context):
    first = lane_masks(KP)
    q2 = q[b, :, at]
    ks = split_heads(k[b, :, at], first)
    vs = split_heads(v[b, :, at], first)
    probs = []
    for e in range(2):
        h = 2 * hp + e
        s = dot_nt(q2, ks[e]) + relative[h][...].astype(F32)
        s = jnp.exp(s - jnp.max(s, axis=-1, keepdims=True))
        p = (s * (1.0 / jnp.sum(s, axis=-1, keepdims=True))).astype(BF)
        attend[b, h] = p
        probs.append(p)
    context[b, :, at] = (dot(probs[0], vs[0]) + dot(probs[1], vs[1])).astype(BF)


def attention_kernel(norm_one, qkv, vec, relative, q, k, v, attend, context):
    images = norm_one.shape[0]
    relative = [relative.at[h] for h in range(HEADS)]
    project(norm_one, qkv, vec, q, k, v)

    def image(b, carry):
        for hp in range(HEADS // 2):
            attend_pair(b, hp, slice(hp * 128, hp * 128 + 128), q, k, v, relative, attend, context)
        return carry

    lax.fori_loop(0, images, image, 0)


def gelu_both(v):
    cdf = 0.5 * (1.0 + lax.erf(v * 0.7071067811865476))
    pdf = jnp.exp(v * v * -0.5) * 0.3989422804014327
    return v * cdf, cdf + v * pdf


def mlp_kernel(tok, ctx, out_hbm, up_hbm, down_hbm, vec, upb, mask, ups,
               layer_out, dout, dup, ddown, gctx, gres, small, small_up,
               outw, upw, downw, hid, att, n2, act, slope, acc, gd, gy_s, sems):
    images = tok.shape[0]
    R = images * SP
    loads = [pltpu.make_async_copy(s, d, sems.at[i]) for i, (s, d) in enumerate(
        ((out_hbm, outw), (up_hbm, upw), (down_hbm, downw)))]
    for l in loads:
        l.start()
    obias, scale1 = vec[OBIAS : OBIAS + 1, :], vec[SCALE1 : SCALE1 + 1, :]
    gain2, shift2 = vec[GAIN2 : GAIN2 + 1, :], vec[SHIFT2 : SHIFT2 + 1, :]
    dbias, scale2 = vec[DBIAS : DBIAS + 1, :], vec[SCALE2 : SCALE2 + 1, :]
    maskt = jnp.transpose(mask[...], (1, 0))
    loads[0].wait()
    for b in range(images):
        attn = dot(ctx[b], outw[...]) + obias
        att[b] = attn
        h = pad_rows(tok[b].astype(F32)) + scale1 * attn
        hid[b] = h
        xhat, _ = xhat_of(h)
        n2[b] = (xhat * gain2 + shift2).astype(BF)
    loads[1].wait()
    loads[2].wait()
    acc[...] = jnp.zeros_like(acc)
    W = 256

    def forward(f, carry):
        at = pl.ds(pl.multiple_of(f * W, W), W)
        for b in range(images):
            u = dot(n2[b], upw[:, at]) + upb[:, at]
            g, s = gelu_both(u)
            g = g.astype(BF)
            act[b, :, at] = g
            slope[b, :, at] = s.astype(BF)
            acc[b] += dot(g, downw[at, :])
        return carry

    lax.fori_loop(0, FF // W, forward, 0)
    sums = [jnp.zeros((1, D), F32) for _ in range(6)]
    for b in range(images):
        down = acc[b] + dbias
        layer_out[b] = (hid[b] + scale2 * down).astype(BF)[:SEQ]
        gy = pad_rows(ups[b].astype(F32)) * maskt[:SP, b : b + 1]
        gy_s[b] = gy.astype(BF)
        sums[0] += colsum(gy * down)
        full = gy * scale2
        sums[1] += colsum(full)
        gd[b] = full.astype(BF)
    acc[...] = jnp.zeros_like(acc)

    def backward(f, carry):
        at = pl.ds(pl.multiple_of(f * W, W), W)
        total = jnp.zeros((1, W), F32)
        lows = []
        for b in range(images):
            gg = dot_nt(gd[b], downw[at, :]) * slope[b, :, at].astype(F32)
            total += colsum(gg)
            low = gg.astype(BF)
            lows.append(low)
            acc[b] += dot_nt(low, upw[:, at])
        small_up[:, at] = total
        low = jnp.concatenate(lows, axis=0)
        dup[:, at] = dot_tn(n2[...].reshape(R, D), low).astype(BF)
        ddown[at, :] = dot_tn(act[:, :, at].reshape(R, W), gd[...].reshape(R, D)).astype(BF)
        return carry

    lax.fori_loop(0, FF // W, backward, 0)
    for b in range(images):
        xhat, rstd = xhat_of(hid[b])
        g = acc[b]
        sums[2] += colsum(g * xhat)
        sums[3] += colsum(g)
        gg = g * gain2
        gh = (gg - rowmean(gg) - xhat * rowmean(gg * xhat)) * rstd
        res = gy_s[b].astype(F32) + gh
        gres[b] = res
        sums[4] += colsum(res * att[b])
        full = res * scale1
        sums[5] += colsum(full)
        n2[b] = full.astype(BF)
    dout[...] = dot_tn(ctx[...].reshape(R, D), n2[...].reshape(R, D)).astype(BF)
    for b in range(images):
        gctx[b] = dot_nt(n2[b], outw[...]).astype(BF)
    small[...] = jnp.concatenate(sums + [jnp.zeros((2, D), F32)], axis=0)


def attend_back(b, hp, at, q, k, v, attend, gctx, gtab, gq, gk, gv, qsum, vsum):
    first = lane_masks(KP)
    firsts = first[:SP]
    v2 = split_heads(v[b, :, at], first)
    k2 = split_heads(k[b, :, at], first)
    q2 = split_heads(q[b, :, at], firsts)
    g2 = gctx[b, :, at]
    gs2 = split_heads(g2, firsts)
    dq = jnp.zeros((SP, 128), F32)
    dk = jnp.zeros((KP, 128), F32)
    dv = jnp.zeros((KP, 128), F32)
    for e in range(2):
        h = 2 * hp + e
        a = attend[b, h]
        af = a.astype(F32)
        ga = dot_nt(g2, v2[e])
        w = af * ga
        inner = jnp.sum(w, axis=-1, keepdims=True)
        gs = w - af * inner
        gtab[h][...] += gs
        low = gs.astype(BF)
        dq += dot(low, k2[e])
        dk += dot_tn(low, q2[e])
        dv += dot_tn(a, gs2[e])
    dq = dq * 0.125
    qsum[:, at] += colsum(dq)
    vsum[:, at] += colsum(dv)
    gq[b, :, at] = dq.astype(BF)
    gk[b, :, at] = dk[:SP].astype(BF)
    gv[b, :, at] = dv[:SP].astype(BF)


def table_rows(gtab, index, total, start, stop):
    ids = lax.broadcasted_iota(jnp.int32, (128, KP), 0).astype(F32).astype(BF)
    ones, zeros = jnp.ones((128, KP), BF), jnp.zeros((128, KP), BF)
    highs = lax.broadcasted_iota(jnp.int32, (8, KP), 0)

    def block(i, acc):
        idx = index[pl.ds(pl.multiple_of(i * 8, 8), 8), :]
        lows = (idx & 127).astype(F32)
        for r in range(8):
            hot = jnp.where(ids == lows[r : r + 1, :].astype(BF), ones, zeros)
            mask = highs == (idx[r : r + 1, :] >> 7)
            g = jnp.concatenate([jnp.where(mask, jnp.broadcast_to(t[pl.ds(i * 8 + r, 1), :], (8, KP)), 0.0) for t in gtab], axis=0)
            g1 = g.astype(BF)
            g2 = (g - g1.astype(F32)).astype(BF)
            acc = acc + dot_nt(jnp.concatenate([g1, g2], axis=0), hot)
        return acc

    return lax.fori_loop(start, stop, block, total)


def table_back(gtab, index, out):
    total = table_rows(gtab, index, jnp.zeros((192, 128), F32), 0, SP // 8)
    out[...] = total[:96] + total[96:]


def back_kernel(tok, norm_one, qkv_hbm, vec, index, q, k, v, attend, gctx, gres,
                tgrad, dqkv, small, tab, gtab, gqkv, qkv, sem):
    images = tok.shape[0]
    R = images * SP
    load = pltpu.make_async_copy(qkv_hbm, qkv, sem)
    load.start()
    gtab[...] = jnp.zeros_like(gtab)
    gtab = [gtab.at[h] for h in range(HEADS)]
    small[...] = jnp.zeros_like(small)
    gq, gk, gv = (gqkv.at[:, :, i * D : (i + 1) * D] for i in range(3))
    qsum, vsum = small.at[0:1, :], small.at[1:2, :]

    for hp in range(HEADS // 2):

        def one(b, carry, hp=hp):
            attend_back(b, hp, slice(hp * 128, hp * 128 + 128), q, k, v, attend, gctx, gtab, gq, gk, gv, qsum, vsum)
            return carry

        lax.fori_loop(0, images, one, 0)
    table_back(gtab, index, tab)

    def chunk(i, carry):
        at = pl.ds(pl.multiple_of(i * 256, 256), 256)
        dqkv[:, at] = dot_tn(norm_one[...].reshape(R, D), gqkv[:, :, at].reshape(R, 256)).astype(BF)
        return carry

    lax.fori_loop(0, 3 * D // 256, chunk, 0)
    load.wait()
    gain = vec[GAIN1 : GAIN1 + 1, :]
    for b in range(images):
        xhat, rstd = xhat_of(pad_rows(tok[b].astype(F32)))
        g = dot_nt(gqkv[b], qkv[...])
        small[2:3, :] += colsum(g * xhat)
        small[3:4, :] += colsum(g)
        gg = g * gain
        gi = (gg - rowmean(gg) - xhat * rowmean(gg * xhat)) * rstd
        tgrad[b] = (gres[b] + gi)[:SEQ]


def params(**kw):
    return pltpu.CompilerParams(vmem_limit_bytes=LIMIT, **kw)


def S(shape, dtype):
    return jax.ShapeDtypeStruct(shape, dtype)


def front(tok, vec, table, index):
    n = tok.shape[0]
    return pl.pallas_call(front_kernel, out_shape=(S((n, SP, D), BF), S((HEADS, SP, KP), BF)),
                          in_specs=[VMEM] * 4, out_specs=(VMEM, VMEM), compiler_params=params(), name="front")(tok, vec, table, index)


def attention(norm_one, qkv, vec, relative):
    n = norm_one.shape[0]
    return pl.pallas_call(attention_kernel,
                          out_shape=(S((n, SP, D), BF), S((n, KP, D), BF), S((n, KP, D), BF), S((n, HEADS, SP, KP), BF), S((n, SP, D), BF)),
                          in_specs=[VMEM] * 4, out_specs=(VMEM,) * 5, compiler_params=params(), name="attention")(norm_one, qkv, vec, relative)


def mlp(tok, ctx, outw, upw, downw, vec, upb, mask, ups):
    n = tok.shape[0]
    return pl.pallas_call(
        mlp_kernel,
        out_shape=(S((n, SEQ, D), BF), S((D, D), BF), S((D, FF), BF), S((FF, D), BF), S((n, SP, D), BF), S((n, SP, D), F32), S((8, D), F32), S((1, FF), F32)),
        in_specs=[VMEM, VMEM, ANY, ANY, ANY, VMEM, VMEM, VMEM, VMEM], out_specs=(VMEM,) * 8,
        scratch_shapes=[pltpu.VMEM((D, D), BF), pltpu.VMEM((D, FF), BF), pltpu.VMEM((FF, D), BF),
                        pltpu.VMEM((n, SP, D), F32), pltpu.VMEM((n, SP, D), F32), pltpu.VMEM((n, SP, D), BF),
                        pltpu.VMEM((n, SP, FF), BF), pltpu.VMEM((n, SP, FF), BF), pltpu.VMEM((n, SP, D), F32),
                        pltpu.VMEM((n, SP, D), BF), pltpu.VMEM((n, SP, D), BF), pltpu.SemaphoreType.DMA((3,))],
        compiler_params=params(), name="mlp")(tok, ctx, outw, upw, downw, vec, upb, mask, ups)


def back(tok, norm_one, qkv, vec, index, q, k, v, attend, gctx, gres):
    n = tok.shape[0]
    return pl.pallas_call(
        back_kernel,
        out_shape=(S((n, SEQ, D), F32), S((D, 3 * D), BF), S((8, D), F32), S((96, 128), F32)),
        in_specs=[VMEM, VMEM, ANY] + [VMEM] * 8, out_specs=(VMEM,) * 4,
        scratch_shapes=[pltpu.VMEM((16, SP, KP), F32), pltpu.VMEM((n, SP, 3 * D), BF), pltpu.VMEM((D, 3 * D), BF), pltpu.SemaphoreType.DMA(())],
        compiler_params=params(), name="back")(tok, norm_one, qkv, vec, index, q, k, v, attend, gctx, gres)


def pad_index(bias_index):
    return jnp.pad(bias_index, ((0, SP - SEQ), (0, KP - SEQ)))
MESH = pl.DeviceIdType.MESH


class Place:
    def __init__(self):
        dp, z = lax.axis_index("dp"), lax.axis_index("fsdp")
        y, x, c = dp // 4, (dp // 2) % 2, dp % 2
        xn, yn = dp + 2 - 4 * x, dp + 4 - 8 * y
        q = dp // 2
        qx, qy = q + 1 - 2 * x, q + 2 - 4 * y
        self.dp, self.z, self.c, self.q = dp, z, c, q
        self.near = (xn * (1 - c) + yn * c, z)
        self.far = (yn * (1 - c) + xn * c, z)
        self.x, self.y = (xn, z), (yn, z)
        self.twin = (dp + 1 - 2 * c, z)
        self.q_near = qx * (1 - c) + qy * c
        self.q_far = qy * (1 - c) + qx * c
        self.q_both = 3 - q

    def up(self, d):
        return (self.dp, (self.z + d) % 4)

    def beside(self, i):
        return ((self.dp + i) % 8, self.z)

    def barrier(self):
        sem = pltpu.get_barrier_semaphore()
        peers = [self.beside(i) for i in range(1, 8)] + [self.up(d) for d in (1, 2, 3)]
        for peer in peers:
            pl.semaphore_signal(sem, inc=1, device_id=peer, device_id_type=MESH)
        pl.semaphore_wait(sem, len(peers))


def aligned(i, size):
    return pl.ds(pl.multiple_of(i * size, size), size)


class Gather:
    def __init__(self, place, shard, full, send, recv, local):
        self.p, self.shard, self.full, self.send, self.recv, self.local = place, shard, full, send, recv, local
        self.rows, self.cols = full.shape[1] // 4, full.shape[2] // 2

    def region(self, zb, q, c):
        return self.full.at[zb, aligned(q, self.rows), aligned(c, self.cols)]

    def copy(self, d, slot, src, dst, peer):
        return pltpu.make_async_remote_copy(src_ref=src, dst_ref=dst, send_sem=self.send.at[d - 1, slot], recv_sem=self.recv.at[d - 1, slot],
                                            device_id=peer, device_id_type=MESH)

    def over_z(self, d):
        p = self.p
        if self.shard is None:
            src = self.region(p.z, p.q, p.c)
        else:
            src = self.shard.at[aligned(p.q, self.rows), aligned(p.c, self.cols)]
        return self.copy(d, 0, src, self.region(p.z, p.q, p.c), p.up(d))

    def passed(self, d, slot, q, peer):
        p = self.p
        r = self.region((p.z + 4 - d) % 4, q, p.c)
        return self.copy(d, slot, r, r, peer)

    def own(self):
        return pltpu.make_async_copy(self.shard, self.full.at[self.p.z], self.local)

    def begin(self):
        for d in (1, 2, 3):
            self.over_z(d).start()
        if self.shard is not None:
            self.own().start()

    def part(self, d, i):
        p = self.p
        slot, q, peer = ((1, p.q, p.near), (2, p.q, p.far), (4, p.q, p.twin), (3, p.q_near, p.far), (5, p.q_near, p.twin),
                         (6, p.q_far, p.twin), (7, p.q_both, p.twin))[i]
        return self.passed(d, slot, q, peer)

    def spread(self, d):
        self.over_z(d).wait_recv()
        for i in (0, 1, 2):
            self.part(d, i).start()

    def relay(self, d):
        self.part(d, 0).wait_recv()
        for i in (3, 4):
            self.part(d, i).start()

    def close(self, d):
        self.part(d, 1).wait_recv()
        self.part(d, 5).start()
        self.part(d, 3).wait_recv()
        self.part(d, 6).start()

    def finish(self):
        if self.shard is not None:
            self.own().wait()
        for d in (1, 2, 3):
            for i in (2, 4, 5, 6):
                self.part(d, i).wait_recv()

    def drain(self):
        for d in (1, 2, 3):
            self.over_z(d).wait_send()
            for i in range(7):
                self.part(d, i).wait_send()

    def steps(self):
        return [lambda d=d: self.spread(d) for d in (1, 2, 3)] + [lambda d=d: self.relay(d) for d in (1, 2, 3)] + [
            lambda d=d: self.close(d) for d in (1, 2, 3)] + [self.finish]


class Reduce:
    def __init__(self, place, grad, got, half, quarter, pieces, out, send, recv, local):
        self.p, self.grad, self.got, self.half, self.quarter, self.pieces, self.out = place, grad, got, half, quarter, pieces, out
        self.send, self.recv, self.local = send, recv, local
        self.rows, self.cols = grad.shape[1] // 4, grad.shape[2] // 2

    def copy(self, slot, src, dst, peer):
        return pltpu.make_async_remote_copy(src_ref=src, dst_ref=dst, send_sem=self.send.at[slot], recv_sem=self.recv.at[slot], device_id=peer, device_id_type=MESH)

    def twin(self, i):
        q = self.quarters()[i]
        return self.copy(14 + i, self.grad.at[:, aligned(q, self.rows), aligned(1 - self.p.c, self.cols)], self.got(q), self.p.twin)

    def quarters(self):
        p = self.p
        return (p.q_far, p.q_both, p.q, p.q_near)

    def mine(self, q):
        return self.grad.at[:, aligned(q, self.rows), aligned(self.p.c, self.cols)]

    def near(self, i):
        q = (self.p.q_near, self.p.q_both)[i]
        return self.copy(1 + i, self.mine(q), self.half.at[i], self.p.near)

    def far(self):
        return self.copy(3, self.half.at[1], self.quarter, self.p.far)

    def over_z(self, d):
        return self.copy(3 + d, self.quarter.at[(self.p.z + d) % 4], self.pieces.at[d - 1], self.p.up(d))

    def region(self, q):
        return self.out.at[aligned(q, self.rows), aligned(self.p.c, self.cols)]

    def passed(self, i):
        p = self.p
        q, peer = ((p.q, p.near), (p.q, p.far), (p.q, p.twin), (p.q_near, p.far), (p.q_near, p.twin), (p.q_far, p.twin), (p.q_both, p.twin))[i]
        src = self.quarter.at[p.z] if i < 3 else self.region(q)
        return self.copy(7 + i, src, self.region(q), peer)

    def own(self):
        return pltpu.make_async_copy(self.quarter.at[self.p.z], self.region(self.p.q), self.local)

    def begin(self):
        for i in range(4):
            self.twin(i).start()

    def add(self, dst, src):
        def one(i, carry):
            dst[i] = (dst[i].astype(F32) + src[i].astype(F32)).astype(BF)
            return carry

        lax.fori_loop(0, 4, one, 0)

    def fold(self, q):
        self.add(self.mine(q), self.got(q))

    def first_a(self):
        self.twin(0).wait_recv()
        self.fold(self.p.q_near)
        self.near(0).start()

    def first_b(self):
        self.twin(1).wait_recv()
        self.fold(self.p.q_both)
        self.near(1).start()

    def first_c(self):
        self.twin(2).wait_recv()
        self.fold(self.p.q)
        self.twin(3).wait_recv()
        self.fold(self.p.q_far)

    def second(self):
        self.near(1).wait_recv()
        self.add(self.half.at[1], self.mine(self.p.q_far))
        self.far().start()
        self.near(0).wait_recv()
        self.add(self.half.at[0], self.mine(self.p.q))

    def third(self):
        self.far().wait_recv()
        self.add(self.quarter, self.half.at[0])
        for d in (1, 2, 3):
            self.over_z(d).start()

    def fourth(self):
        for d in (1, 2, 3):
            self.over_z(d).wait_recv()
        total = self.quarter[self.p.z].astype(F32)
        for d in (1, 2, 3):
            total += self.pieces[d - 1].astype(F32)
        self.quarter[self.p.z] = total.astype(BF)
        for i in (0, 1, 2):
            self.passed(i).start()
        self.own().start()

    def fifth(self):
        self.passed(0).wait_recv()
        self.passed(3).start()
        self.passed(4).start()

    def sixth(self):
        self.passed(1).wait_recv()
        self.passed(5).start()
        self.passed(3).wait_recv()
        self.passed(6).start()

    def finish(self):
        for i in (2, 4, 5, 6):
            self.passed(i).wait_recv()
        self.own().wait()

    def drain(self):
        for i in range(4):
            self.twin(i).wait_send()
        self.near(0).wait_send()
        self.near(1).wait_send()
        self.far().wait_send()
        for d in (1, 2, 3):
            self.over_z(d).wait_send()
        for i in range(7):
            self.passed(i).wait_send()

    def steps(self):
        return [self.first_a, self.first_b, self.first_c, self.second, self.third, self.fourth, self.fifth, self.sixth]
def unstack_small(block, vec, upb, table):
    vec[...] = jnp.zeros_like(vec)
    table[...] = jnp.zeros_like(table)
    for z in range(4):
        part = block[z].astype(F32)
        vec[:, z * 192 : z * 192 + 192] = part[:16, :192]
        upb[:, z * 768 : z * 768 + 768] = part[10:11, :]
        table[:, z * 183 : z * 183 + 183] = part[16:32, :183]


def head_view(ref, h):
    return ref.at[h // 3, :, (h % 3) * 256 : (h % 3) * 256 + 256]


def layer_kernel(tok, ups, idx_in, mask_in, table_in, ub_in, v0, v1, v2, v3, v4, v5, v6, v7, v8, v9, qkv_s, out_s, up_s, down_s,
                 lo_hbm, tg_hbm, sm_out, rqkv, rout, rup, rdown,
                 qw0, qw1, qw2, outw, upw, downw, A, B, hid, att, acc, n1, q, k, v, ctx, n2, gd, lo, attend, vec, upb, table, block, small_in, small_f, index, mask,
                 sums, upsum, tab, sm, sm_got, sm_piece,
                 half0, quart0, piece0, half1, quart1, piece1, got2, half2, quart2, piece2, got3, half3, quart3, piece3,
                 got4, half4, quart4, piece4, got5, half5, quart5, piece5,
                 gsend, grecv, rsend, rrecv, local, ssend, srecv, qsem, free):
    p = Place()
    images = tok.shape[0]
    R = images * SP
    qw = (qw0, qw1, qw2)
    groups = [[pltpu.make_async_copy(qkv_s.at[:, j * D + g * 256 : j * D + g * 256 + 256], qw[g].at[p.z, :, j * 256 : j * 256 + 256], qsem.at[g, j])
               for j in range(3)] for g in range(3)]
    for group in groups:
        for c in group:
            c.start()
    small_f[...] = jnp.zeros_like(small_f)
    for i, vector in enumerate((v0, v1, v2, v3, v4, v5, v6, v7, v8, v9)):
        small_f[i, :192] = vector[...].astype(F32)
    small_f[10, :] = ub_in[...].astype(F32)
    small_f[16:28, :183] = table_in[...].astype(F32)
    small_in[...] = small_f[...].astype(BF)
    p.barrier()

    units = [(None, qw[g]) for g in range(3)] + [(out_s, outw), (up_s, upw), (down_s, downw)]
    gathers = [Gather(p, s, f, gsend.at[i], grecv.at[i], local.at[i]) for i, (s, f) in enumerate(units)]
    block[p.z] = small_in[...]
    smalls = [pltpu.make_async_remote_copy(src_ref=small_in, dst_ref=block.at[p.z], send_sem=ssend.at[d - 1], recv_sem=srecv.at[d - 1], device_id=p.up(d), device_id_type=MESH) for d in (1, 2, 3)]
    for s in smalls:
        s.start()
    for g in range(4):
        if g < 3:
            for c in groups[g]:
                c.wait()
        gathers[g].begin()
    index[...] = jnp.zeros_like(index)
    index[:SEQ, :SEQ] = idx_in[...]
    mask[...] = jnp.zeros_like(mask)
    mask[:images, :SEQ] = mask_in[...].astype(F32)
    for s in smalls:
        s.wait_recv()
    unstack_small(block, vec, upb, table)
    row = lambda i: vec[i : i + 1, :]
    todo = []

    def plan(steps, times):
        todo.extend(zip(times, steps))
        todo.sort(key=lambda e: e[0])

    def advance(now):
        while todo and todo[0][0] <= now:
            todo.pop(0)[1]()

    for g, (spread, relay, close, finish) in zip(gathers, GATHER_PLAN):
        plan(g.steps(), (spread, spread + 0.5, spread + 1, relay, relay + 0.5, relay + 1, close, close + 0.5, close + 1, finish))
    plan([gathers[4].begin, gathers[5].begin], BEGIN_PLAN)
    for b in range(images):
        xhat, _ = xhat_of(pad_rows(tok[b].astype(F32)))
        n1[b] = (xhat * row(GAIN1) + row(SHIFT1)).astype(BF)
        advance(5 + b)
    relative = [head_view(gd, h) for h in range(HEADS)]
    lookup(table, index, relative)

    k[:, SP:, :] = jnp.zeros((images, KP - SP, D), BF)
    v[:, SP:, :] = jnp.zeros((images, KP - SP, D), BF)
    for g in range(3):
        at = slice(g * 256, g * 256 + 256)
        advance(GATHER_PLAN[g][3])

        def weight(j, g=g):
            return qw[g][:, :, j * 256 : j * 256 + 256].reshape(D, 256)

        rows = n1[...].reshape(R, D)
        q[:, :, at] = ((dot(rows, weight(0)) + vec[QBIAS : QBIAS + 1, at]) * 0.125).astype(BF).reshape(images, SP, 256)
        k[:, :SP, at] = dot(rows, weight(1)).astype(BF).reshape(images, SP, 256)
        v[:, :SP, at] = (dot(rows, weight(2)) + vec[VBIAS : VBIAS + 1, at]).astype(BF).reshape(images, SP, 256)
        advance(17 + 8 * g)
        for hp in (2 * g, 2 * g + 1):

            def one(b, carry, hp=hp):
                attend_pair(b, hp, slice(hp * 128, hp * 128 + 128), q, k, v, relative, attend, ctx)
                return carry

            lax.fori_loop(0, images, one, 0)
            advance(20 + 8 * g + 3 * (hp - 2 * g))

    advance(GATHER_PLAN[3][3])
    for b in range(images):
        attn = dot(ctx[b], outw[...].reshape(D, D)) + row(OBIAS)
        att[b] = attn
        h = pad_rows(tok[b].astype(F32)) + row(SCALE1) * attn
        hid[b] = h
        xhat, _ = xhat_of(h)
        n2[b] = (xhat * row(GAIN2) + row(SHIFT2)).astype(BF)
    advance(GATHER_PLAN[4][3])
    W = 256

    def expand(f, carry):
        at = aligned(f, W)
        u = dot(n2[...].reshape(R, D), upw[:, :, at].reshape(D, W)) + upb[:, at]
        g, s = gelu_both(u)
        A[:, :, at] = g.astype(BF).reshape(images, SP, W)
        B[:, :, at] = s.astype(BF).reshape(images, SP, W)
        return carry

    for part in range(4):
        lax.fori_loop(part * 3, part * 3 + 3, expand, 0)
        advance(46 + 3 * part)
    advance(1000)
    for i in range(D // 256):
        at = slice(i * 256, i * 256 + 256)
        acc[:, :, at] = dot(A[...].reshape(R, FF), downw[:, :, at].reshape(FF, 256)).reshape(images, SP, 256)
    maskt = jnp.transpose(mask[...], (1, 0))
    sums[...] = jnp.zeros_like(sums)

    def add_sum(i, value):
        sums[i : i + 1, :] += colsum(value)

    def grad_y(b):
        return pad_rows(ups[b].astype(F32)) * maskt[:SP, b : b + 1]

    for b in range(images):
        down = acc[b] + row(DBIAS)
        lo[b] = (hid[b] + row(SCALE2) * down).astype(BF)
        gy = grad_y(b)
        add_sum(SCALE2, gy * down)
        full = gy * row(SCALE2)
        add_sum(DBIAS, full)
        gd[b] = full.astype(BF)
    lo_copy = pltpu.make_async_copy(lo, lo_hbm, local.at[12])
    lo_copy.start()

    for g in gathers:
        g.drain()

    def contract(f, carry):
        at = aligned(f, W)
        z, r = f // 3, f % 3
        rows = aligned(r, W)
        gg = dot_nt(gd[...].reshape(R, D), downw[z, rows, :]) * B[:, :, at].reshape(R, W).astype(F32)
        upsum[:, at] = colsum(gg)
        B[:, :, at] = gg.astype(BF).reshape(images, SP, W)
        downw[z, rows, :] = dot_tn(A[:, :, at].reshape(R, W), gd[...].reshape(R, D)).astype(BF)
        return carry

    lax.fori_loop(0, FF // W, contract, 0)
    pl.semaphore_signal(free, inc=1, device_id=p.twin, device_id_type=MESH)

    def got_down(q):
        return A.at[:, :192, pl.ds(pl.multiple_of(1536 + q * 384, 128), 384)]

    def got_up(q):
        return A.at[:, aligned(q, 48), :1536]

    def got_of(ref, rows):
        return lambda q: ref.at[:, aligned(q, rows), :]

    parts = ((downw, got_down, half0, quart0, piece0, rdown), (upw, got_up, half1, quart1, piece1, rup),
             (outw, got_of(got2, 48), half2, quart2, piece2, rout), (qw0, got_of(got3, 48), half3, quart3, piece3, rqkv.at[0]),
             (qw1, got_of(got4, 48), half4, quart4, piece4, rqkv.at[1]), (qw2, got_of(got5, 48), half5, quart5, piece5, rqkv.at[2]))
    red = [Reduce(p, *part, rsend.at[i], rrecv.at[i], local.at[6 + i]) for i, part in enumerate(parts)]

    def launch(i):
        red[i].begin()
        plan(red[i].steps(), REDUCE_PLAN[i])

    pl.semaphore_wait(free, 1)
    launch(0)
    for i in range(4):
        acc[:, :, i * 192 : i * 192 + 192] = dot_nt(B[...].reshape(R, FF), upw[i]).reshape(images, SP, 192)
        advance(13.5 + 1.5 * i)

    def widen(f, carry):
        at = aligned(f, W)
        upw[:, :, at] = dot_tn(n2[...].reshape(R, D), B[:, :, at].reshape(R, W)).astype(BF).reshape(4, D // 4, W)
        return carry

    for i in range(4):
        lax.fori_loop(3 * i, 3 * i + 3, widen, 0)
        advance(20 + 2 * i)
    launch(1)
    for b in range(images):
        xhat, rstd = xhat_of(hid[b])
        g = acc[b]
        add_sum(GAIN2, g * xhat)
        add_sum(SHIFT2, g)
        gg = g * row(GAIN2)
        res = grad_y(b) + (gg - rowmean(gg) - xhat * rowmean(gg * xhat)) * rstd
        hid[b] = res
        add_sum(SCALE1, res * att[b])
        full = res * row(SCALE1)
        add_sum(OBIAS, full)
        n2[b] = full.astype(BF)
        advance(27 + b)
    gctx = B.at[:, :, 3 * D :]
    for b in range(images):
        gctx[b] = dot_nt(n2[b], outw[...].reshape(D, D)).astype(BF)
    for i in range(3):
        at = slice(i * 256, i * 256 + 256)
        outw[:, :, at] = dot_tn(ctx[...].reshape(R, D), n2[:, :, at].reshape(R, 256)).astype(BF).reshape(4, D // 4, 256)
    launch(2)
    advance(33)

    acc[...] = jnp.zeros_like(acc)
    gtab = [head_view(acc, h) for h in range(HEADS)]
    gq, gk, gv = (B.at[:, :, i * D : (i + 1) * D] for i in range(3))
    qsum, vsum = sums.at[QBIAS : QBIAS + 1, :], sums.at[VBIAS : VBIAS + 1, :]
    for g in range(3):
        now = 33 + 11 * g
        for hp in (2 * g, 2 * g + 1):
            for part in range(2):

                def one(i, carry, hp=hp, part=part):
                    attend_back(part * (images // 2) + i, hp, slice(hp * 128, hp * 128 + 128), q, k, v, attend, gctx, gtab, gq, gk, gv, qsum, vsum)
                    return carry

                lax.fori_loop(0, images // 2, one, 0)
                now += 2
                advance(now)
        grads = [B.at[:, :, j * D + g * 256 : j * D + g * 256 + 256] for j in range(3)]
        term = sum(dot_nt(grads[j][...].reshape(R, 256), qw[g][:, :, j * 256 : j * 256 + 256].reshape(D, 256)) for j in range(3)).reshape(images, SP, D)
        att[...] = term if g == 0 else att[...] + term
        for j in range(3):
            qw[g][:, :, j * 256 : j * 256 + 256] = dot_tn(n1[...].reshape(R, D), grads[j][...].reshape(R, 256)).astype(BF).reshape(4, D // 4, 256)
        launch(3 + g)
        advance(now + 3)
    for b in range(images):
        xhat, rstd = xhat_of(pad_rows(tok[b].astype(F32)))
        g = att[b]
        add_sum(GAIN1, g * xhat)
        add_sum(SHIFT1, g)
        gg = g * row(GAIN1)
        att[b] = hid[b] + (gg - rowmean(gg) - xhat * rowmean(gg * xhat)) * rstd
        advance(67 + b)
    tg_copy = pltpu.make_async_copy(att, tg_hbm, local.at[13])
    tg_copy.start()
    total = jnp.zeros((192, 128), F32)
    for i in range(5):
        total = table_rows(gtab, index, total, 5 * i, 5 * i + 5)
        advance(72 + 2 * (i + 1))
    tab[...] = total[:96] + total[96:]
    sm[...] = jnp.zeros_like(sm)
    flat = table
    for h in range(HEADS):
        for c in range(6):
            flat[h : h + 1, c * 128 : c * 128 + 128] = tab[h * 8 + c : h * 8 + c + 1, :]
    for z in range(4):
        sm[z, 0:16, 0:192] = sums[:, z * 192 : z * 192 + 192]
        for i in range(3):
            sm[z, 10 + i : 11 + i, :] = upsum[:, z * 768 + i * 256 : z * 768 + i * 256 + 256]
        sm[z, 16:32, 0:183] = flat[:, z * 183 : z * 183 + 183]

    parts = [pltpu.make_async_remote_copy(src_ref=sm.at[(p.z + d) % 4], dst_ref=sm_piece.at[d - 1], send_sem=ssend.at[2 + d], recv_sem=srecv.at[2 + d], device_id=p.up(d), device_id_type=MESH) for d in (1, 2, 3)]
    for s in parts:
        s.start()
    advance(86)
    for s in parts:
        s.wait_recv()
    sm_got[p.dp] = sm[p.z] + sm_piece[0] + sm_piece[1] + sm_piece[2]
    shares = [pltpu.make_async_remote_copy(src_ref=sm_got.at[p.dp], dst_ref=sm_got.at[p.dp], send_sem=ssend.at[5 + i], recv_sem=srecv.at[5 + i], device_id=p.beside(i), device_id_type=MESH) for i in range(1, 8)]
    for s in shares:
        s.start()
    advance(90)
    for s in shares:
        s.wait_recv()
    whole_sum = sm_got[0]
    for i in range(1, 8):
        whole_sum += sm_got[i]
    sm_out[...] = whole_sum
    advance(1000)
    for r in red:
        r.finish()
    lo_copy.wait()
    tg_copy.wait()
    for s in smalls + parts + shares:
        s.wait_send()
    for r in red:
        r.drain()


GATHER_PLAN = ((5, 8, 10, 13), (8.2, 11, 13.2, 16), (11.2, 14, 17, 20), (14.2, 18, 20.2, 23), (24, 30, 35, 38), (36, 44, 49, 52))
BEGIN_PLAN = (5, 9)
REDUCE_PLAN = ((15, 17, 19, 30, 37, 50, 53, 56), (28, 30, 32, 45, 52, 65, 68, 71), (35, 35.5, 36, 47, 50.5, 56, 58, 61),
               (46, 47, 48, 52.5, 56.5, 62, 65, 68), (57, 58, 59, 63, 66, 71, 74, 77), (68, 69, 70, 74, 77, 82, 85, 88))


def layer(tok, ups, index, mask, table, up_bias, vectors, qkv_s, out_s, up_s, down_s):
    n = tok.shape[0]
    shards = (qkv_s, out_s, up_s, down_s)

    def vm(shape, dtype=BF):
        return pltpu.VMEM(shape, dtype)

    row3, bufs = (n, SP, D), []
    for i, s in enumerate((down_s, up_s, out_s, out_s, out_s, out_s)):
        rows, h = s.shape[0], s.shape[1] // 2
        bufs += [vm((4, rows, h))] * (i > 1) + [vm((2, 4, rows // 4, h)), vm((4, rows // 4, h)), vm((3, rows // 4, h))]
    dma = pltpu.SemaphoreType.DMA
    scratch = [vm((4,) + s.shape) for s in (out_s, out_s, out_s, out_s, up_s, down_s)] + [vm((n, SP, FF)), vm((n, SP, FF)), vm(row3, F32), vm(row3, F32), vm(row3, F32),
               vm(row3), vm(row3), vm((n, KP, D)), vm((n, KP, D)), vm(row3), vm(row3), vm(row3), vm(row3), vm((n, HEADS, SP, KP)),
               vm((16, D), F32), vm((1, FF), F32), vm((16, D), F32), vm((4, 32, D)), vm((32, D)), vm((32, D), F32), vm((SP, KP), jnp.int32), vm((8, KP), F32),
               vm((16, D), F32), vm((1, FF), F32), vm((96, 128), F32), vm((4, 32, 256), F32), vm((8, 32, 256), F32), vm((3, 32, 256), F32)]
    return pl.pallas_call(
        layer_kernel,
        out_shape=(S(row3, BF), S(row3, F32), S((32, 256), F32)) + (S((3, qkv_s.shape[0], D), BF),) + tuple(S(s.shape, BF) for s in shards[1:]),
        in_specs=[VMEM] * 16 + [ANY] * 4, out_specs=(ANY, ANY, VMEM, ANY, ANY, ANY, ANY),
        scratch_shapes=scratch + bufs + [dma((6, 3, 8)), dma((6, 3, 8)), dma((6, 18)), dma((6, 18)), dma((14,)), dma((13,)), dma((13,)), dma((3, 3)), pltpu.SemaphoreType.REGULAR],
        compiler_params=params(collective_id=0, has_side_effects=True), name="layer")(tok, ups, index, mask, table, up_bias, *vectors, *shards)


def finish_kernel(sm, rq, ro, ru, rd, dq, do, du, dd, gub, tab, *vectors):
    for g in range(3):
        for j in range(3):
            dq[:, j * D + g * 256 : j * D + g * 256 + 256] = rq[g, :, j * 256 : j * 256 + 256].astype(F32)
    do[...] = ro[...].astype(F32)
    du[...] = ru[...].astype(F32)
    dd[...] = rd[...].astype(F32)
    for i, v in enumerate(vectors):
        v[...] = sm[i, :192]
    gub[...] = jnp.concatenate([sm[i : i + 1, :] for i in (10, 11, 12)], axis=1)[0]
    tab[...] = sm[16:28, :183]


def finish(sm, rq, ro, ru, rd):
    outs = (S((192, 3 * D), F32), S(ro.shape, F32), S(ru.shape, F32), S(rd.shape, F32), S((FF // 4,), F32), S((HEADS, 183), F32)) + (S((192,), F32),) * 10
    return pl.pallas_call(finish_kernel, out_shape=outs, in_specs=[VMEM] * 5, out_specs=(VMEM,) * 16, compiler_params=params(), name="finish")(sm, rq, ro, ru, rd)


def wide_body(tokens, first_gain, first_shift, qkv_weight, query_bias, value_bias, bias_table, bias_index, out_weight, out_bias, first_scale,
              second_gain, second_shift, up_weight, up_bias, down_weight, down_bias, second_scale, patch_mask, upstream):
    n = tokens.shape[0]

    def whole(v):
        return lax.all_gather(v, "fsdp", axis=0, tiled=True)

    vectors = (first_gain, first_shift, query_bias, value_bias, out_bias, first_scale, second_gain, second_shift, down_bias, second_scale)
    vec = jnp.pad(lax.all_gather(jnp.stack(vectors), "fsdp", axis=1, tiled=True).astype(F32), ((0, 6), (0, 0)))
    upb = whole(up_bias).astype(F32).reshape(1, FF)
    table = jnp.pad(whole(bias_table).T.astype(F32), ((0, 4), (0, 768 - RELS)))
    qkv, outw, upw, downw = whole(qkv_weight), whole(out_weight), whole(up_weight), whole(down_weight)
    index = pad_index(bias_index)
    mask = jnp.pad(patch_mask.astype(F32), ((0, 8 - n), (0, KP - SEQ)))
    norm_one, relative = front(tokens, vec, table, index)
    q, k, v, attend, context = attention(norm_one, qkv, vec, relative)
    layer_out, dout, dup, ddown, gctx, gres, small_mlp, small_up = mlp(tokens, context, outw, upw, downw, vec, upb, mask, upstream)
    tgrad, dqkv, small, tab = back(tokens, norm_one, qkv, vec, index, q, k, v, attend, gctx, gres)
    tab = tab.reshape(HEADS, 8, 128)[:, :6].reshape(HEADS, 768)[:, :RELS].T

    def summed(g):
        part = lax.psum_scatter(g.astype(BF), "fsdp", scatter_dimension=0, tiled=True)
        return lax.psum(part.astype(F32), "dp")

    rows = lax.psum(lax.psum_scatter(jnp.concatenate([small[2:4], small[0:2], small_mlp[::-1][2:]]), "fsdp", scatter_dimension=1, tiled=True), "dp")
    g1, s1, qb, vb, ob, sc1, s2, g2, db, sc2 = rows
    return (layer_out, tgrad, g1, s1, summed(dqkv), qb, vb, summed(tab), summed(dout), ob, sc1, g2, s2, summed(dup), summed(small_up.reshape(FF)), summed(ddown), db, sc2)


def body(wide, tokens, first_gain, first_shift, qkv_weight, query_bias, value_bias, bias_table, bias_index, out_weight, out_bias, first_scale,
         second_gain, second_shift, up_weight, up_bias, down_weight, down_bias, second_scale, patch_mask, upstream):
    if wide:
        return wide_body(tokens, first_gain, first_shift, qkv_weight, query_bias, value_bias, bias_table, bias_index, out_weight, out_bias, first_scale,
                         second_gain, second_shift, up_weight, up_bias, down_weight, down_bias, second_scale, patch_mask, upstream)
    n = tokens.shape[0]
    vectors = (first_gain, first_shift, query_bias, value_bias, out_bias, first_scale, second_gain, second_shift, down_bias, second_scale)
    lo, tg, sm, rqkv, rout, rup, rdown = layer(tokens, upstream, bias_index, patch_mask, bias_table.T, up_bias, vectors,
                                               qkv_weight, out_weight, up_weight, down_weight)
    layer_out, tgrad = lo[:, :SEQ], tg[:, :SEQ]
    dq, do, du, dd, gub, gtab, g1, s1, qb, vb, ob, sc1, g2, s2, db, sc2 = finish(sm, rqkv, rout, rup, rdown)
    return (layer_out, tgrad, g1, s1, dq, qb, vb, gtab.T, do, ob, sc1, g2, s2, du, gub, dd, db, sc2)


def solution(mesh):
    vector, matrix, batch = P("fsdp"), P("fsdp", None), P(("dp", "fsdp"), None, None)
    in_specs = (batch, vector, vector, matrix, vector, vector, matrix, P(), matrix, vector, vector, vector, vector, matrix, vector, matrix, vector, vector,
                P(("dp", "fsdp"), None), batch)
    out_specs = (batch, batch, vector, vector, matrix, vector, vector, matrix, matrix, vector, vector, vector, vector, matrix, vector, matrix, vector, vector)
    wide = mesh.shape["dp"] != 8 or mesh.shape["fsdp"] != 4
    return jax.shard_map(functools.partial(body, wide), mesh=mesh, in_specs=in_specs, out_specs=out_specs, check_vma=False)
```

```python
import functools
import jax
import jax.numpy as jnp
from jax import lax
from jax.experimental import pallas as pl
from jax.experimental.pallas import tpu as pltpu
from jax.sharding import PartitionSpec as P

D = 768
HEADS = 12
HEAD_DIM = 64
FF = 3072
SEQ = 197
RELS = 732
SP = 208
KP = 256
HALF = SP * KP
EPS = 1e-06
BF = jnp.bfloat16
F32 = jnp.float32
VMEM = pl.BlockSpec(memory_space=pltpu.VMEM)
ANY = pl.BlockSpec(memory_space=pl.ANY)
LIMIT = 63 * 2**20


def dot(a, b):
    return lax.dot_general(a, b, (((1,), (0,)), ((), ())), preferred_element_type=F32)


def dot_nt(a, b):
    return lax.dot_general(a, b, (((1,), (1,)), ((), ())), preferred_element_type=F32)


def dot_tn(a, b):
    return lax.dot_general(a, b, (((0,), (0,)), ((), ())), preferred_element_type=F32)


def rowmean(v):
    return jnp.sum(v, axis=-1, keepdims=True) * (1.0 / D)


def colsum(v):
    return jnp.sum(v, axis=0, keepdims=True)


def xhat_of(v):
    centred = v - rowmean(v)
    rstd = lax.rsqrt(rowmean(centred * centred) + EPS)
    return centred * rstd, rstd


def pad_rows(v):
    return jnp.concatenate([v, jnp.zeros((SP - SEQ, v.shape[1]), v.dtype)], axis=0)


GAIN1, SHIFT1, QBIAS, VBIAS, OBIAS, SCALE1, GAIN2, SHIFT2, DBIAS, SCALE2 = range(10)


def front_kernel(tok, vec, table, index, norm_one, relative):
    images = tok.shape[0]
    gain, shift = vec[GAIN1 : GAIN1 + 1, :], vec[SHIFT1 : SHIFT1 + 1, :]
    for b in range(images):
        xhat, _ = xhat_of(pad_rows(tok[b].astype(F32)))
        norm_one[b] = (xhat * gain + shift).astype(BF)
    lookup(table, index, [relative.at[h] for h in range(HEADS)])


def lookup(table, index, relative):
    lanes = lax.broadcasted_iota(jnp.int32, (16, 128), 1)

    def rows(r, carry):
        at = pl.ds(pl.multiple_of(r * 16, 16), 16)
        for half in range(2):
            idx = index[at, half * 128 : half * 128 + 128]
            low = idx & 127
            high = idx >> 7
            for h in range(HEADS):
                out = jnp.zeros((16, 128), F32)
                for c in range(6):
                    part = jnp.broadcast_to(table[h : h + 1, c * 128 : c * 128 + 128], (16, 128))
                    got = jnp.take_along_axis(part, low, axis=1, mode="promise_in_bounds")
                    out = jnp.where(high == c, got, out)
                if half == 1:
                    out = jnp.where(lanes < SEQ - 128, out, -1e30)
                relative[h][at, half * 128 : half * 128 + 128] = out.astype(BF)
        return carry

    lax.fori_loop(0, SP // 16, rows, 0)


def lane_masks(rows):
    lane = lax.broadcasted_iota(jnp.int32, (rows, 128), 1)
    return lane < HEAD_DIM


def split_heads(v, first):
    zero = jnp.zeros_like(v)
    return jnp.where(first, v, zero), jnp.where(first, zero, v)


def project(norm_one, qkv, vec, q, k, v):
    images = norm_one.shape[0]
    k[:, SP:, :] = jnp.zeros((images, KP - SP, D), BF)
    v[:, SP:, :] = jnp.zeros((images, KP - SP, D), BF)

    def chunk(i, carry):
        at = pl.ds(pl.multiple_of(i * 256, 256), 256)
        rows = norm_one[...].reshape(images * SP, D)
        pq = dot(rows, qkv[:, at])
        q[:, :, at] = ((pq + vec[QBIAS : QBIAS + 1, at]) * 0.125).astype(BF).reshape(images, SP, 256)
        pk = dot(rows, qkv[:, pl.ds(pl.multiple_of(D + i * 256, 256), 256)])
        k[:, :SP, at] = pk.astype(BF).reshape(images, SP, 256)
        pv = dot(rows, qkv[:, pl.ds(pl.multiple_of(2 * D + i * 256, 256), 256)])
        v[:, :SP, at] = (pv + vec[VBIAS : VBIAS + 1, at]).astype(BF).reshape(images, SP, 256)
        return carry

    lax.fori_loop(0, D // 256, chunk, 0)


def attend_pair(b, hp, at, q, k, v, relative, attend, context):
    first = lane_masks(KP)
    q2 = q[b, :, at]
    ks = split_heads(k[b, :, at], first)
    vs = split_heads(v[b, :, at], first)
    probs = []
    for e in range(2):
        h = 2 * hp + e
        s = dot_nt(q2, ks[e]) + relative[h][...].astype(F32)
        s = jnp.exp(s - jnp.max(s, axis=-1, keepdims=True))
        p = (s * (1.0 / jnp.sum(s, axis=-1, keepdims=True))).astype(BF)
        attend[b, h] = p
        probs.append(p)
    context[b, :, at] = (dot(probs[0], vs[0]) + dot(probs[1], vs[1])).astype(BF)


def attention_kernel(norm_one, qkv, vec, relative, q, k, v, attend, context):
    images = norm_one.shape[0]
    relative = [relative.at[h] for h in range(HEADS)]
    project(norm_one, qkv, vec, q, k, v)

    def image(b, carry):
        for hp in range(HEADS // 2):
            attend_pair(b, hp, slice(hp * 128, hp * 128 + 128), q, k, v, relative, attend, context)
        return carry

    lax.fori_loop(0, images, image, 0)


def gelu_both(v):
    cdf = 0.5 * (1.0 + lax.erf(v * 0.7071067811865476))
    pdf = jnp.exp(v * v * -0.5) * 0.3989422804014327
    return v * cdf, cdf + v * pdf


def mlp_kernel(tok, ctx, out_hbm, up_hbm, down_hbm, vec, upb, mask, ups,
               layer_out, dout, dup, ddown, gctx, gres, small, small_up,
               outw, upw, downw, hid, att, n2, act, slope, acc, gd, gy_s, sems):
    images = tok.shape[0]
    R = images * SP
    loads = [pltpu.make_async_copy(s, d, sems.at[i]) for i, (s, d) in enumerate(
        ((out_hbm, outw), (up_hbm, upw), (down_hbm, downw)))]
    for l in loads:
        l.start()
    obias, scale1 = vec[OBIAS : OBIAS + 1, :], vec[SCALE1 : SCALE1 + 1, :]
    gain2, shift2 = vec[GAIN2 : GAIN2 + 1, :], vec[SHIFT2 : SHIFT2 + 1, :]
    dbias, scale2 = vec[DBIAS : DBIAS + 1, :], vec[SCALE2 : SCALE2 + 1, :]
    maskt = jnp.transpose(mask[...], (1, 0))
    loads[0].wait()
    for b in range(images):
        attn = dot(ctx[b], outw[...]) + obias
        att[b] = attn
        h = pad_rows(tok[b].astype(F32)) + scale1 * attn
        hid[b] = h
        xhat, _ = xhat_of(h)
        n2[b] = (xhat * gain2 + shift2).astype(BF)
    loads[1].wait()
    loads[2].wait()
    acc[...] = jnp.zeros_like(acc)
    W = 256

    def forward(f, carry):
        at = pl.ds(pl.multiple_of(f * W, W), W)
        for b in range(images):
            u = dot(n2[b], upw[:, at]) + upb[:, at]
            g, s = gelu_both(u)
            g = g.astype(BF)
            act[b, :, at] = g
            slope[b, :, at] = s.astype(BF)
            acc[b] += dot(g, downw[at, :])
        return carry

    lax.fori_loop(0, FF // W, forward, 0)
    sums = [jnp.zeros((1, D), F32) for _ in range(6)]
    for b in range(images):
        down = acc[b] + dbias
        layer_out[b] = (hid[b] + scale2 * down).astype(BF)[:SEQ]
        gy = pad_rows(ups[b].astype(F32)) * maskt[:SP, b : b + 1]
        gy_s[b] = gy.astype(BF)
        sums[0] += colsum(gy * down)
        full = gy * scale2
        sums[1] += colsum(full)
        gd[b] = full.astype(BF)
    acc[...] = jnp.zeros_like(acc)

    def backward(f, carry):
        at = pl.ds(pl.multiple_of(f * W, W), W)
        total = jnp.zeros((1, W), F32)
        lows = []
        for b in range(images):
            gg = dot_nt(gd[b], downw[at, :]) * slope[b, :, at].astype(F32)
            total += colsum(gg)
            low = gg.astype(BF)
            lows.append(low)
            acc[b] += dot_nt(low, upw[:, at])
        small_up[:, at] = total
        low = jnp.concatenate(lows, axis=0)
        dup[:, at] = dot_tn(n2[...].reshape(R, D), low).astype(BF)
        ddown[at, :] = dot_tn(act[:, :, at].reshape(R, W), gd[...].reshape(R, D)).astype(BF)
        return carry

    lax.fori_loop(0, FF // W, backward, 0)
    for b in range(images):
        xhat, rstd = xhat_of(hid[b])
        g = acc[b]
        sums[2] += colsum(g * xhat)
        sums[3] += colsum(g)
        gg = g * gain2
        gh = (gg - rowmean(gg) - xhat * rowmean(gg * xhat)) * rstd
        res = gy_s[b].astype(F32) + gh
        gres[b] = res
        sums[4] += colsum(res * att[b])
        full = res * scale1
        sums[5] += colsum(full)
        n2[b] = full.astype(BF)
    dout[...] = dot_tn(ctx[...].reshape(R, D), n2[...].reshape(R, D)).astype(BF)
    for b in range(images):
        gctx[b] = dot_nt(n2[b], outw[...]).astype(BF)
    small[...] = jnp.concatenate(sums + [jnp.zeros((2, D), F32)], axis=0)


def attend_back(b, hp, at, q, k, v, attend, gctx, gtab, gq, gk, gv, qsum, vsum):
    first = lane_masks(KP)
    firsts = first[:SP]
    v2 = split_heads(v[b, :, at], first)
    k2 = split_heads(k[b, :, at], first)
    q2 = split_heads(q[b, :, at], firsts)
    g2 = gctx[b, :, at]
    gs2 = split_heads(g2, firsts)
    dq = jnp.zeros((SP, 128), F32)
    dk = jnp.zeros((KP, 128), F32)
    dv = jnp.zeros((KP, 128), F32)
    for e in range(2):
        h = 2 * hp + e
        a = attend[b, h]
        af = a.astype(F32)
        ga = dot_nt(g2, v2[e])
        w = af * ga
        inner = jnp.sum(w, axis=-1, keepdims=True)
        gs = w - af * inner
        gtab[h][...] += gs
        low = gs.astype(BF)
        dq += dot(low, k2[e])
        dk += dot_tn(low, q2[e])
        dv += dot_tn(a, gs2[e])
    dq = dq * 0.125
    qsum[:, at] += colsum(dq)
    vsum[:, at] += colsum(dv)
    gq[b, :, at] = dq.astype(BF)
    gk[b, :, at] = dk[:SP].astype(BF)
    gv[b, :, at] = dv[:SP].astype(BF)


def table_rows(gtab, index, total, start, stop):
    ids = lax.broadcasted_iota(jnp.int32, (128, KP), 0).astype(F32).astype(BF)
    ones, zeros = jnp.ones((128, KP), BF), jnp.zeros((128, KP), BF)
    highs = lax.broadcasted_iota(jnp.int32, (8, KP), 0)

    def block(i, acc):
        idx = index[pl.ds(pl.multiple_of(i * 8, 8), 8), :]
        lows = (idx & 127).astype(F32)
        for r in range(8):
            hot = jnp.where(ids == lows[r : r + 1, :].astype(BF), ones, zeros)
            mask = highs == (idx[r : r + 1, :] >> 7)
            g = jnp.concatenate([jnp.where(mask, jnp.broadcast_to(t[pl.ds(i * 8 + r, 1), :], (8, KP)), 0.0) for t in gtab], axis=0)
            g1 = g.astype(BF)
            g2 = (g - g1.astype(F32)).astype(BF)
            acc = acc + dot_nt(jnp.concatenate([g1, g2], axis=0), hot)
        return acc

    return lax.fori_loop(start, stop, block, total)


def table_back(gtab, index, out):
    total = table_rows(gtab, index, jnp.zeros((192, 128), F32), 0, SP // 8)
    out[...] = total[:96] + total[96:]


def back_kernel(tok, norm_one, qkv_hbm, vec, index, q, k, v, attend, gctx, gres,
                tgrad, dqkv, small, tab, gtab, gqkv, qkv, sem):
    images = tok.shape[0]
    R = images * SP
    load = pltpu.make_async_copy(qkv_hbm, qkv, sem)
    load.start()
    gtab[...] = jnp.zeros_like(gtab)
    gtab = [gtab.at[h] for h in range(HEADS)]
    small[...] = jnp.zeros_like(small)
    gq, gk, gv = (gqkv.at[:, :, i * D : (i + 1) * D] for i in range(3))
    qsum, vsum = small.at[0:1, :], small.at[1:2, :]

    for hp in range(HEADS // 2):

        def one(b, carry, hp=hp):
            attend_back(b, hp, slice(hp * 128, hp * 128 + 128), q, k, v, attend, gctx, gtab, gq, gk, gv, qsum, vsum)
            return carry

        lax.fori_loop(0, images, one, 0)
    table_back(gtab, index, tab)

    def chunk(i, carry):
        at = pl.ds(pl.multiple_of(i * 256, 256), 256)
        dqkv[:, at] = dot_tn(norm_one[...].reshape(R, D), gqkv[:, :, at].reshape(R, 256)).astype(BF)
        return carry

    lax.fori_loop(0, 3 * D // 256, chunk, 0)
    load.wait()
    gain = vec[GAIN1 : GAIN1 + 1, :]
    for b in range(images):
        xhat, rstd = xhat_of(pad_rows(tok[b].astype(F32)))
        g = dot_nt(gqkv[b], qkv[...])
        small[2:3, :] += colsum(g * xhat)
        small[3:4, :] += colsum(g)
        gg = g * gain
        gi = (gg - rowmean(gg) - xhat * rowmean(gg * xhat)) * rstd
        tgrad[b] = (gres[b] + gi)[:SEQ]


def params(**kw):
    return pltpu.CompilerParams(vmem_limit_bytes=LIMIT, **kw)


def S(shape, dtype):
    return jax.ShapeDtypeStruct(shape, dtype)


def front(tok, vec, table, index):
    n = tok.shape[0]
    return pl.pallas_call(front_kernel, out_shape=(S((n, SP, D), BF), S((HEADS, SP, KP), BF)),
                          in_specs=[VMEM] * 4, out_specs=(VMEM, VMEM), compiler_params=params(), name="front")(tok, vec, table, index)


def attention(norm_one, qkv, vec, relative):
    n = norm_one.shape[0]
    return pl.pallas_call(attention_kernel,
                          out_shape=(S((n, SP, D), BF), S((n, KP, D), BF), S((n, KP, D), BF), S((n, HEADS, SP, KP), BF), S((n, SP, D), BF)),
                          in_specs=[VMEM] * 4, out_specs=(VMEM,) * 5, compiler_params=params(), name="attention")(norm_one, qkv, vec, relative)


def mlp(tok, ctx, outw, upw, downw, vec, upb, mask, ups):
    n = tok.shape[0]
    return pl.pallas_call(
        mlp_kernel,
        out_shape=(S((n, SEQ, D), BF), S((D, D), BF), S((D, FF), BF), S((FF, D), BF), S((n, SP, D), BF), S((n, SP, D), F32), S((8, D), F32), S((1, FF), F32)),
        in_specs=[VMEM, VMEM, ANY, ANY, ANY, VMEM, VMEM, VMEM, VMEM], out_specs=(VMEM,) * 8,
        scratch_shapes=[pltpu.VMEM((D, D), BF), pltpu.VMEM((D, FF), BF), pltpu.VMEM((FF, D), BF),
                        pltpu.VMEM((n, SP, D), F32), pltpu.VMEM((n, SP, D), F32), pltpu.VMEM((n, SP, D), BF),
                        pltpu.VMEM((n, SP, FF), BF), pltpu.VMEM((n, SP, FF), BF), pltpu.VMEM((n, SP, D), F32),
                        pltpu.VMEM((n, SP, D), BF), pltpu.VMEM((n, SP, D), BF), pltpu.SemaphoreType.DMA((3,))],
        compiler_params=params(), name="mlp")(tok, ctx, outw, upw, downw, vec, upb, mask, ups)


def back(tok, norm_one, qkv, vec, index, q, k, v, attend, gctx, gres):
    n = tok.shape[0]
    return pl.pallas_call(
        back_kernel,
        out_shape=(S((n, SEQ, D), F32), S((D, 3 * D), BF), S((8, D), F32), S((96, 128), F32)),
        in_specs=[VMEM, VMEM, ANY] + [VMEM] * 8, out_specs=(VMEM,) * 4,
        scratch_shapes=[pltpu.VMEM((16, SP, KP), F32), pltpu.VMEM((n, SP, 3 * D), BF), pltpu.VMEM((D, 3 * D), BF), pltpu.SemaphoreType.DMA(())],
        compiler_params=params(), name="back")(tok, norm_one, qkv, vec, index, q, k, v, attend, gctx, gres)


def pad_index(bias_index):
    return jnp.pad(bias_index, ((0, SP - SEQ), (0, KP - SEQ)))
MESH = pl.DeviceIdType.MESH


class Place:
    def __init__(self):
        dp, z = lax.axis_index("dp"), lax.axis_index("fsdp")
        y, x, c = dp // 4, (dp // 2) % 2, dp % 2
        xn, yn = dp + 2 - 4 * x, dp + 4 - 8 * y
        q = dp // 2
        qx, qy = q + 1 - 2 * x, q + 2 - 4 * y
        self.dp, self.z, self.c, self.q = dp, z, c, q
        self.near = (xn * (1 - c) + yn * c, z)
        self.far = (yn * (1 - c) + xn * c, z)
        self.x, self.y = (xn, z), (yn, z)
        self.twin = (dp + 1 - 2 * c, z)
        self.q_near = qx * (1 - c) + qy * c
        self.q_far = qy * (1 - c) + qx * c
        self.q_both = 3 - q

    def up(self, d):
        return (self.dp, (self.z + d) % 4)

    def beside(self, i):
        return ((self.dp + i) % 8, self.z)

    def barrier(self):
        sem = pltpu.get_barrier_semaphore()
        peers = [self.beside(i) for i in range(1, 8)] + [self.up(d) for d in (1, 2, 3)]
        for peer in peers:
            pl.semaphore_signal(sem, inc=1, device_id=peer, device_id_type=MESH)
        pl.semaphore_wait(sem, len(peers))


def aligned(i, size):
    return pl.ds(pl.multiple_of(i * size, size), size)


class Gather:
    def __init__(self, place, shard, full, send, recv, local):
        self.p, self.shard, self.full, self.send, self.recv, self.local = place, shard, full, send, recv, local
        self.rows, self.cols = full.shape[1] // 4, full.shape[2] // 2

    def region(self, zb, q, c):
        return self.full.at[zb, aligned(q, self.rows), aligned(c, self.cols)]

    def copy(self, d, slot, src, dst, peer):
        return pltpu.make_async_remote_copy(src_ref=src, dst_ref=dst, send_sem=self.send.at[d - 1, slot], recv_sem=self.recv.at[d - 1, slot],
                                            device_id=peer, device_id_type=MESH)

    def over_z(self, d):
        p = self.p
        if self.shard is None:
            src = self.region(p.z, p.q, p.c)
        else:
            src = self.shard.at[aligned(p.q, self.rows), aligned(p.c, self.cols)]
        return self.copy(d, 0, src, self.region(p.z, p.q, p.c), p.up(d))

    def passed(self, d, slot, q, peer):
        p = self.p
        r = self.region((p.z + 4 - d) % 4, q, p.c)
        return self.copy(d, slot, r, r, peer)

    def own(self):
        return pltpu.make_async_copy(self.shard, self.full.at[self.p.z], self.local)

    def begin(self):
        for d in (1, 2, 3):
            self.over_z(d).start()
        if self.shard is not None:
            self.own().start()

    def part(self, d, i):
        p = self.p
        slot, q, peer = ((1, p.q, p.near), (2, p.q, p.far), (4, p.q, p.twin), (3, p.q_near, p.far), (5, p.q_near, p.twin),
                         (6, p.q_far, p.twin), (7, p.q_both, p.twin))[i]
        return self.passed(d, slot, q, peer)

    def spread(self, d):
        self.over_z(d).wait_recv()
        for i in (0, 1, 2):
            self.part(d, i).start()

    def relay(self, d):
        self.part(d, 0).wait_recv()
        for i in (3, 4):
            self.part(d, i).start()

    def close(self, d):
        self.part(d, 1).wait_recv()
        self.part(d, 5).start()
        self.part(d, 3).wait_recv()
        self.part(d, 6).start()

    def finish(self):
        if self.shard is not None:
            self.own().wait()
        for d in (1, 2, 3):
            for i in (2, 4, 5, 6):
                self.part(d, i).wait_recv()

    def drain(self):
        for d in (1, 2, 3):
            self.over_z(d).wait_send()
            for i in range(7):
                self.part(d, i).wait_send()

    def steps(self):
        return [lambda d=d: self.spread(d) for d in (1, 2, 3)] + [lambda d=d: self.relay(d) for d in (1, 2, 3)] + [
            lambda d=d: self.close(d) for d in (1, 2, 3)] + [self.finish]


class Reduce:
    def __init__(self, place, grad, got, half, quarter, pieces, out, send, recv, local, straight=False):
        self.straight = straight
        self.p, self.grad, self.got, self.half, self.quarter, self.pieces, self.out = place, grad, got, half, quarter, pieces, out
        self.send, self.recv, self.local = send, recv, local
        self.rows, self.cols = grad.shape[1] // 4, grad.shape[2] // 2

    def copy(self, slot, src, dst, peer):
        return pltpu.make_async_remote_copy(src_ref=src, dst_ref=dst, send_sem=self.send.at[slot], recv_sem=self.recv.at[slot], device_id=peer, device_id_type=MESH)

    def twin(self, i):
        q = self.quarters()[i]
        return self.copy(14 + i, self.grad.at[:, aligned(q, self.rows), aligned(1 - self.p.c, self.cols)], self.got(q), self.p.twin)

    def quarters(self):
        p = self.p
        return (p.q_far, p.q_both, p.q, p.q_near)

    def mine(self, q):
        return self.grad.at[:, aligned(q, self.rows), aligned(self.p.c, self.cols)]

    def near(self, i):
        q = (self.p.q_near, self.p.q_both)[i]
        return self.copy(1 + i, self.mine(q), self.half.at[i], self.p.near)

    def far(self):
        return self.copy(3, self.half.at[1], self.quarter, self.p.far)

    def over_z(self, d):
        return self.copy(3 + d, self.quarter.at[(self.p.z + d) % 4], self.pieces.at[d - 1], self.p.up(d))

    def region(self, q):
        return self.out.at[aligned(q, self.rows), aligned(self.p.c, self.cols)]

    def passed(self, i):
        p = self.p
        q, peer = ((p.q, p.near), (p.q, p.far), (p.q, p.twin), (p.q_near, p.far), (p.q_near, p.twin), (p.q_far, p.twin), (p.q_both, p.twin))[i]
        if self.straight:
            q, peer = p.q, p.beside(i + 1)
        src = self.quarter.at[p.z] if i < 3 or self.straight else self.region(q)
        return self.copy(7 + i, src, self.region(q), peer)

    def own(self):
        return pltpu.make_async_copy(self.quarter.at[self.p.z], self.region(self.p.q), self.local)

    def begin(self):
        for i in range(4):
            self.twin(i).start()

    def add(self, dst, src):
        def one(i, carry):
            dst[i] = (dst[i].astype(F32) + src[i].astype(F32)).astype(BF)
            return carry

        lax.fori_loop(0, 4, one, 0)

    def fold(self, q):
        self.add(self.mine(q), self.got(q))

    def first_a(self):
        self.twin(0).wait_recv()
        self.fold(self.p.q_near)
        self.near(0).start()

    def first_b(self):
        self.twin(1).wait_recv()
        self.fold(self.p.q_both)
        self.near(1).start()

    def first_c(self):
        self.twin(2).wait_recv()
        self.fold(self.p.q)
        self.twin(3).wait_recv()
        self.fold(self.p.q_far)

    def second(self):
        self.near(1).wait_recv()
        self.add(self.half.at[1], self.mine(self.p.q_far))
        self.far().start()
        self.near(0).wait_recv()
        self.add(self.half.at[0], self.mine(self.p.q))

    def third(self):
        self.far().wait_recv()
        self.add(self.quarter, self.half.at[0])
        for d in (1, 2, 3):
            self.over_z(d).start()

    def fourth(self):
        for d in (1, 2, 3):
            self.over_z(d).wait_recv()
        total = self.quarter[self.p.z].astype(F32)
        for d in (1, 2, 3):
            total += self.pieces[d - 1].astype(F32)
        self.quarter[self.p.z] = total.astype(BF)
        for i in range(7 if self.straight else 3):
            self.passed(i).start()
        self.own().start()

    def fifth(self):
        if self.straight:
            return
        self.passed(0).wait_recv()
        self.passed(3).start()
        self.passed(4).start()

    def sixth(self):
        if self.straight:
            return
        self.passed(1).wait_recv()
        self.passed(5).start()
        self.passed(3).wait_recv()
        self.passed(6).start()

    def finish(self):
        for i in range(7) if self.straight else (2, 4, 5, 6):
            self.passed(i).wait_recv()
        self.own().wait()

    def drain(self):
        for i in range(4):
            self.twin(i).wait_send()
        self.near(0).wait_send()
        self.near(1).wait_send()
        self.far().wait_send()
        for d in (1, 2, 3):
            self.over_z(d).wait_send()
        for i in range(7):
            self.passed(i).wait_send()

    def steps(self):
        return [self.first_a, self.first_b, self.first_c, self.second, self.third, self.fourth, self.fifth, self.sixth]
def unstack_small(block, vec, upb, table):
    vec[...] = jnp.zeros_like(vec)
    table[...] = jnp.zeros_like(table)
    for z in range(4):
        part = block[z].astype(F32)
        vec[:, z * 192 : z * 192 + 192] = part[:16, :192]
        upb[:, z * 768 : z * 768 + 768] = part[10:11, :]
        table[:, z * 183 : z * 183 + 183] = part[16:32, :183]


def head_view(ref, h):
    return ref.at[h // 3, :, (h % 3) * 256 : (h % 3) * 256 + 256]


def layer_kernel(tok, ups, idx_in, mask_in, table_in, ub_in, v0, v1, v2, v3, v4, v5, v6, v7, v8, v9, qkv_s, out_s, up_s, down_s,
                 lo_hbm, tg_hbm, sm_out, rqkv, rout, rup, rdown,
                 qw0, qw1, qw2, outw, upw, downw, A, B, hid, att, acc, n1, q, k, v, ctx, n2, gd, lo, attend, vec, upb, table, block, small_in, small_f, index, mask,
                 sums, upsum, tab, sm, sm_got, sm_piece,
                 half0, quart0, piece0, half1, quart1, piece1, got2, half2, quart2, piece2, got3, half3, quart3, piece3,
                 got4, half4, quart4, piece4, got5, half5, quart5, piece5,
                 gsend, grecv, rsend, rrecv, local, ssend, srecv, qsem, free):
    p = Place()
    images = tok.shape[0]
    R = images * SP
    qw = (qw0, qw1, qw2)
    groups = [[pltpu.make_async_copy(qkv_s.at[:, j * D + g * 256 : j * D + g * 256 + 256], qw[g].at[p.z, :, j * 256 : j * 256 + 256], qsem.at[g, j])
               for j in range(3)] for g in range(3)]
    for group in groups:
        for c in group:
            c.start()
    small_f[...] = jnp.zeros_like(small_f)
    for i, vector in enumerate((v0, v1, v2, v3, v4, v5, v6, v7, v8, v9)):
        small_f[i, :192] = vector[...].astype(F32)
    small_f[10, :] = ub_in[...].astype(F32)
    small_f[16:28, :183] = table_in[...].astype(F32)
    small_in[...] = small_f[...].astype(BF)
    p.barrier()

    units = [(None, qw[g]) for g in range(3)] + [(out_s, outw), (up_s, upw), (down_s, downw)]
    gathers = [Gather(p, s, f, gsend.at[i], grecv.at[i], local.at[i]) for i, (s, f) in enumerate(units)]
    block[p.z] = small_in[...]
    smalls = [pltpu.make_async_remote_copy(src_ref=small_in, dst_ref=block.at[p.z], send_sem=ssend.at[d - 1], recv_sem=srecv.at[d - 1], device_id=p.up(d), device_id_type=MESH) for d in (1, 2, 3)]
    for s in smalls:
        s.start()
    for g in range(4):
        if g < 3:
            for c in groups[g]:
                c.wait()
        gathers[g].begin()
    index[...] = jnp.zeros_like(index)
    index[:SEQ, :SEQ] = idx_in[...]
    mask[...] = jnp.zeros_like(mask)
    mask[:images, :SEQ] = mask_in[...].astype(F32)
    for s in smalls:
        s.wait_recv()
    unstack_small(block, vec, upb, table)
    row = lambda i: vec[i : i + 1, :]
    todo = []

    def plan(steps, times):
        todo.extend(zip(times, steps))
        todo.sort(key=lambda e: e[0])

    def advance(now):
        while todo and todo[0][0] <= now:
            todo.pop(0)[1]()

    for g, (spread, relay, close, finish) in zip(gathers, GATHER_PLAN):
        plan(g.steps(), (spread, spread + 0.5, spread + 1, relay, relay + 0.5, relay + 1, close, close + 0.5, close + 1, finish))
    plan([gathers[4].begin, gathers[5].begin], BEGIN_PLAN)
    for b in range(images):
        xhat, _ = xhat_of(pad_rows(tok[b].astype(F32)))
        n1[b] = (xhat * row(GAIN1) + row(SHIFT1)).astype(BF)
        advance(5 + b)
    relative = [head_view(gd, h) for h in range(HEADS)]
    lookup(table, index, relative)

    k[:, SP:, :] = jnp.zeros((images, KP - SP, D), BF)
    v[:, SP:, :] = jnp.zeros((images, KP - SP, D), BF)
    for g in range(3):
        at = slice(g * 256, g * 256 + 256)
        advance(GATHER_PLAN[g][3])

        def weight(j, g=g):
            return qw[g][:, :, j * 256 : j * 256 + 256].reshape(D, 256)

        rows = n1[...].reshape(R, D)
        q[:, :, at] = ((dot(rows, weight(0)) + vec[QBIAS : QBIAS + 1, at]) * 0.125).astype(BF).reshape(images, SP, 256)
        k[:, :SP, at] = dot(rows, weight(1)).astype(BF).reshape(images, SP, 256)
        v[:, :SP, at] = (dot(rows, weight(2)) + vec[VBIAS : VBIAS + 1, at]).astype(BF).reshape(images, SP, 256)
        advance(17 + 8 * g)
        for hp in (2 * g, 2 * g + 1):

            def one(b, carry, hp=hp):
                attend_pair(b, hp, slice(hp * 128, hp * 128 + 128), q, k, v, relative, attend, ctx)
                return carry

            lax.fori_loop(0, images, one, 0)
            advance(20 + 8 * g + 3 * (hp - 2 * g))

    advance(GATHER_PLAN[3][3])
    for b in range(images):
        attn = dot(ctx[b], outw[...].reshape(D, D)) + row(OBIAS)
        att[b] = attn
        h = pad_rows(tok[b].astype(F32)) + row(SCALE1) * attn
        hid[b] = h
        xhat, _ = xhat_of(h)
        n2[b] = (xhat * row(GAIN2) + row(SHIFT2)).astype(BF)
    advance(GATHER_PLAN[4][3])
    W = 256

    def expand(f, carry):
        at = aligned(f, W)
        u = dot(n2[...].reshape(R, D), upw[:, :, at].reshape(D, W)) + upb[:, at]
        g, s = gelu_both(u)
        A[:, :, at] = g.astype(BF).reshape(images, SP, W)
        B[:, :, at] = s.astype(BF).reshape(images, SP, W)
        return carry

    for part in range(4):
        lax.fori_loop(part * 3, part * 3 + 3, expand, 0)
        advance(46 + 3 * part)
    advance(1000)
    for i in range(D // 256):
        at = slice(i * 256, i * 256 + 256)
        acc[:, :, at] = dot(A[...].reshape(R, FF), downw[:, :, at].reshape(FF, 256)).reshape(images, SP, 256)
    maskt = jnp.transpose(mask[...], (1, 0))
    sums[...] = jnp.zeros_like(sums)

    def add_sum(i, value):
        sums[i : i + 1, :] += colsum(value)

    def grad_y(b):
        return pad_rows(ups[b].astype(F32)) * maskt[:SP, b : b + 1]

    for b in range(images):
        down = acc[b] + row(DBIAS)
        lo[b] = (hid[b] + row(SCALE2) * down).astype(BF)
        gy = grad_y(b)
        add_sum(SCALE2, gy * down)
        full = gy * row(SCALE2)
        add_sum(DBIAS, full)
        gd[b] = full.astype(BF)
    lo_copy = pltpu.make_async_copy(lo, lo_hbm, local.at[12])
    lo_copy.start()

    for g in gathers:
        g.drain()

    def contract(f, carry):
        at = aligned(f, W)
        z, r = f // 3, f % 3
        rows = aligned(r, W)
        gg = dot_nt(gd[...].reshape(R, D), downw[z, rows, :]) * B[:, :, at].reshape(R, W).astype(F32)
        upsum[:, at] = colsum(gg)
        B[:, :, at] = gg.astype(BF).reshape(images, SP, W)
        downw[z, rows, :] = dot_tn(A[:, :, at].reshape(R, W), gd[...].reshape(R, D)).astype(BF)
        return carry

    lax.fori_loop(0, FF // W, contract, 0)
    pl.semaphore_signal(free, inc=1, device_id=p.twin, device_id_type=MESH)

    def got_down(q):
        return A.at[:, :192, pl.ds(pl.multiple_of(1536 + q * 384, 128), 384)]

    def got_up(q):
        return A.at[:, aligned(q, 48), :1536]

    def got_of(ref, rows):
        return lambda q: ref.at[:, aligned(q, rows), :]

    parts = ((downw, got_down, half0, quart0, piece0, rdown), (upw, got_up, half1, quart1, piece1, rup),
             (outw, got_of(got2, 48), half2, quart2, piece2, rout), (qw0, got_of(got3, 48), half3, quart3, piece3, rqkv.at[0]),
             (qw1, got_of(got4, 48), half4, quart4, piece4, rqkv.at[1]), (qw2, got_of(got5, 48), half5, quart5, piece5, rqkv.at[2]))
    red = [Reduce(p, *part, rsend.at[i], rrecv.at[i], local.at[6 + i], straight=i == 5) for i, part in enumerate(parts)]

    def launch(i):
        red[i].begin()
        plan(red[i].steps(), REDUCE_PLAN[i])

    pl.semaphore_wait(free, 1)
    launch(0)
    for i in range(4):
        acc[:, :, i * 192 : i * 192 + 192] = dot_nt(B[...].reshape(R, FF), upw[i]).reshape(images, SP, 192)
        advance(13.5 + 1.5 * i)

    def widen(f, carry):
        at = aligned(f, W)
        upw[:, :, at] = dot_tn(n2[...].reshape(R, D), B[:, :, at].reshape(R, W)).astype(BF).reshape(4, D // 4, W)
        return carry

    for i in range(4):
        lax.fori_loop(3 * i, 3 * i + 3, widen, 0)
        advance(20 + 2 * i)
    launch(1)
    for b in range(images):
        xhat, rstd = xhat_of(hid[b])
        g = acc[b]
        add_sum(GAIN2, g * xhat)
        add_sum(SHIFT2, g)
        gg = g * row(GAIN2)
        res = grad_y(b) + (gg - rowmean(gg) - xhat * rowmean(gg * xhat)) * rstd
        hid[b] = res
        add_sum(SCALE1, res * att[b])
        full = res * row(SCALE1)
        add_sum(OBIAS, full)
        n2[b] = full.astype(BF)
        advance(27 + b)
    gctx = B.at[:, :, 3 * D :]
    for b in range(images):
        gctx[b] = dot_nt(n2[b], outw[...].reshape(D, D)).astype(BF)
    for i in range(3):
        at = slice(i * 256, i * 256 + 256)
        outw[:, :, at] = dot_tn(ctx[...].reshape(R, D), n2[:, :, at].reshape(R, 256)).astype(BF).reshape(4, D // 4, 256)
    launch(2)
    advance(33)

    acc[...] = jnp.zeros_like(acc)
    gtab = [head_view(acc, h) for h in range(HEADS)]
    gq, gk, gv = (B.at[:, :, i * D : (i + 1) * D] for i in range(3))
    qsum, vsum = sums.at[QBIAS : QBIAS + 1, :], sums.at[VBIAS : VBIAS + 1, :]
    for g in range(3):
        now = 33 + 11 * g
        for hp in (2 * g, 2 * g + 1):
            for part in range(2):

                def one(i, carry, hp=hp, part=part):
                    attend_back(part * (images // 2) + i, hp, slice(hp * 128, hp * 128 + 128), q, k, v, attend, gctx, gtab, gq, gk, gv, qsum, vsum)
                    return carry

                lax.fori_loop(0, images // 2, one, 0)
                now += 2
                advance(now)
        grads = [B.at[:, :, j * D + g * 256 : j * D + g * 256 + 256] for j in range(3)]
        term = sum(dot_nt(grads[j][...].reshape(R, 256), qw[g][:, :, j * 256 : j * 256 + 256].reshape(D, 256)) for j in range(3)).reshape(images, SP, D)
        att[...] = term if g == 0 else att[...] + term
        for j in range(3):
            qw[g][:, :, j * 256 : j * 256 + 256] = dot_tn(n1[...].reshape(R, D), grads[j][...].reshape(R, 256)).astype(BF).reshape(4, D // 4, 256)
        launch(3 + g)
        advance(now + 3)
    for b in range(images):
        xhat, rstd = xhat_of(pad_rows(tok[b].astype(F32)))
        g = att[b]
        add_sum(GAIN1, g * xhat)
        add_sum(SHIFT1, g)
        gg = g * row(GAIN1)
        att[b] = hid[b] + (gg - rowmean(gg) - xhat * rowmean(gg * xhat)) * rstd
        advance(67 + b)
    tg_copy = pltpu.make_async_copy(att, tg_hbm, local.at[13])
    tg_copy.start()
    total = jnp.zeros((192, 128), F32)
    for i in range(5):
        total = table_rows(gtab, index, total, 5 * i, 5 * i + 5)
        advance(72 + 2 * (i + 1))
    tab[...] = total[:96] + total[96:]
    sm[...] = jnp.zeros_like(sm)
    flat = table
    for h in range(HEADS):
        for c in range(6):
            flat[h : h + 1, c * 128 : c * 128 + 128] = tab[h * 8 + c : h * 8 + c + 1, :]
    for z in range(4):
        sm[z, 0:16, 0:192] = sums[:, z * 192 : z * 192 + 192]
        for i in range(3):
            sm[z, 10 + i : 11 + i, :] = upsum[:, z * 768 + i * 256 : z * 768 + i * 256 + 256]
        sm[z, 16:32, 0:183] = flat[:, z * 183 : z * 183 + 183]

    parts = [pltpu.make_async_remote_copy(src_ref=sm.at[(p.z + d) % 4], dst_ref=sm_piece.at[d - 1], send_sem=ssend.at[2 + d], recv_sem=srecv.at[2 + d], device_id=p.up(d), device_id_type=MESH) for d in (1, 2, 3)]
    for s in parts:
        s.start()
    advance(86)
    for s in parts:
        s.wait_recv()
    sm_got[p.dp] = sm[p.z] + sm_piece[0] + sm_piece[1] + sm_piece[2]
    shares = [pltpu.make_async_remote_copy(src_ref=sm_got.at[p.dp], dst_ref=sm_got.at[p.dp], send_sem=ssend.at[5 + i], recv_sem=srecv.at[5 + i], device_id=p.beside(i), device_id_type=MESH) for i in range(1, 8)]
    for s in shares:
        s.start()
    advance(90)
    for s in shares:
        s.wait_recv()
    whole_sum = sm_got[0]
    for i in range(1, 8):
        whole_sum += sm_got[i]
    sm_out[...] = whole_sum
    advance(1000)
    for r in red:
        r.finish()
    lo_copy.wait()
    tg_copy.wait()
    for s in smalls + parts + shares:
        s.wait_send()
    for r in red:
        r.drain()


GATHER_PLAN = ((5, 8, 10, 13), (8.2, 11, 13.2, 16), (11.2, 14, 17, 20), (14.2, 18, 20.2, 23), (24, 30, 35, 38), (36, 44, 49, 52))
BEGIN_PLAN = (5, 9)
REDUCE_PLAN = ((15, 17, 19, 30, 37, 50, 53, 56), (28, 30, 32, 45, 52, 65, 68, 71), (35, 35.5, 36, 47, 50.5, 56, 58, 61),
               (46, 47, 48, 52.5, 56.5, 62, 65, 68), (57, 58, 59, 63, 66, 71, 74, 77), (68, 69, 70, 74, 77, 82, 85, 88))


def layer(tok, ups, index, mask, table, up_bias, vectors, qkv_s, out_s, up_s, down_s):
    n = tok.shape[0]
    shards = (qkv_s, out_s, up_s, down_s)

    def vm(shape, dtype=BF):
        return pltpu.VMEM(shape, dtype)

    row3, bufs = (n, SP, D), []
    for i, s in enumerate((down_s, up_s, out_s, out_s, out_s, out_s)):
        rows, h = s.shape[0], s.shape[1] // 2
        bufs += [vm((4, rows, h))] * (i > 1) + [vm((2, 4, rows // 4, h)), vm((4, rows // 4, h)), vm((3, rows // 4, h))]
    dma = pltpu.SemaphoreType.DMA
    scratch = [vm((4,) + s.shape) for s in (out_s, out_s, out_s, out_s, up_s, down_s)] + [vm((n, SP, FF)), vm((n, SP, FF)), vm(row3, F32), vm(row3, F32), vm(row3, F32),
               vm(row3), vm(row3), vm((n, KP, D)), vm((n, KP, D)), vm(row3), vm(row3), vm(row3), vm(row3), vm((n, HEADS, SP, KP)),
               vm((16, D), F32), vm((1, FF), F32), vm((16, D), F32), vm((4, 32, D)), vm((32, D)), vm((32, D), F32), vm((SP, KP), jnp.int32), vm((8, KP), F32),
               vm((16, D), F32), vm((1, FF), F32), vm((96, 128), F32), vm((4, 32, 256), F32), vm((8, 32, 256), F32), vm((3, 32, 256), F32)]
    return pl.pallas_call(
        layer_kernel,
        out_shape=(S(row3, BF), S(row3, F32), S((32, 256), F32)) + (S((3, qkv_s.shape[0], D), BF),) + tuple(S(s.shape, BF) for s in shards[1:]),
        in_specs=[VMEM] * 16 + [ANY] * 4, out_specs=(ANY, ANY, VMEM, ANY, ANY, ANY, ANY),
        scratch_shapes=scratch + bufs + [dma((6, 3, 8)), dma((6, 3, 8)), dma((6, 18)), dma((6, 18)), dma((14,)), dma((13,)), dma((13,)), dma((3, 3)), pltpu.SemaphoreType.REGULAR],
        compiler_params=params(collective_id=0, has_side_effects=True), name="layer")(tok, ups, index, mask, table, up_bias, *vectors, *shards)


def finish_kernel(sm, rq, ro, ru, rd, dq, do, du, dd, gub, tab, *vectors):
    for g in range(3):
        for j in range(3):
            dq[:, j * D + g * 256 : j * D + g * 256 + 256] = rq[g, :, j * 256 : j * 256 + 256].astype(F32)
    do[...] = ro[...].astype(F32)
    du[...] = ru[...].astype(F32)
    dd[...] = rd[...].astype(F32)
    for i, v in enumerate(vectors):
        v[...] = sm[i, :192]
    gub[...] = jnp.concatenate([sm[i : i + 1, :] for i in (10, 11, 12)], axis=1)[0]
    tab[...] = sm[16:28, :183]


def finish(sm, rq, ro, ru, rd):
    outs = (S((192, 3 * D), F32), S(ro.shape, F32), S(ru.shape, F32), S(rd.shape, F32), S((FF // 4,), F32), S((HEADS, 183), F32)) + (S((192,), F32),) * 10
    return pl.pallas_call(finish_kernel, out_shape=outs, in_specs=[VMEM] * 5, out_specs=(VMEM,) * 16, compiler_params=params(), name="finish")(sm, rq, ro, ru, rd)


def wide_body(tokens, first_gain, first_shift, qkv_weight, query_bias, value_bias, bias_table, bias_index, out_weight, out_bias, first_scale,
              second_gain, second_shift, up_weight, up_bias, down_weight, down_bias, second_scale, patch_mask, upstream):
    n = tokens.shape[0]

    def whole(v):
        return lax.all_gather(v, "fsdp", axis=0, tiled=True)

    vectors = (first_gain, first_shift, query_bias, value_bias, out_bias, first_scale, second_gain, second_shift, down_bias, second_scale)
    vec = jnp.pad(lax.all_gather(jnp.stack(vectors), "fsdp", axis=1, tiled=True).astype(F32), ((0, 6), (0, 0)))
    upb = whole(up_bias).astype(F32).reshape(1, FF)
    table = jnp.pad(whole(bias_table).T.astype(F32), ((0, 4), (0, 768 - RELS)))
    qkv, outw, upw, downw = whole(qkv_weight), whole(out_weight), whole(up_weight), whole(down_weight)
    index = pad_index(bias_index)
    mask = jnp.pad(patch_mask.astype(F32), ((0, 8 - n), (0, KP - SEQ)))
    norm_one, relative = front(tokens, vec, table, index)
    q, k, v, attend, context = attention(norm_one, qkv, vec, relative)
    layer_out, dout, dup, ddown, gctx, gres, small_mlp, small_up = mlp(tokens, context, outw, upw, downw, vec, upb, mask, upstream)
    tgrad, dqkv, small, tab = back(tokens, norm_one, qkv, vec, index, q, k, v, attend, gctx, gres)
    tab = tab.reshape(HEADS, 8, 128)[:, :6].reshape(HEADS, 768)[:, :RELS].T

    def summed(g):
        part = lax.psum_scatter(g.astype(BF), "fsdp", scatter_dimension=0, tiled=True)
        return lax.psum(part.astype(F32), "dp")

    rows = lax.psum(lax.psum_scatter(jnp.concatenate([small[2:4], small[0:2], small_mlp[::-1][2:]]), "fsdp", scatter_dimension=1, tiled=True), "dp")
    g1, s1, qb, vb, ob, sc1, s2, g2, db, sc2 = rows
    return (layer_out, tgrad, g1, s1, summed(dqkv), qb, vb, summed(tab), summed(dout), ob, sc1, g2, s2, summed(dup), summed(small_up.reshape(FF)), summed(ddown), db, sc2)


def body(wide, tokens, first_gain, first_shift, qkv_weight, query_bias, value_bias, bias_table, bias_index, out_weight, out_bias, first_scale,
         second_gain, second_shift, up_weight, up_bias, down_weight, down_bias, second_scale, patch_mask, upstream):
    if wide:
        return wide_body(tokens, first_gain, first_shift, qkv_weight, query_bias, value_bias, bias_table, bias_index, out_weight, out_bias, first_scale,
                         second_gain, second_shift, up_weight, up_bias, down_weight, down_bias, second_scale, patch_mask, upstream)
    n = tokens.shape[0]
    vectors = (first_gain, first_shift, query_bias, value_bias, out_bias, first_scale, second_gain, second_shift, down_bias, second_scale)
    lo, tg, sm, rqkv, rout, rup, rdown = layer(tokens, upstream, bias_index, patch_mask, bias_table.T, up_bias, vectors,
                                               qkv_weight, out_weight, up_weight, down_weight)
    layer_out, tgrad = lo[:, :SEQ], tg[:, :SEQ]
    dq, do, du, dd, gub, gtab, g1, s1, qb, vb, ob, sc1, g2, s2, db, sc2 = finish(sm, rqkv, rout, rup, rdown)
    return (layer_out, tgrad, g1, s1, dq, qb, vb, gtab.T, do, ob, sc1, g2, s2, du, gub, dd, db, sc2)


def solution(mesh):
    vector, matrix, batch = P("fsdp"), P("fsdp", None), P(("dp", "fsdp"), None, None)
    in_specs = (batch, vector, vector, matrix, vector, vector, matrix, P(), matrix, vector, vector, vector, vector, matrix, vector, matrix, vector, vector,
                P(("dp", "fsdp"), None), batch)
    out_specs = (batch, batch, vector, vector, matrix, vector, vector, matrix, matrix, vector, vector, vector, vector, matrix, vector, matrix, vector, vector)
    wide = mesh.shape["dp"] != 8 or mesh.shape["fsdp"] != 4
    return jax.shard_map(functools.partial(body, wide), mesh=mesh, in_specs=in_specs, out_specs=out_specs, check_vma=False)
```
